256 devices in a mesh: tmpl: 8 (over z), chan: 16 (over x_hi, y, core), tm: 2 (over x_lo).
Axes of the slice: x: 4 (x_hi: 2, x_lo: 2; x = x_hi * 2 + x_lo), y: 4, z: 8, core: 2. Of those that a mesh axis runs over, the one named last changes fastest.
Arguments:
- raw: bfloat16 [1024, 8192], P('chan', ('tmpl', 'tm')), may hold values from -6 to 6
- dead_mask: int32 [1024], P('chan'), may hold values 0 or 1
- templates: bfloat16 [32, 1024, 512], P('tmpl', 'chan'), may hold values from -0.0078125 to 0.0078125
- assign: int32 [32], P('tmpl'), may hold values from 0 to 31, as said below
- w_enc: bfloat16 [16, 1, 3, 3], replicated, may hold values from -2 to 2
- b_enc: float32 [16], replicated, may hold values from -3 to 3
- w_mid: bfloat16 [32, 16, 3, 3], replicated, may hold values from -0.5 to 0.5
- b_mid: float32 [32], replicated, may hold values from -3 to 3
- w_dec: bfloat16 [16, 48, 3, 3], replicated, may hold values from -0.3125 to 0.3125
- b_dec: float32 [16], replicated, may hold values from -3 to 3
- w_out: bfloat16 [16], replicated, may hold values from -1.5 to 1.5
- b_out: float32 [1], replicated, may hold values from -3 to 3
Outputs:
- denoised: bfloat16 [1024, 8192], P('chan', ('tmpl', 'tm'))
- corr: float32 [32, 8, 2, 512], P('tmpl', None, 'tm', 'chan')
The draws below stay inside these ranges and needn't reach their ends.
Inputs may be any that keep to these rules, and one draw needn't show every extreme that they name: `assign`: for each j, entries 4 * j to 4 * j + 3 hold exactly those numbers in some order.
All inputs are finite; a program needn't handle non-finite values. No bound on the sum of `dead_mask` on one device may be relied on, other than what follows from the above.
Results may differ from the reference program's by a relative error of at most 0.018.
Values may be sent and summed in bfloat16 or wider, within the bound.
A program may use at most 128 MiB of HBM per device.

```python
import math
import jax
import jax.numpy as jnp
from jax import lax

TM_DEV = 4
TL = 512
F = 16
CH = 1024
NTMPL = 32
NPAIR = 8
NBLK = 16
NT = 8192


def draw_assign(key, part):
    owners = NTMPL // TM_DEV
    base_ids = jnp.arange(NTMPL, dtype=jnp.int32) // TM_DEV * TM_DEV
    owner_keys = jax.random.split(key, owners)
    orders = jax.vmap(lambda owner_key: jax.random.permutation(owner_key, TM_DEV))(owner_keys)
    return (orders.reshape(-1).astype(jnp.int32) + base_ids).astype(jnp.int32)


def touch_ends(values, own_key, least, largest):
    longest = values.shape.index(max(values.shape))
    spots = []
    for shift in (0, 1):
        where = [jax.random.randint(jax.random.fold_in(own_key, axis), (), 0, length) for axis, length in enumerate(values.shape)]
        where[longest] = (where[longest] + shift) % values.shape[longest]
        spots.append(tuple(where))
    return values.at[spots[0]].set(least).at[spots[1]].set(largest)


def block_scale(own_key, dims, shards, low, largest):
    loudness = 1.0
    for axis_at, shards_of in shards:
        steps = jax.random.uniform(jax.random.fold_in(jax.random.fold_in(own_key, 6), axis_at), (shards_of,), jnp.float32, low / len(shards), largest / len(shards))
        loudness = loudness * jnp.repeat(jnp.exp(steps), dims[axis_at] // shards_of).reshape((-1,) + (1,) * (len(dims) - 1 - axis_at))
    return loudness


def bell_draw(key, dims, spread, reach, cuts=(), kind=jnp.bfloat16):
    level = block_scale(key, dims, cuts, -0.22, 0.18) if cuts else 1.0
    drawn = jax.random.normal(key, dims, jnp.float32) * spread * level
    return jnp.minimum(jnp.maximum(drawn, -reach), reach).astype(kind)


def setup_inputs(seed: int = 0) -> dict:
    streams_of = jax.random.split(jax.random.key(seed), 13)
    return {
        "raw": bell_draw(streams_of[0], (CH, NT), 1.0, 6.0, ((0, 16), (1, 16))),
        "dead_mask": touch_ends((jax.random.randint(streams_of[1], (CH,), 0, 8) < 7).astype(jnp.int32), jax.random.fold_in(streams_of[1], 1), 0, 1),
        "templates": bell_draw(streams_of[2], (NTMPL, CH, TL), (CH * TL) ** -0.5, 0.0078125, ((0, 8), (1, 16))),
        "assign": draw_assign(jax.random.fold_in(streams_of[12], 71), 0),
        "w_enc": bell_draw(streams_of[4], (F, 1, 3, 3), 9 ** -0.5, 2.0),
        "b_enc": bell_draw(streams_of[5], (F,), 0.5, 3.0, (), jnp.float32),
        "w_mid": bell_draw(streams_of[6], (2 * F, F, 3, 3), (9 * F) ** -0.5, 0.5),
        "b_mid": bell_draw(streams_of[7], (2 * F,), 0.5, 3.0, (), jnp.float32),
        "w_dec": bell_draw(streams_of[8], (F, 3 * F, 3, 3), (27 * F) ** -0.5, 0.3125),
        "b_dec": bell_draw(streams_of[9], (F,), 0.5, 3.0, (), jnp.float32),
        "w_out": bell_draw(streams_of[10], (F,), F ** -0.5, 1.5),
        "b_out": bell_draw(streams_of[11], (1,), 0.5, 3.0, (), jnp.float32),
    }


def forward_table(patch_len):
    sample_ids = jnp.arange(patch_len, dtype=jnp.int32)[:, None]
    freq_ids = jnp.arange(2 * patch_len, dtype=jnp.int32)[None, :]
    phase = ((sample_ids * freq_ids) % (2 * patch_len)).astype(jnp.float32) * (math.pi / patch_len)
    return jnp.concatenate([jnp.cos(phase), -jnp.sin(phase)], axis=1).astype(jnp.bfloat16)


def inverse_table(patch_len):
    freq_ids = jnp.arange(2 * patch_len, dtype=jnp.int32)[:, None]
    lag_ids = jnp.arange(patch_len, dtype=jnp.int32)[None, :]
    phase = ((freq_ids * lag_ids) % (2 * patch_len)).astype(jnp.float32) * (math.pi / patch_len)
    return jnp.concatenate([jnp.cos(phase), -jnp.sin(phase)], axis=0) / (2.0 * patch_len)


def alternate_signs(patch_len):
    single = jnp.where(jnp.arange(2 * patch_len) % 2 == 0, 1.0, -1.0).astype(jnp.float32)
    return jnp.concatenate([single, single])


def conv_ref(picture, weight, bias_term):
    result = lax.conv_general_dilated(picture.astype(jnp.float32), weight.astype(jnp.float32), (1, 1), ((1, 1), (1, 1)), dimension_numbers=("NCHW", "OIHW", "NCHW"), precision=lax.Precision.HIGHEST)
    return jax.nn.relu(result + bias_term[None, :, None, None]).astype(jnp.bfloat16)


def cross_products(spectrum, tspectrum, half_len):
    spec_re = spectrum[..., :half_len].astype(jnp.float32)
    spec_im = spectrum[..., half_len:].astype(jnp.float32)
    tmpl_re = tspectrum[..., :half_len].astype(jnp.float32)
    tmpl_im = tspectrum[..., half_len:].astype(jnp.float32)
    hp = lax.Precision.HIGHEST
    real_part = jnp.einsum("bcf,kcf->kbf", spec_re, tmpl_re, precision=hp) + jnp.einsum("bcf,kcf->kbf", spec_im, tmpl_im, precision=hp)
    imag_part = jnp.einsum("bcf,kcf->kbf", spec_im, tmpl_re, precision=hp) - jnp.einsum("bcf,kcf->kbf", spec_re, tmpl_im, precision=hp)
    return jnp.concatenate([real_part, imag_part], axis=-1)


def reference(raw, dead_mask, templates, assign, w_enc, b_enc, w_mid, b_mid, w_dec, b_dec, w_out, b_out):
    alive = dead_mask.astype(jnp.float32)
    cleaned = raw * alive[:, None].astype(jnp.bfloat16)
    patches = cleaned.reshape(CH, NBLK, TL).transpose(1, 0, 2)

    def denoise(patch):
        picture = patch[None, None]
        encoded = conv_ref(picture, w_enc, b_enc)
        pooled = encoded.astype(jnp.float32).reshape(1, F, CH // 2, 2, TL // 2, 2).mean(axis=(3, 5)).astype(jnp.bfloat16)
        middle = conv_ref(pooled, w_mid, b_mid)
        upsampled = jnp.repeat(jnp.repeat(middle, 2, axis=2), 2, axis=3)
        merged = jnp.concatenate([upsampled, encoded], axis=1)
        decoded = conv_ref(merged, w_dec, b_dec)
        branch = jnp.einsum("g,gct->ct", w_out.astype(jnp.float32), decoded[0].astype(jnp.float32), precision=lax.Precision.HIGHEST)
        return (alive[:, None] * (patch.astype(jnp.float32) + branch + b_out[0])).astype(jnp.bfloat16)

    denoised_blocks = lax.map(denoise, patches)
    denoised = denoised_blocks.transpose(1, 0, 2).reshape(CH, NT)
    forward = forward_table(TL).astype(jnp.float32)
    spectra = jnp.einsum("bct,tf->bcf", denoised_blocks.astype(jnp.float32), forward, precision=lax.Precision.HIGHEST).astype(jnp.bfloat16)
    tspectra = jnp.einsum("kct,tf->kcf", templates.astype(jnp.float32), forward, precision=lax.Precision.HIGHEST).astype(jnp.bfloat16)
    products = cross_products(spectra, tspectra, 2 * TL)
    following = jnp.concatenate([products[:, 1:], jnp.zeros_like(products[:, :1])], axis=1)
    combined = products + alternate_signs(TL) * following
    lagged = jnp.dot(combined.reshape(-1, 4 * TL), inverse_table(TL), precision=lax.Precision.HIGHEST).reshape(NTMPL, NBLK, TL)
    ordered = lagged[assign]
    return denoised, ordered.reshape(NTMPL, NPAIR, 2, TL)
```

```python
import functools
import math

import jax
import jax.numpy as jnp
import numpy as np
from jax import lax
from jax.experimental import pallas as pl
from jax.experimental.pallas import tpu as pltpu
from jax.sharding import PartitionSpec as P

BF = jnp.bfloat16
F32 = jnp.float32
MESH = pl.DeviceIdType.MESH
ROWS = 64
TL = 512
HALF = 256
NZ = 8
NC = 16
BIG = -1e30


def middle_table():
    q = np.zeros((16, 3, 3, 512), np.float32)
    for g in range(16):
        for rr in range(3):
            for v in range(3):
                q[g, rr, v, rr * 48 + v * 16 + g] = 1
    return q.reshape(144, 512)


def encoder_table():
    q = np.zeros((4, 3, 3, 128), np.float32)
    for v in range(4):
        for rr in range(3):
            for dt in range(3):
                q[v, rr, dt, rr * 8 + v + dt] = 1
    return q.reshape(4, 9, 128)


def decoder_table():
    q = np.zeros((4, 48, 3, 3, 640), np.float32)
    for ps in range(2):
        for pr in range(2):
            n = ps * 2 + pr
            for rr in range(4):
                for v in range(4):
                    if 0 <= rr - pr <= 2 and 0 <= v - ps <= 2:
                        for g in range(16):
                            q[n, 32 + g, rr - pr, v - ps, rr * 64 + v * 16 + g] = 1
            for dr in range(3):
                for dt in range(3):
                    rr = (pr + dr - 1) // 2 + 1
                    v = (ps + dt - 1) // 2 + 1
                    for m in range(32):
                        q[n, m, dr, dt, 256 + rr * 96 + v * 32 + m] = 1
    return q.reshape(4, 432, 640)


def spectrum_table():
    s = np.arange(TL)[:, None]
    f = np.arange(TL)[None, :]
    phase = ((s * f) % (2 * TL)) * (math.pi / TL)
    re = np.cos(phase)
    im = -np.sin(phase)
    im[:, 0] = np.where(np.arange(TL) % 2 == 0, 1.0, -1.0)
    return np.concatenate([re, im], axis=1).astype(np.float32)


def lag_table():
    f = np.arange(TL)[:, None]
    j = np.arange(TL)[None, :]
    phase = ((f * j) % (2 * TL)) * (math.pi / TL)
    re = np.cos(phase) * 2
    im = -np.sin(phase) * 2
    re[0] = 1
    im[0] = np.where(np.arange(TL) % 2 == 0, 1.0, -1.0)
    full = (np.concatenate([re, im], axis=0) / (2 * TL)).astype(np.float32)
    hi = full.astype(BF)
    lo = (full - hi.astype(np.float32)).astype(BF)
    return hi, lo


def iota(shape, dim):
    return lax.broadcasted_iota(jnp.int32, shape, dim)


def mm(a, b):
    return jnp.dot(a, b, preferred_element_type=F32)


def column(ref, count, lanes):
    rows = iota((count, lanes), 0)
    out = jnp.zeros((count, lanes), F32)
    for g in range(count):
        out = jnp.where(rows == g, ref[g], out)
    return out


def kernel(
    raw_ref, mask_ref, tmpl_ref, assign_ref, wenc_ref, benc_ref, wmid_ref, bmid_ref,
    wdec_ref, bdec_ref, wout_ref, bout_ref, q1_ref, q2_ref, q3_ref, f_hbm, ih_hbm, il_hbm,
    den_ref, corr_ref,
    f_ref, ih_ref, il_ref, clean_ref, halo_ref, cv_ref, w1_ref, w2_ref, w3s_ref, w3m_ref,
    ev_ref, pv_ref, mv_ref, dp_ref, own_ref, alive_ref, b2_ref, b3_ref, tg_ref, ts_ref, sd_ref, xw_ref,
    z_ref, g_ref, lag_ref, rs_ref, rr_ref, as_ref, ar_ref,
    tab_sem, halo_send, halo_recv, ring_send, ring_recv, x_send, x_recv,
    rs_send, rs_recv, a_send, a_recv,
):
    z = lax.axis_index("tmpl")
    c = lax.axis_index("chan")
    p = lax.axis_index("tm")
    me = p * NC + c

    barrier = pltpu.get_barrier_semaphore()

    def signal(dz, dc, dp):
        pl.semaphore_signal(barrier, inc=1, device_id=(dz, dc, dp), device_id_type=MESH)

    @pl.loop(1, 2 * NC)
    def _(d):
        other = lax.rem(me + d, 2 * NC)
        signal(z, lax.rem(other, NC), other // NC)

    @pl.loop(1, NZ)
    def _(d):
        signal(lax.rem(z + d, NZ), c, p)

    zr = lax.rem(z + 1, NZ)
    zl = lax.rem(z + NZ - 1, NZ)
    signal(zr, c, 1 - p)
    signal(zl, c, 1 - p)

    tabs = [
        pltpu.make_async_copy(f_hbm, f_ref, tab_sem.at[0]),
        pltpu.make_async_copy(ih_hbm, ih_ref, tab_sem.at[1]),
        pltpu.make_async_copy(il_hbm, il_ref, tab_sem.at[2]),
    ]
    for t in tabs:
        t.start()

    mask = mask_ref[...].astype(F32)
    diag = jnp.where(iota((ROWS, ROWS), 0) == iota((ROWS, ROWS), 1), mask, 0.0).astype(BF)
    clean = mm(diag, raw_ref[...]).astype(BF)
    clean_ref[...] = clean
    rows = iota((128, 256), 0)
    pick = (rows % 4) * 64 + p * 32 + rows // 4 == iota((128, 256), 1)
    tg_ref[z] = mm(jnp.where(pick, 1.0, 0.0).astype(BF), tmpl_ref[...].reshape(256, TL)).astype(BF)

    pl.semaphore_wait(barrier, 2 * NC - 1 + NZ - 1 + 2)

    up = lax.rem(c + NC - 1, NC)
    down = lax.rem(c + 1, NC)
    halos = [
        pltpu.make_async_remote_copy(
            src_ref=clean_ref.at[pl.ds(0, 16)], dst_ref=halo_ref.at[1],
            send_sem=halo_send.at[0], recv_sem=halo_recv.at[0],
            device_id=(z, up, p), device_id_type=MESH),
        pltpu.make_async_remote_copy(
            src_ref=clean_ref.at[pl.ds(48, 16)], dst_ref=halo_ref.at[0],
            send_sem=halo_send.at[1], recv_sem=halo_recv.at[1],
            device_id=(z, down, p), device_id_type=MESH),
    ]
    for h in halos:
        h.start()

    def right(s):
        slot = lax.rem(z - s + NZ, NZ)
        return pltpu.make_async_remote_copy(
            src_ref=tg_ref.at[slot], dst_ref=tg_ref.at[slot],
            send_sem=ring_send.at[0, s], recv_sem=ring_recv.at[0, s],
            device_id=(zr, c, p), device_id_type=MESH)

    def left(s):
        slot = lax.rem(z + s, NZ)
        return pltpu.make_async_remote_copy(
            src_ref=tg_ref.at[slot], dst_ref=tg_ref.at[slot],
            send_sem=ring_send.at[1, s], recv_sem=ring_recv.at[1, s],
            device_id=(zl, c, p), device_id_type=MESH)

    def forward(s):
        right(s - 1).wait_recv()
        right(s).start()
        left(s - 1).wait_recv()
        if s < 3:
            left(s).start()

    right(0).start()
    left(0).start()

    lane128 = iota((64, 128), 1)
    row64 = iota((64, 128), 0)
    bias = column(benc_ref, 16, 128)
    hi = bias.astype(BF).astype(F32)
    mid = (bias - hi).astype(BF).astype(F32)
    low = bias - hi - mid
    four = lambda x: jnp.concatenate([x] * 4, axis=0)
    fixed = jnp.where(lane128 == 6, four(hi), 0.0)
    fixed = jnp.where(lane128 == 14, four(mid), fixed)
    fixed = jnp.where(lane128 == 22, four(low), fixed)
    fixed = jnp.where((lane128 == 7) & (row64 < 16), BIG, fixed)
    fixed = jnp.where((lane128 == 15) & (row64 >= 48), BIG, fixed)
    base1 = jnp.concatenate([mm(wenc_ref[...], q1_ref[v]) for v in range(4)], axis=0)
    for r in range(8):
        w1_ref[pl.ds(r * 64, 64), :] = (
            (pltpu.roll(base1, 8 * r, 1) if r else base1) + fixed
        ).astype(BF)
    base2 = mm(wmid_ref[...], q2_ref[...])
    for r in range(8):
        w2_ref[pl.ds(r * 32, 32), :] = (
            pltpu.roll(base2, 48 * r, 1) if r else base2
        ).astype(BF)
    w3s_ref[...] = jnp.zeros(w3s_ref.shape, BF)
    for n in range(4):
        base3 = mm(wdec_ref[...], q3_ref[n])
        skip = base3[:, :256].astype(BF)
        wide = jnp.concatenate([base3[:, 256:], jnp.zeros((16, 256), F32)], axis=1)
        for r in range(4):
            w3s_ref[pl.ds(r * 64 + n * 16, 16), pl.ds(128 * r, 256)] = skip
            w3m_ref[pl.ds(r * 64 + n * 16, 16), :] = (
                pltpu.roll(wide, 96 * r, 1) if r else wide
            ).astype(BF)
    b2_ref[...] = column(bmid_ref, 32, HALF)
    b3_ref[...] = column(bdec_ref, 16, HALF)
    rep = (iota((16, 256), 1) % 16 == iota((16, 256), 0)).astype(F32).astype(BF)
    wrow = mm(wout_ref[...], rep)
    orow = iota((16, 256), 0)
    block = (orow % 8 // 2) * 4 + orow // 8 * 2 + orow % 2
    wo = jnp.where(iota((16, 256), 1) // 16 == block, wrow, 0.0).astype(BF)
    scol = iota((TL, TL), 1)
    split = jnp.where(
        iota((TL, TL), 0) == (scol % HALF) * 2 + scol // HALF, 1.0, 0.0
    ).astype(BF)
    own_ref[...] = mm(clean, split)
    alive_ref[...] = mm(diag, jnp.ones((ROWS, HALF), BF))

    for h in halos:
        h.wait_recv()
    prow = iota((80, 16), 0)
    pcol = iota((80, 16), 1)
    above = jnp.where((prow + 11 == pcol) & (c > 0), 1.0, 0.0).astype(BF)
    below = jnp.where((prow == pcol + 69) & (pcol < 5) & (c < NC - 1), 1.0, 0.0).astype(BF)
    inner = jnp.where(iota((80, 64), 0) == iota((80, 64), 1) + 5, 1.0, 0.0).astype(BF)
    tall = mm(inner, clean) + mm(above, halo_ref[0]) + mm(below, halo_ref[1])
    parted = mm(tall.astype(BF), split)
    even = parted[:, :HALF]
    odd = parted[:, HALF:]
    lane80 = iota((80, HALF), 1)
    later = lambda x, lanes: jnp.where(lanes == 0, 0.0, pltpu.roll(x, 1, 1))
    sooner = lambda x, lanes: jnp.where(lanes == HALF - 1, 0.0, pltpu.roll(x, HALF - 1, 1))
    slots = [later(even, lane80), later(odd, lane80), even, odd, sooner(even, lane80), sooner(odd, lane80)]
    slots.append(jnp.ones((80, HALF), F32))
    edge = jnp.where(iota((80, HALF), 0) % 2 == 0, 0, HALF - 1)
    slots.append(jnp.where(lane80 == edge, 1.0, 0.0))
    for n in range(8):
        for h in range(2):
            cv_ref[h, pl.ds(n, 80, stride=8), :] = slots[n][:, h * 128 : (h + 1) * 128]

    @pl.loop(0, 9)
    def _(q):
        first = pl.multiple_of(q * 64, 64)
        for h in range(2):
            window = cv_ref[h, pl.ds(first, 128), :].astype(BF)
            e = mm(w1_ref[...], window)
            ev_ref[pl.ds(pl.multiple_of(q * 512, 512), 512), h * 128 : (h + 1) * 128] = (
                jnp.maximum(e, 0.0).astype(BF)
            )

    @pl.when(c == 0)
    def _():
        ev_ref[0:256, :] = jnp.zeros((256, HALF), BF)

    @pl.when(c == NC - 1)
    def _():
        ev_ref[68 * 64 : 72 * 64, :] = jnp.zeros((256, HALF), BF)

    forward(1)

    lane16 = iota((16, HALF), 1)

    @pl.loop(0, 36, unroll=4)
    def _(i):
        first = pl.multiple_of(i * 128, 128)
        part = lambda o: ev_ref[pl.ds(first + o, 16), :].astype(F32)
        pooled = (part(16) + part(32) + part(80) + part(96)) * 0.25
        at = pl.multiple_of(i * 48, 16)
        pv_ref[pl.ds(at, 16), :] = later(pooled, lane16).astype(BF)
        pv_ref[pl.ds(at + 16, 16), :] = pooled.astype(BF)
        pv_ref[pl.ds(at + 32, 16), :] = sooner(pooled, lane16).astype(BF)

    lane32 = iota((32, HALF), 1)

    def middle(first_row, count, acc):
        for r in range(count):
            m = jnp.maximum(acc[r * 32 : (r + 1) * 32] + b2_ref[...], 0.0)
            at = pl.multiple_of((first_row + r) * 96, 32)
            mv_ref[pl.ds(at, 32), :] = later(m, lane32).astype(BF)
            mv_ref[pl.ds(at + 32, 32), :] = m.astype(BF)
            mv_ref[pl.ds(at + 64, 32), :] = sooner(m, lane32).astype(BF)

    @pl.loop(0, 4)
    def _(q):
        window = pv_ref[pl.ds(pl.multiple_of(q * 384, 128), 480), :]
        middle(q * 8, 8, mm(w2_ref[:, :480], window))

    middle(32, 2, mm(w2_ref[0:64, :192], pv_ref[pl.ds(1536, 192), :]))

    @pl.when(c == 0)
    def _():
        mv_ref[0:96, :] = jnp.zeros((96, HALF), BF)

    @pl.when(c == NC - 1)
    def _():
        mv_ref[33 * 96 : 34 * 96, :] = jnp.zeros((96, HALF), BF)

    forward(2)

    @pl.loop(0, 8)
    def _(q):
        skips = ev_ref[pl.ds(pl.multiple_of(q * 512, 512) + 192, 640), :]
        mids = mv_ref[pl.ds(pl.multiple_of(q * 384, 128), 576), :]
        acc = mm(w3s_ref[...], skips) + mm(w3m_ref[:, :576], mids)
        acc = acc.reshape(16, 16, HALF) + b3_ref[...][None]
        decoded = jnp.maximum(acc, 0.0).astype(BF).reshape(256, HALF)
        branch = mm(wo, decoded)
        here = pl.ds(pl.multiple_of(q * 8, 8), 8)
        alive = alive_ref[here, :]
        for ps in range(2):
            lanes = slice(ps * HALF, (ps + 1) * HALF)
            dp_ref[here, lanes] = alive * (
                own_ref[here, lanes] + branch[ps * 8 : ps * 8 + 8] + bout_ref[0]
            )

    forward(3)

    natural = lax.dot_general(
        dp_ref[...].astype(BF), split, (((1,), (1,)), ((), ())), preferred_element_type=F32
    ).astype(BF)
    den_ref[...] = natural
    sd_ref[...] = natural.reshape(2, 32, TL)

    to_partner = pltpu.make_async_remote_copy(
        src_ref=sd_ref.at[1 - p], dst_ref=xw_ref.at[p],
        send_sem=x_send.at[0], recv_sem=x_recv.at[0],
        device_id=(z, c, 1 - p), device_id_type=MESH)
    to_partner.start()

    def to_previous(h):
        return pltpu.make_async_remote_copy(
            src_ref=sd_ref.at[h], dst_ref=xw_ref.at[2],
            send_sem=x_send.at[1 + h], recv_sem=x_recv.at[1],
            device_id=(zl, c, h), device_id_type=MESH)

    @pl.when(p == 0)
    def _():
        to_previous(0).start()
        to_previous(1).start()

    xw_ref[p] = sd_ref[p]

    tabs[0].wait()
    for s in range(1):
        right(3).wait_recv()

    @pl.loop(0, NZ)
    def _(k):
        ts_ref[k] = mm(tg_ref[k], f_ref[...])

    to_partner.wait_recv()
    to_previous(0).wait_recv()
    rrow = iota((128, 32), 0)
    repeat = jnp.where(rrow // 4 == iota((128, 32), 1), 1.0, 0.0).astype(BF)
    lane1k = iota((128, 2 * TL), 1)
    sign = jnp.where((lane1k % 2 == 1), -1.0, 1.0)
    spectra = []
    for n in range(3):
        block_rows = xw_ref[n]
        if n == 2:
            block_rows = block_rows * jnp.where(z == NZ - 1, 0.0, 1.0).astype(BF)
        spectra.append(mm(mm(repeat, block_rows).astype(BF), f_ref[...]))
    z_ref[0] = spectra[0] + sign * spectra[1]
    z_ref[1] = spectra[1] + sign * spectra[2]

    lane512 = iota((8, TL), 1)

    @pl.loop(0, NZ)
    def _(k):
        for n in range(2):
            a = jnp.zeros((8, TL), F32)
            b = jnp.zeros((8, TL), F32)
            d = jnp.zeros((8, TL), F32)
            for s in range(16):
                here = pl.ds(s * 8, 8)
                tr = ts_ref[k, here, 0:TL]
                ti = ts_ref[k, here, TL : 2 * TL]
                sr = z_ref[n, here, 0:TL]
                si = z_ref[n, here, TL : 2 * TL]
                a = a + sr * tr
                b = b + si * ti
                d = d + (si * tr - sr * ti)
            a = a + pltpu.roll(a, 4, 0)
            b = b + pltpu.roll(b, 4, 0)
            d = d + pltpu.roll(d, 4, 0)
            at = pl.ds(pl.multiple_of(n * 64 + k * 8, 8), 8)
            g_ref[at, 0:TL] = jnp.where(lane512 == 0, a, a + b)
            g_ref[at, TL : 2 * TL] = jnp.where(lane512 == 0, b, d)

    tabs[1].wait()
    tabs[2].wait()
    g = g_ref[...]
    g_hi = g.astype(BF)
    g_lo = (g - g_hi.astype(F32)).astype(BF)
    lags = mm(g_hi, ih_ref[...]) + (mm(g_lo, ih_ref[...]) + mm(g_hi, il_ref[...]))
    for t in range(4):
        lag_ref[t] = lags[:, t * 128 : (t + 1) * 128]

    lane8 = iota((8, 128), 1) // 32
    for n in range(2):
        for t in range(4):
            quarter = [lag_ref[t, pl.ds(n * 64 + k, 8, stride=8), :] for k in range(4)]
            for o in range(4):
                piece = jnp.zeros((8, 128), F32)
                for k in range(4):
                    shift = (k - o) % 4 * 32
                    moved = pltpu.roll(quarter[k], shift, 1) if shift else quarter[k]
                    piece = jnp.where(lane8 == k, moved, piece)
                rs_ref[n * NC + t * 4 + o] = piece

    def scatter(d):
        other = lax.rem(me + d, 2 * NC)
        return pltpu.make_async_remote_copy(
            src_ref=rs_ref.at[other], dst_ref=rr_ref.at[me],
            send_sem=rs_send.at[d], recv_sem=rs_recv.at[me],
            device_id=(z, lax.rem(other, NC), other // NC), device_id_type=MESH)

    def arrival(d):
        other = lax.rem(me + d, 2 * NC)
        return pltpu.make_async_remote_copy(
            src_ref=rs_ref.at[other], dst_ref=rr_ref.at[other],
            send_sem=rs_send.at[d], recv_sem=rs_recv.at[other],
            device_id=(z, lax.rem(other, NC), other // NC), device_id_type=MESH)

    @pl.loop(1, 2 * NC)
    def _(d):
        scatter(d).start()

    @pl.loop(1, 2 * NC)
    def _(d):
        arrival(d).wait_recv()

    total = lax.fori_loop(
        1, 2 * NC, lambda d, t: t + rr_ref[lax.rem(me + d, 2 * NC)], rs_ref[me]
    )
    as_ref[...] = total.reshape(8, 1, 128)

    def spread(d):
        other = lax.rem(z + d, NZ)
        return pltpu.make_async_remote_copy(
            src_ref=as_ref.at[other], dst_ref=ar_ref.at[z],
            send_sem=a_send.at[d], recv_sem=a_recv.at[z],
            device_id=(other, c, p), device_id_type=MESH)

    def landing(d):
        other = lax.rem(z + d, NZ)
        return pltpu.make_async_remote_copy(
            src_ref=as_ref.at[other], dst_ref=ar_ref.at[other],
            send_sem=a_send.at[d], recv_sem=a_recv.at[other],
            device_id=(other, c, p), device_id_type=MESH)

    @pl.loop(1, NZ)
    def _(d):
        spread(d).start()

    ar_ref[z] = as_ref[z]

    @pl.loop(1, NZ)
    def _(d):
        landing(d).wait_recv()

    found = ar_ref[...].reshape(8, 128)
    turned = [found] + [pltpu.roll(found, 128 - 32 * k, 1) for k in range(1, 4)]
    for r in range(4):
        local = lax.rem(assign_ref[r], 4)
        row = jnp.zeros((8, 128), F32)
        for k in range(4):
            row = row + jnp.where(local == k, 1.0, 0.0) * turned[k]
        corr_ref[r] = row[:, :32]

    for h in halos:
        h.wait_send()
    for s in range(4):
        right(s).wait_send()
        if s < 3:
            left(s).wait_send()
    to_partner.wait_send()

    @pl.when(p == 0)
    def _():
        to_previous(0).wait_send()
        to_previous(1).wait_send()

    @pl.loop(1, 2 * NC)
    def _(d):
        scatter(d).wait_send()

    @pl.loop(1, NZ)
    def _(d):
        spread(d).wait_send()


def body(raw, dead_mask, templates, assign, w_enc, b_enc, w_mid, b_mid, w_dec, b_dec, w_out, b_out):
    hi, lo = lag_table()
    vm = pl.BlockSpec(memory_space=pltpu.VMEM)
    sm = pl.BlockSpec(memory_space=pltpu.SMEM)
    hbm = pl.BlockSpec(memory_space=pl.ANY)
    dma = pltpu.SemaphoreType.DMA
    denoised, corr = pl.pallas_call(
        kernel,
        out_shape=(
            jax.ShapeDtypeStruct((ROWS, TL), BF),
            jax.ShapeDtypeStruct((4, 8, 32), F32),
        ),
        in_specs=[vm, vm, vm, sm, vm, sm, vm, sm, vm, sm, vm, sm, vm, vm, vm, hbm, hbm, hbm],
        out_specs=(vm, vm),
        scratch_shapes=[
            pltpu.VMEM((TL, 2 * TL), BF),
            pltpu.VMEM((2 * TL, TL), BF),
            pltpu.VMEM((2 * TL, TL), BF),
            pltpu.VMEM((ROWS, TL), BF),
            pltpu.VMEM((2, 16, TL), BF),
            pltpu.VMEM((2, 640, 128), F32),
            pltpu.VMEM((512, 128), BF),
            pltpu.VMEM((256, 512), BF),
            pltpu.VMEM((256, 640), BF),
            pltpu.VMEM((256, 640), BF),
            pltpu.VMEM((72 * 64, HALF), BF),
            pltpu.VMEM((36 * 48, HALF), BF),
            pltpu.VMEM((34 * 96, HALF), BF),
            pltpu.VMEM((ROWS, TL), F32),
            pltpu.VMEM((ROWS, TL), F32),
            pltpu.VMEM((ROWS, HALF), F32),
            pltpu.VMEM((32, HALF), F32),
            pltpu.VMEM((16, HALF), F32),
            pltpu.VMEM((NZ, 128, TL), BF),
            pltpu.VMEM((NZ, 128, 2 * TL), F32),
            pltpu.VMEM((2, 32, TL), BF),
            pltpu.VMEM((3, 32, TL), BF),
            pltpu.VMEM((2, 128, 2 * TL), F32),
            pltpu.VMEM((128, 2 * TL), F32),
            pltpu.VMEM((4, 128, 128), F32),
            pltpu.VMEM((2 * NC, 8, 128), F32),
            pltpu.VMEM((2 * NC, 8, 128), F32),
            pltpu.VMEM((NZ, 1, 128), F32),
            pltpu.VMEM((NZ, 1, 128), F32),
            dma((3,)),
            dma((2,)),
            dma((2,)),
            dma((2, 4)),
            dma((2, 4)),
            dma((3,)),
            dma((2,)),
            dma((2 * NC,)),
            dma((2 * NC,)),
            dma((NZ,)),
            dma((NZ,)),
        ],
        compiler_params=pltpu.CompilerParams(
            collective_id=0, has_side_effects=True, vmem_limit_bytes=48 * 1024 * 1024
        ),
    )(
        raw,
        dead_mask.reshape(1, ROWS),
        templates,
        assign,
        w_enc.reshape(16, 9),
        b_enc,
        w_mid.reshape(32, 144),
        b_mid,
        w_dec.reshape(16, 432),
        b_dec,
        w_out.reshape(1, 16),
        b_out,
        jnp.asarray(encoder_table(), BF),
        jnp.asarray(middle_table(), BF),
        jnp.asarray(decoder_table(), BF),
        jnp.asarray(spectrum_table(), BF),
        jnp.asarray(hi),
        jnp.asarray(lo),
    )
    return denoised, corr.reshape(4, 8, 1, 32)


def solution(mesh):
    return jax.shard_map(
        body,
        mesh=mesh,
        in_specs=(
            P("chan", ("tmpl", "tm")),
            P("chan"),
            P("tmpl", "chan", None),
            P("tmpl"),
            P(),
            P(),
            P(),
            P(),
            P(),
            P(),
            P(),
            P(),
        ),
        out_specs=(P("chan", ("tmpl", "tm")), P("tmpl", None, "tm", "chan")),
        check_vma=False,
    )
```

```python
import functools
import math

import jax
import jax.numpy as jnp
import numpy as np
from jax import lax
from jax.experimental import pallas as pl
from jax.experimental.pallas import tpu as pltpu
from jax.sharding import PartitionSpec as P

BF = jnp.bfloat16
F32 = jnp.float32
MESH = pl.DeviceIdType.MESH
ROWS = 64
TL = 512
HALF = 256
NZ = 8
NC = 16
BIG = -1e30


def middle_table():
    q = np.zeros((3, 3, 16, 512), np.float32)
    for g in range(16):
        for rr in range(3):
            for v in range(3):
                q[rr, v, g, rr * 48 + v * 16 + g] = 1
    return q.reshape(144, 512)


def encoder_table():
    q = np.zeros((4, 3, 3, 128), np.float32)
    for v in range(4):
        for rr in range(3):
            for dt in range(3):
                q[v, rr, dt, rr * 8 + v + dt] = 1
    return q.reshape(4, 9, 128)


def decoder_tables():
    qs = np.zeros((4, 3, 3, 16, 256), np.float32)
    qm = np.zeros((4, 3, 3, 32, 384), np.float32)
    for ps in range(2):
        for pr in range(2):
            n = ps * 2 + pr
            for rr in range(4):
                for v in range(4):
                    if 0 <= rr - pr <= 2 and 0 <= v - ps <= 2:
                        for g in range(16):
                            qs[n, rr - pr, v - ps, g, rr * 64 + v * 16 + g] = 1
            for dr in range(3):
                for dt in range(3):
                    rr = (pr + dr - 1) // 2 + 1
                    v = (ps + dt - 1) // 2 + 1
                    for m in range(32):
                        qm[n, dr, dt, m, rr * 96 + v * 32 + m] = 1
    return qs.reshape(4, 144, 256), qm.reshape(4, 288, 384)


def spectrum_table():
    s = np.arange(TL)[:, None]
    f = np.arange(TL)[None, :]
    phase = ((s * f) % (2 * TL)) * (math.pi / TL)
    re = np.cos(phase)
    im = -np.sin(phase)
    im[:, 0] = np.where(np.arange(TL) % 2 == 0, 1.0, -1.0)
    return np.concatenate([re, im], axis=1).astype(np.float32)


def lag_table():
    f = np.arange(TL)[:, None]
    j = np.arange(TL)[None, :]
    phase = ((f * j) % (2 * TL)) * (math.pi / TL)
    re = np.cos(phase) * 2
    im = -np.sin(phase) * 2
    re[0] = 1
    im[0] = np.where(np.arange(TL) % 2 == 0, 1.0, -1.0)
    return (np.concatenate([re, im], axis=0) / (2 * TL)).astype(np.float32)


def iota(shape, dim):
    return lax.broadcasted_iota(jnp.int32, shape, dim)


def mm(a, b):
    return jnp.dot(a, b, preferred_element_type=F32)


def column(ref, count, lanes):
    rows = iota((count, lanes), 0)
    out = jnp.zeros((count, lanes), F32)
    for g in range(count):
        out = jnp.where(rows == g, ref[g], out)
    return out


def kernel(
    raw_hbm, mask_hbm, tmpl_hbm, assign_hbm, wenc_hbm, benc_hbm, wmid_hbm, bmid_hbm,
    wdec_hbm, bdec_hbm, wout_hbm, bout_hbm, q1_hbm, q2_hbm, q3s_hbm, q3m_hbm, f_hbm, i_hbm,
    den_ref, corr_ref,
    raw_ref, mask_ref, tmpl_ref, assign_ref, wenc_ref, benc_ref, wmid_ref, bmid_ref,
    wdec_ref, bdec_ref, wout_ref, bout_ref, q1_ref, q2_ref, q3s_ref, q3m_ref, f_ref, i_ref,
    clean_ref, halo_ref, cv_ref, w1_ref, w2_ref, w3s_ref, w3m_ref,
    ev_ref, pv_ref, mv_ref, dp_ref, own_ref, alive_ref, b2_ref, b3_ref, tg_ref, ts_ref, sd_ref, xw_ref,
    xr_ref, z_ref, g_ref, lag_ref, rs_ref, rr_ref, as_ref, ar_ref,
    tab_sem, halo_send, halo_recv, ring_send, ring_recv, x_send, x_recv,
    rs_send, rs_recv, a_send, a_recv,
):
    z = lax.axis_index("tmpl")
    c = lax.axis_index("chan")
    p = lax.axis_index("tm")
    me = p * NC + c
    zr = lax.rem(z + 1, NZ)
    zl = lax.rem(z + NZ - 1, NZ)

    loads = {}
    for n, (name, source, target) in enumerate([
        ("raw", raw_hbm, raw_ref), ("mask", mask_hbm, mask_ref), ("tmpl", tmpl_hbm, tmpl_ref),
        ("wenc", wenc_hbm, wenc_ref), ("q1", q1_hbm, q1_ref), ("benc", benc_hbm, benc_ref),
        ("wmid", wmid_hbm, wmid_ref), ("q2", q2_hbm, q2_ref), ("bmid", bmid_hbm, bmid_ref),
        ("wdec", wdec_hbm, wdec_ref), ("q3s", q3s_hbm, q3s_ref), ("q3m", q3m_hbm, q3m_ref),
        ("bdec", bdec_hbm, bdec_ref), ("wout", wout_hbm, wout_ref), ("bout", bout_hbm, bout_ref),
        ("f", f_hbm, f_ref), ("assign", assign_hbm, assign_ref), ("i", i_hbm, i_ref),
    ]):
        loads[name] = pltpu.make_async_copy(source, target, tab_sem.at[n])
        loads[name].start()

    def ready(*names):
        for name in names:
            loads[name].wait()

    barrier = pltpu.get_barrier_semaphore()

    def signal(dz, dc, dp):
        pl.semaphore_signal(barrier, inc=1, device_id=(dz, dc, dp), device_id_type=MESH)

    @pl.loop(1, 2 * NC)
    def _(d):
        other = lax.rem(me + d, 2 * NC)
        signal(z, lax.rem(other, NC), other // NC)

    @pl.loop(1, NZ)
    def _(d):
        signal(lax.rem(z + d, NZ), c, p)

    signal(zr, c, 1 - p)
    signal(zl, c, 1 - p)

    ready("raw", "mask")
    mask = mask_ref[...].astype(F32)
    diag = jnp.where(iota((ROWS, ROWS), 0) == iota((ROWS, ROWS), 1), mask, 0.0).astype(BF)
    clean = mm(diag, raw_ref[...]).astype(BF)
    clean_ref[...] = clean

    pl.semaphore_wait(barrier, 2 * NC - 1 + NZ - 1 + 2)

    up = lax.rem(c + NC - 1, NC)
    down = lax.rem(c + 1, NC)
    halos = [
        pltpu.make_async_remote_copy(
            src_ref=clean_ref.at[pl.ds(0, 16)], dst_ref=halo_ref.at[1],
            send_sem=halo_send.at[0], recv_sem=halo_recv.at[0],
            device_id=(z, up, p), device_id_type=MESH),
        pltpu.make_async_remote_copy(
            src_ref=clean_ref.at[pl.ds(48, 16)], dst_ref=halo_ref.at[0],
            send_sem=halo_send.at[1], recv_sem=halo_recv.at[1],
            device_id=(z, down, p), device_id_type=MESH),
    ]
    for h in halos:
        h.start()

    ready("tmpl")
    rows = iota((128, 256), 0)
    pick = (rows % 4) * 64 + p * 32 + rows // 4 == iota((128, 256), 1)
    tg_ref[0] = mm(jnp.where(pick, 1.0, 0.0).astype(BF), tmpl_ref[...].reshape(256, TL)).astype(BF)

    def right(s):
        part = pl.ds(0, 64 if s == 3 else 128)
        return pltpu.make_async_remote_copy(
            src_ref=tg_ref.at[s, part], dst_ref=tg_ref.at[s + 1, part],
            send_sem=ring_send.at[0, s], recv_sem=ring_recv.at[0, s],
            device_id=(zr, c, p), device_id_type=MESH)

    def left(s):
        part = pl.ds(64, 64) if s == 3 else pl.ds(0, 128)
        return pltpu.make_async_remote_copy(
            src_ref=tg_ref.at[(NZ - s) % NZ, part], dst_ref=tg_ref.at[NZ - 1 - s, part],
            send_sem=ring_send.at[1, s], recv_sem=ring_recv.at[1, s],
            device_id=(zl, c, p), device_id_type=MESH)

    def forward(s):
        right(s - 1).wait_recv()
        right(s).start()
        left(s - 1).wait_recv()
        left(s).start()

    right(0).start()
    left(0).start()

    scol = iota((TL, TL), 1)
    split = jnp.where(
        iota((TL, TL), 0) == (scol % HALF) * 2 + scol // HALF, 1.0, 0.0
    ).astype(BF)
    later = lambda x, lanes: jnp.where(lanes == 0, 0.0, pltpu.roll(x, 1, 1))
    sooner = lambda x, lanes: jnp.where(lanes == HALF - 1, 0.0, pltpu.roll(x, HALF - 1, 1))

    def variants(tall):
        parted = mm(tall.astype(BF), split)
        even = parted[:, :HALF]
        odd = parted[:, HALF:]
        lanes = iota(even.shape, 1)
        return [
            later(even, lanes), later(odd, lanes), even, odd, sooner(even, lanes), sooner(odd, lanes)
        ]

    inner = jnp.where(iota((80, 64), 0) == iota((80, 64), 1) + 5, 1.0, 0.0).astype(BF)
    slots = variants(mm(inner, clean))
    slots.append(jnp.ones((80, HALF), F32))
    edge = jnp.where(iota((80, HALF), 0) % 2 == 0, 0, HALF - 1)
    slots.append(jnp.where(iota((80, HALF), 1) == edge, 1.0, 0.0))
    for n in range(8):
        for h in range(2):
            cv_ref[h, pl.ds(n, 80, stride=8), :] = slots[n][:, h * 128 : (h + 1) * 128]

    ready("wenc", "q1", "benc")
    lane128 = iota((64, 128), 1)
    row64 = iota((64, 128), 0)
    bias = column(benc_ref, 16, 128)
    hi = bias.astype(BF).astype(F32)
    mid = (bias - hi).astype(BF).astype(F32)
    low = bias - hi - mid
    four = lambda x: jnp.concatenate([x] * 4, axis=0)
    fixed = jnp.where(lane128 == 6, four(hi), 0.0)
    fixed = jnp.where(lane128 == 14, four(mid), fixed)
    fixed = jnp.where(lane128 == 22, four(low), fixed)
    fixed = jnp.where((lane128 == 7) & (row64 < 16), BIG, fixed)
    fixed = jnp.where((lane128 == 15) & (row64 >= 48), BIG, fixed)
    wenc = jnp.concatenate([wenc_ref[r] for r in range(3)], axis=0)
    over = lambda w, q: lax.dot_general(w, q, (((0,), (0,)), ((), ())), preferred_element_type=F32)
    base1 = jnp.concatenate([over(wenc, q1_ref[v]) for v in range(4)], axis=0)
    for r in range(8):
        w1_ref[pl.ds(r * 64, 64), :] = (
            (pltpu.roll(base1, 8 * r, 1) if r else base1) + fixed
        ).astype(BF)

    def encode(q):
        first = pl.multiple_of(q * 64, 64)
        for h in range(2):
            window = cv_ref[h, pl.ds(first, 128), :].astype(BF)
            e = mm(w1_ref[...], window)
            ev_ref[pl.ds(pl.multiple_of(q * 512, 512), 512), h * 128 : (h + 1) * 128] = (
                jnp.maximum(e, 0.0).astype(BF)
            )

    pl.loop(1, 8)(encode)

    lane16 = iota((16, HALF), 1)

    def pool(i):
        first = pl.multiple_of(i * 128, 128)
        part = lambda o: ev_ref[pl.ds(first + o, 16), :].astype(F32)
        pooled = (part(16) + part(32) + part(80) + part(96)) * 0.25
        at = pl.multiple_of(i * 48, 16)
        pv_ref[pl.ds(at, 16), :] = later(pooled, lane16).astype(BF)
        pv_ref[pl.ds(at + 16, 16), :] = pooled.astype(BF)
        pv_ref[pl.ds(at + 32, 16), :] = sooner(pooled, lane16).astype(BF)

    pl.loop(4, 32, unroll=4)(pool)

    for h in halos:
        h.wait_recv()
    far = iota((24, 16), 0)
    far = jnp.where(far < 8, far, far + 56)
    away = iota((24, 16), 1)
    above = jnp.where((far + 11 == away) & (c > 0), 1.0, 0.0).astype(BF)
    below = jnp.where((far == away + 69) & (away < 5) & (c < NC - 1), 1.0, 0.0).astype(BF)
    near = iota((24, 64), 0)
    near = jnp.where(near < 8, near, near + 56)
    kept = jnp.where(near == iota((24, 64), 1) + 5, 1.0, 0.0).astype(BF)
    edges = variants(mm(kept, clean) + mm(above, halo_ref[0]) + mm(below, halo_ref[1]))
    for n in range(6):
        for h in range(2):
            cut = edges[n][:, h * 128 : (h + 1) * 128]
            cv_ref[h, pl.ds(n, 8, stride=8), :] = cut[:8]
            cv_ref[h, pl.ds(512 + n, 16, stride=8), :] = cut[8:]
    encode(0)
    encode(8)

    @pl.when(c == 0)
    def _():
        ev_ref[0:256, :] = jnp.zeros((256, HALF), BF)

    @pl.when(c == NC - 1)
    def _():
        ev_ref[68 * 64 : 72 * 64, :] = jnp.zeros((256, HALF), BF)

    for i in (0, 1, 2, 3, 32, 33, 34, 35):
        pool(i)

    forward(1)

    ready("wmid", "q2", "bmid")
    base2 = over(wmid_ref[...].reshape(144, 32), q2_ref[...])
    for r in range(8):
        w2_ref[pl.ds(r * 32, 32), :] = (
            pltpu.roll(base2, 48 * r, 1) if r else base2
        ).astype(BF)
    b2_ref[...] = column(bmid_ref, 32, HALF)

    lane32 = iota((32, HALF), 1)

    def middle(first_row, count, acc):
        for r in range(count):
            m = jnp.maximum(acc[r * 32 : (r + 1) * 32] + b2_ref[...], 0.0)
            at = pl.multiple_of((first_row + r) * 96, 32)
            mv_ref[pl.ds(at, 32), :] = later(m, lane32).astype(BF)
            mv_ref[pl.ds(at + 32, 32), :] = m.astype(BF)
            mv_ref[pl.ds(at + 64, 32), :] = sooner(m, lane32).astype(BF)

    @pl.loop(0, 4)
    def _(q):
        window = pv_ref[pl.ds(pl.multiple_of(q * 384, 128), 480), :]
        middle(q * 8, 8, mm(w2_ref[:, :480], window))

    middle(32, 2, mm(w2_ref[0:64, :192], pv_ref[pl.ds(1536, 192), :]))

    @pl.when(c == 0)
    def _():
        mv_ref[0:96, :] = jnp.zeros((96, HALF), BF)

    @pl.when(c == NC - 1)
    def _():
        mv_ref[33 * 96 : 34 * 96, :] = jnp.zeros((96, HALF), BF)

    ready("wdec", "q3s", "q3m", "bdec", "wout", "bout")
    taps = [wdec_ref[dr, dt] for dr in range(3) for dt in range(3)]
    wskip = jnp.concatenate([t[:, 32:] for t in taps], axis=1)
    wup = jnp.concatenate([t[:, :32] for t in taps], axis=1)
    w3s_ref[...] = jnp.zeros(w3s_ref.shape, BF)
    for n in range(4):
        skip = mm(wskip, q3s_ref[n]).astype(BF)
        wide = jnp.concatenate([mm(wup, q3m_ref[n]), jnp.zeros((16, 256), F32)], axis=1)
        for r in range(4):
            w3s_ref[pl.ds(r * 64 + n * 16, 16), pl.ds(128 * r, 256)] = skip
            w3m_ref[pl.ds(r * 64 + n * 16, 16), :] = (
                pltpu.roll(wide, 96 * r, 1) if r else wide
            ).astype(BF)
    b3_ref[...] = column(bdec_ref, 16, HALF)
    rep = (iota((16, 256), 1) % 16 == iota((16, 256), 0)).astype(F32).astype(BF)
    wrow = mm(wout_ref[...], rep)
    orow = iota((16, 256), 0)
    block = (orow % 8 // 2) * 4 + orow // 8 * 2 + orow % 2
    wo = jnp.where(iota((16, 256), 1) // 16 == block, wrow, 0.0).astype(BF)
    own_ref[...] = mm(clean, split)
    alive_ref[...] = mm(diag, jnp.ones((ROWS, HALF), BF))

    def decode(q):
        skips = ev_ref[pl.ds(pl.multiple_of(q * 512, 512) + 192, 640), :]
        mids = mv_ref[pl.ds(pl.multiple_of(q * 384, 128), 576), :]
        acc = mm(w3s_ref[...], skips) + mm(w3m_ref[:, :576], mids)
        acc = acc.reshape(16, 16, HALF) + b3_ref[...][None]
        decoded = jnp.maximum(acc, 0.0).astype(BF).reshape(256, HALF)
        branch = mm(wo, decoded)
        here = pl.ds(pl.multiple_of(q * 8, 8), 8)
        alive = alive_ref[here, :]
        for ps in range(2):
            lanes = slice(ps * HALF, (ps + 1) * HALF)
            dp_ref[here, lanes] = alive * (
                own_ref[here, lanes] + branch[ps * 8 : ps * 8 + 8] + bout_ref[0]
            )

    def finish(h):
        here = pl.ds(pl.multiple_of(h * 32, 32), 32)
        natural = lax.dot_general(
            dp_ref[here, :].astype(BF), split, (((1,), (1,)), ((), ())), preferred_element_type=F32
        ).astype(BF)
        den_ref[here, :] = natural
        sd_ref[h] = natural

    to_partner = pltpu.make_async_remote_copy(
        src_ref=sd_ref.at[1 - p], dst_ref=xw_ref.at[p],
        send_sem=x_send.at[0], recv_sem=x_recv.at[0],
        device_id=(z, c, 1 - p), device_id_type=MESH)

    def to_previous(h):
        return pltpu.make_async_remote_copy(
            src_ref=sd_ref.at[h], dst_ref=xw_ref.at[2],
            send_sem=x_send.at[1 + h], recv_sem=x_recv.at[1],
            device_id=(zl, c, h), device_id_type=MESH)

    other_half = (1 - p) * 4
    pl.loop(other_half, other_half + 4)(decode)
    finish(1 - p)
    to_partner.start()

    @pl.when(p == 0)
    def _():
        to_previous(1).start()

    forward(2)

    own_half = p * 4
    pl.loop(own_half, own_half + 4)(decode)
    finish(p)

    @pl.when(p == 0)
    def _():
        to_previous(0).start()

    xw_ref[p] = sd_ref[p]

    forward(3)

    ready("f")
    wide3 = mm(tg_ref[0:4].reshape(512, TL), f_ref[...])
    ts_ref[0:4] = wide3.reshape(4, 128, 2 * TL)
    wide3 = mm(tg_ref[5:8].reshape(384, TL), f_ref[...])
    ts_ref[5:8] = wide3.reshape(3, 128, 2 * TL)
    right(3).wait_recv()
    left(3).wait_recv()
    ts_ref[4] = mm(tg_ref[4], f_ref[...])

    rrow = iota((128, 32), 0)
    repeat = jnp.where(rrow // 4 == iota((128, 32), 1), 1.0, 0.0).astype(BF)
    lane1k = iota((128, 2 * TL), 1)
    sign = jnp.where((lane1k % 2 == 1), -1.0, 1.0)
    to_partner.wait_recv()
    to_previous(0).wait_recv()
    for n in range(3):
        block_rows = xw_ref[n]
        if n == 2:
            block_rows = block_rows * jnp.where(z == NZ - 1, 0.0, 1.0).astype(BF)
        xr_ref[pl.ds(n * 128, 128), :] = mm(repeat, block_rows).astype(BF)
    spectra = mm(xr_ref[...], f_ref[...])
    z_ref[0] = spectra[0:128] + sign * spectra[128:256]
    z_ref[1] = spectra[128:256] + sign * spectra[256:384]

    lane512 = iota((8, TL), 1)

    @pl.loop(0, NZ)
    def _(k):
        for n in range(2):
            a = jnp.zeros((8, TL), F32)
            b = jnp.zeros((8, TL), F32)
            d = jnp.zeros((8, TL), F32)
            for s in range(16):
                here = pl.ds(s * 8, 8)
                tr = ts_ref[k, here, 0:TL]
                ti = ts_ref[k, here, TL : 2 * TL]
                sr = z_ref[n, here, 0:TL]
                si = z_ref[n, here, TL : 2 * TL]
                a = a + sr * tr
                b = b + si * ti
                d = d + (si * tr - sr * ti)
            a = a + pltpu.roll(a, 4, 0)
            b = b + pltpu.roll(b, 4, 0)
            d = d + pltpu.roll(d, 4, 0)
            at = pl.ds(pl.multiple_of(n * 64 + k * 8, 8), 8)
            g_ref[at, 0:TL] = jnp.where(lane512 == 0, a, a + b)
            g_ref[at, TL : 2 * TL] = jnp.where(lane512 == 0, b, d)

    ready("i")
    lags = mm(g_ref[...].astype(BF), i_ref[...])
    for t in range(4):
        lag_ref[t] = lags[:, t * 128 : (t + 1) * 128]

    lane8 = iota((8, 128), 1) // 32
    for n in range(2):
        for t in range(4):
            quarter = [lag_ref[t, pl.ds(n * 64 + k, 8, stride=8), :] for k in range(4)]
            for o in range(4):
                piece = jnp.zeros((8, 128), F32)
                for k in range(4):
                    shift = (k - o) % 4 * 32
                    moved = pltpu.roll(quarter[k], shift, 1) if shift else quarter[k]
                    piece = jnp.where(lane8 == k, moved, piece)
                rs_ref[n * NC + t * 4 + o] = piece

    @pl.loop(1, 2 * NC)
    def _(d):
        other = lax.rem(me + d, 2 * NC)
        pltpu.make_async_remote_copy(
            src_ref=rs_ref.at[other], dst_ref=rr_ref.at[d - 1],
            send_sem=rs_send.at[0], recv_sem=rs_recv.at[0],
            device_id=(z, lax.rem(other, NC), other // NC), device_id_type=MESH).start()

    shares = pltpu.make_async_remote_copy(
        src_ref=rr_ref, dst_ref=rr_ref, send_sem=rs_send.at[0], recv_sem=rs_recv.at[0],
        device_id=(z, c, 1 - p), device_id_type=MESH)
    shares.wait_recv()
    parts = [rs_ref[me]] + [rr_ref[d] for d in range(2 * NC - 1)]
    while len(parts) > 1:
        parts = [parts[n] + parts[n + 1] for n in range(0, len(parts), 2)]
    as_ref[...] = parts[0].reshape(8, 1, 128)

    for d in range(1, NZ):
        pltpu.make_async_remote_copy(
            src_ref=as_ref.at[d], dst_ref=ar_ref.at[z],
            send_sem=a_send.at[d], recv_sem=a_recv.at[z],
            device_id=(lax.rem(z + NZ - d, NZ), c, p), device_id_type=MESH).start()

    ar_ref[z] = as_ref[0]

    def landing(d):
        other = lax.rem(z + d, NZ)
        return pltpu.make_async_remote_copy(
            src_ref=as_ref.at[d], dst_ref=ar_ref.at[other],
            send_sem=a_send.at[d], recv_sem=a_recv.at[other],
            device_id=(other, c, p), device_id_type=MESH)

    for d in range(1, NZ):
        landing(d).wait_recv()

    found = ar_ref[...].reshape(8, 128)
    turned = [found] + [pltpu.roll(found, 128 - 32 * k, 1) for k in range(1, 4)]
    ready("assign")
    for r in range(4):
        local = lax.rem(assign_ref[r], 4)
        row = jnp.zeros((8, 128), F32)
        for k in range(4):
            row = row + jnp.where(local == k, 1.0, 0.0) * turned[k]
        corr_ref[r] = row[:, :32].reshape(8, 1, 32)

    for h in halos:
        h.wait_send()
    for s in range(4):
        right(s).wait_send()
        left(s).wait_send()
    to_partner.wait_send()

    @pl.when(p == 0)
    def _():
        to_previous(0).wait_send()
        to_previous(1).wait_send()

    shares.wait_send()
    for d in range(1, NZ):
        landing(d).wait_send()


def body(raw, dead_mask, templates, assign, w_enc, b_enc, w_mid, b_mid, w_dec, b_dec, w_out, b_out):
    vm = pl.BlockSpec(memory_space=pltpu.VMEM)
    hbm = pl.BlockSpec(memory_space=pltpu.HBM)
    dma = pltpu.SemaphoreType.DMA
    q3s, q3m = decoder_tables()
    tables = [
        jnp.asarray(t, BF)
        for t in (encoder_table(), middle_table(), q3s, q3m, spectrum_table(), lag_table())
    ]
    operands = [
        raw,
        dead_mask.reshape(1, ROWS),
        templates,
        assign,
        w_enc.transpose(1, 2, 3, 0).reshape(3, 3, 16),
        b_enc,
        w_mid.transpose(2, 3, 1, 0),
        b_mid,
        w_dec.transpose(2, 3, 0, 1),
        b_dec,
        w_out.reshape(1, 16),
        b_out,
    ] + tables
    scalars = (3, 5, 7, 9, 11)
    landing_places = [
        (pltpu.SMEM if n in scalars else pltpu.VMEM)(x.shape, x.dtype)
        for n, x in enumerate(operands)
    ]
    return pl.pallas_call(
        kernel,
        out_shape=(
            jax.ShapeDtypeStruct((ROWS, TL), BF),
            jax.ShapeDtypeStruct((4, 8, 1, 32), F32),
        ),
        in_specs=[hbm] * len(operands),
        out_specs=(vm, vm),
        scratch_shapes=landing_places + [
            pltpu.VMEM((ROWS, TL), BF),
            pltpu.VMEM((2, 16, TL), BF),
            pltpu.VMEM((2, 640, 128), F32),
            pltpu.VMEM((512, 128), BF),
            pltpu.VMEM((256, 512), BF),
            pltpu.VMEM((256, 640), BF),
            pltpu.VMEM((256, 640), BF),
            pltpu.VMEM((72 * 64, HALF), BF),
            pltpu.VMEM((36 * 48, HALF), BF),
            pltpu.VMEM((34 * 96, HALF), BF),
            pltpu.VMEM((ROWS, TL), F32),
            pltpu.VMEM((ROWS, TL), F32),
            pltpu.VMEM((ROWS, HALF), F32),
            pltpu.VMEM((32, HALF), F32),
            pltpu.VMEM((16, HALF), F32),
            pltpu.VMEM((NZ, 128, TL), BF),
            pltpu.VMEM((NZ, 128, 2 * TL), F32),
            pltpu.VMEM((2, 32, TL), BF),
            pltpu.VMEM((3, 32, TL), BF),
            pltpu.VMEM((384, TL), BF),
            pltpu.VMEM((2, 128, 2 * TL), F32),
            pltpu.VMEM((128, 2 * TL), F32),
            pltpu.VMEM((4, 128, 128), F32),
            pltpu.VMEM((2 * NC, 8, 128), F32),
            pltpu.VMEM((2 * NC - 1, 8, 128), F32),
            pltpu.VMEM((NZ, 1, 128), F32),
            pltpu.VMEM((NZ, 1, 128), F32),
            dma((len(operands),)),
            dma((2,)),
            dma((2,)),
            dma((2, 4)),
            dma((2, 4)),
            dma((3,)),
            dma((2,)),
            dma((1,)),
            dma((1,)),
            dma((NZ,)),
            dma((NZ,)),
        ],
        compiler_params=pltpu.CompilerParams(
            collective_id=0, has_side_effects=True, vmem_limit_bytes=56 * 1024 * 1024
        ),
    )(*operands)


def solution(mesh):
    return jax.shard_map(
        body,
        mesh=mesh,
        in_specs=(
            P("chan", ("tmpl", "tm")),
            P("chan"),
            P("tmpl", "chan", None),
            P("tmpl"),
            P(),
            P(),
            P(),
            P(),
            P(),
            P(),
            P(),
            P(),
        ),
        out_specs=(P("chan", ("tmpl", "tm")), P("tmpl", None, "tm", "chan")),
        check_vma=False,
    )
```

```python
import functools
import math

import jax
import jax.numpy as jnp
import numpy as np
from jax import lax
from jax.experimental import pallas as pl
from jax.experimental.pallas import tpu as pltpu
from jax.sharding import PartitionSpec as P

BF = jnp.bfloat16
F32 = jnp.float32
MESH = pl.DeviceIdType.MESH
ROWS = 64
TL = 512
HALF = 256
NZ = 8
NC = 16
BIG = -1e30


def middle_table():
    q = np.zeros((3, 3, 16, 512), np.float32)
    for g in range(16):
        for rr in range(3):
            for v in range(3):
                q[rr, v, g, rr * 48 + v * 16 + g] = 1
    return q.reshape(144, 512)


def encoder_table():
    q = np.zeros((4, 3, 3, 128), np.float32)
    for v in range(4):
        for rr in range(3):
            for dt in range(3):
                q[v, rr, dt, rr * 8 + v + dt] = 1
    return q.reshape(4, 9, 128)


def decoder_tables():
    qs = np.zeros((4, 3, 3, 16, 256), np.float32)
    qm = np.zeros((4, 3, 3, 32, 384), np.float32)
    for ps in range(2):
        for pr in range(2):
            n = ps * 2 + pr
            for rr in range(4):
                for v in range(4):
                    if 0 <= rr - pr <= 2 and 0 <= v - ps <= 2:
                        for g in range(16):
                            qs[n, rr - pr, v - ps, g, rr * 64 + v * 16 + g] = 1
            for dr in range(3):
                for dt in range(3):
                    rr = (pr + dr - 1) // 2 + 1
                    v = (ps + dt - 1) // 2 + 1
                    for m in range(32):
                        qm[n, dr, dt, m, rr * 96 + v * 32 + m] = 1
    return qs.reshape(4, 144, 256), qm.reshape(4, 288, 384)


def spectrum_table():
    s = np.arange(TL)[:, None]
    f = np.arange(TL)[None, :]
    phase = ((s * f) % (2 * TL)) * (math.pi / TL)
    re = np.cos(phase)
    im = -np.sin(phase)
    im[:, 0] = np.where(np.arange(TL) % 2 == 0, 1.0, -1.0)
    return np.concatenate([re, im], axis=1).astype(np.float32)


def lag_table():
    f = np.arange(TL)[:, None]
    j = np.arange(TL)[None, :]
    phase = ((f * j) % (2 * TL)) * (math.pi / TL)
    re = np.cos(phase) * 2
    im = -np.sin(phase) * 2
    re[0] = 1
    im[0] = np.where(np.arange(TL) % 2 == 0, 1.0, -1.0)
    return (np.concatenate([re, im], axis=0) / (2 * TL)).astype(np.float32)


def iota(shape, dim):
    return lax.broadcasted_iota(jnp.int32, shape, dim)


def mm(a, b):
    return jnp.dot(a, b, preferred_element_type=F32)


def column(ref, count, lanes):
    rows = iota((count, lanes), 0)
    out = jnp.zeros((count, lanes), F32)
    for g in range(count):
        out = jnp.where(rows == g, ref[g], out)
    return out


def kernel(
    raw_hbm, mask_hbm, tmpl_hbm, assign_hbm, wenc_hbm, benc_hbm, wmid_hbm, bmid_hbm,
    wdec_hbm, bdec_hbm, wout_hbm, bout_hbm, q1_hbm, q2_hbm, q3s_hbm, q3m_hbm, f_hbm, i_hbm,
    den_ref, corr_ref,
    raw_ref, mask_ref, tmpl_ref, assign_ref, wenc_ref, benc_ref, wmid_ref, bmid_ref,
    wdec_ref, bdec_ref, wout_ref, bout_ref, q1_ref, q2_ref, q3s_ref, q3m_ref, f_ref, i_ref,
    clean_ref, halo_ref, cv_ref, w1_ref, w2_ref, w3s_ref, w3m_ref,
    ev_ref, pv_ref, mv_ref, dp_ref, own_ref, alive_ref, b2_ref, b3_ref, tg_ref, ts_ref, sd_ref, xw_ref,
    xr_ref, z_ref, g_ref, lag_ref, rs_ref, rr_ref, as_ref, ar_ref,
    tab_sem, den_sem, halo_send, halo_recv, ring_send, ring_recv, x_send, x_recv,
    rs_send, rs_recv, a_send, a_recv,
):
    z = lax.axis_index("tmpl")
    c = lax.axis_index("chan")
    p = lax.axis_index("tm")
    me = p * NC + c
    zr = lax.rem(z + 1, NZ)
    zl = lax.rem(z + NZ - 1, NZ)

    loads = {}
    for n, (name, source, target) in enumerate([
        ("raw", raw_hbm, raw_ref), ("mask", mask_hbm, mask_ref), ("tmpl", tmpl_hbm, tmpl_ref),
        ("wenc", wenc_hbm, wenc_ref), ("q1", q1_hbm, q1_ref), ("benc", benc_hbm, benc_ref),
        ("wmid", wmid_hbm, wmid_ref), ("q2", q2_hbm, q2_ref), ("bmid", bmid_hbm, bmid_ref),
        ("wdec", wdec_hbm, wdec_ref), ("q3s", q3s_hbm, q3s_ref), ("q3m", q3m_hbm, q3m_ref),
        ("bdec", bdec_hbm, bdec_ref), ("wout", wout_hbm, wout_ref), ("bout", bout_hbm, bout_ref),
        ("f", f_hbm, f_ref), ("assign", assign_hbm, assign_ref), ("i", i_hbm, i_ref),
    ]):
        loads[name] = pltpu.make_async_copy(source, target, tab_sem.at[n])
        loads[name].start()

    def ready(*names):
        for name in names:
            loads[name].wait()

    barrier = pltpu.get_barrier_semaphore()

    def signal(dz, dc, dp):
        pl.semaphore_signal(barrier, inc=1, device_id=(dz, dc, dp), device_id_type=MESH)

    @pl.loop(1, 2 * NC)
    def _(d):
        other = lax.rem(me + d, 2 * NC)
        signal(z, lax.rem(other, NC), other // NC)

    @pl.loop(1, NZ)
    def _(d):
        signal(lax.rem(z + d, NZ), c, p)

    signal(zr, c, 1 - p)
    signal(zl, c, 1 - p)

    ready("raw", "mask")
    mask = mask_ref[...].astype(F32)
    diag = jnp.where(iota((ROWS, ROWS), 0) == iota((ROWS, ROWS), 1), mask, 0.0).astype(BF)
    clean = mm(diag, raw_ref[...]).astype(BF)
    clean_ref[...] = clean

    ready("tmpl")
    rows = iota((128, 256), 0)
    pick = (rows % 4) * 64 + p * 32 + rows // 4 == iota((128, 256), 1)
    tg_ref[0] = mm(jnp.where(pick, 1.0, 0.0).astype(BF), tmpl_ref[...].reshape(256, TL)).astype(BF)

    pl.semaphore_wait(barrier, 2 * NC - 1 + NZ - 1 + 2)

    up = lax.rem(c + NC - 1, NC)
    down = lax.rem(c + 1, NC)
    halos = [
        pltpu.make_async_remote_copy(
            src_ref=clean_ref.at[pl.ds(0, 16)], dst_ref=halo_ref.at[1],
            send_sem=halo_send.at[0], recv_sem=halo_recv.at[0],
            device_id=(z, up, p), device_id_type=MESH),
        pltpu.make_async_remote_copy(
            src_ref=clean_ref.at[pl.ds(48, 16)], dst_ref=halo_ref.at[0],
            send_sem=halo_send.at[1], recv_sem=halo_recv.at[1],
            device_id=(z, down, p), device_id_type=MESH),
    ]
    for h in halos:
        h.start()

    def right(s, n):
        part = pl.ds(n * 64, 64)
        return pltpu.make_async_remote_copy(
            src_ref=tg_ref.at[max(2 * s - 1, 0), part], dst_ref=tg_ref.at[2 * s + 1, part],
            send_sem=ring_send.at[0, 2 * s + n], recv_sem=ring_recv.at[0, 2 * s + n],
            device_id=(zr, c, p), device_id_type=MESH)

    def left(s, n):
        part = pl.ds(n * 64, 64)
        return pltpu.make_async_remote_copy(
            src_ref=tg_ref.at[2 * s, part], dst_ref=tg_ref.at[min(2 * s + 2, 7), part],
            send_sem=ring_send.at[1, 2 * s + n], recv_sem=ring_recv.at[1, 2 * s + n],
            device_id=(zl, c, p), device_id_type=MESH)

    def forward(s, n):
        right(s - 1, n).wait_recv()
        right(s, n).start()
        left(s - 1, 1 - n).wait_recv()
        left(s, 1 - n).start()

    for n in range(2):
        right(0, n).start()
        left(0, 1 - n).start()

    scol = iota((TL, TL), 1)
    split = jnp.where(
        iota((TL, TL), 0) == (scol % HALF) * 2 + scol // HALF, 1.0, 0.0
    ).astype(BF)
    later = lambda x, lanes: jnp.where(lanes == 0, 0.0, pltpu.roll(x, 1, 1))
    sooner = lambda x, lanes: jnp.where(lanes == HALF - 1, 0.0, pltpu.roll(x, HALF - 1, 1))

    def variants(tall):
        parted = mm(tall.astype(BF), split)
        even = parted[:, :HALF]
        odd = parted[:, HALF:]
        lanes = iota(even.shape, 1)
        return [
            later(even, lanes), later(odd, lanes), even, odd, sooner(even, lanes), sooner(odd, lanes)
        ]

    inner = jnp.where(iota((80, 64), 0) == iota((80, 64), 1) + 5, 1.0, 0.0).astype(BF)
    slots = variants(mm(inner, clean))
    slots.append(jnp.ones((80, HALF), F32))
    edge = jnp.where(iota((80, HALF), 0) % 2 == 0, 0, HALF - 1)
    slots.append(jnp.where(iota((80, HALF), 1) == edge, 1.0, 0.0))
    for n in range(8):
        for h in range(2):
            cv_ref[h, pl.ds(n, 80, stride=8), :] = slots[n][:, h * 128 : (h + 1) * 128]

    ready("wenc", "q1", "benc")
    lane128 = iota((64, 128), 1)
    row64 = iota((64, 128), 0)
    bias = column(benc_ref, 16, 128)
    hi = bias.astype(BF).astype(F32)
    mid = (bias - hi).astype(BF).astype(F32)
    low = bias - hi - mid
    four = lambda x: jnp.concatenate([x] * 4, axis=0)
    fixed = jnp.where(lane128 == 6, four(hi), 0.0)
    fixed = jnp.where(lane128 == 14, four(mid), fixed)
    fixed = jnp.where(lane128 == 22, four(low), fixed)
    fixed = jnp.where((lane128 == 7) & (row64 < 16), BIG, fixed)
    fixed = jnp.where((lane128 == 15) & (row64 >= 48), BIG, fixed)
    wenc = jnp.concatenate([wenc_ref[r] for r in range(3)], axis=0)
    over = lambda w, q: lax.dot_general(w, q, (((0,), (0,)), ((), ())), preferred_element_type=F32)
    base1 = jnp.concatenate([over(wenc, q1_ref[v]) for v in range(4)], axis=0)
    for r in range(8):
        w1_ref[pl.ds(r * 64, 64), :] = (
            (pltpu.roll(base1, 8 * r, 1) if r else base1) + fixed
        ).astype(BF)

    def encode(q):
        first = pl.multiple_of(q * 64, 64)
        for h in range(2):
            window = cv_ref[h, pl.ds(first, 128), :].astype(BF)
            e = mm(w1_ref[...], window)
            ev_ref[pl.ds(pl.multiple_of(q * 512, 512), 512), h * 128 : (h + 1) * 128] = (
                jnp.maximum(e, 0.0).astype(BF)
            )

    pl.loop(1, 8)(encode)

    lane16 = iota((16, HALF), 1)

    def pool(i):
        first = pl.multiple_of(i * 128, 128)
        part = lambda o: ev_ref[pl.ds(first + o, 16), :].astype(F32)
        pooled = (part(16) + part(32) + part(80) + part(96)) * 0.25
        at = pl.multiple_of(i * 48, 16)
        pv_ref[pl.ds(at, 16), :] = later(pooled, lane16).astype(BF)
        pv_ref[pl.ds(at + 16, 16), :] = pooled.astype(BF)
        pv_ref[pl.ds(at + 32, 16), :] = sooner(pooled, lane16).astype(BF)

    pl.loop(4, 32, unroll=4)(pool)

    ready("wmid", "q2", "bmid")
    base2 = over(wmid_ref[...].reshape(144, 32), q2_ref[...])
    for r in range(8):
        w2_ref[pl.ds(r * 32, 32), :] = (
            pltpu.roll(base2, 48 * r, 1) if r else base2
        ).astype(BF)
    b2_ref[...] = column(bmid_ref, 32, HALF)

    lane32 = iota((32, HALF), 1)

    def middle(first_row, count, acc):
        for r in range(count):
            m = jnp.maximum(acc[r * 32 : (r + 1) * 32] + b2_ref[...], 0.0)
            at = pl.multiple_of((first_row + r) * 96, 32)
            mv_ref[pl.ds(at, 32), :] = later(m, lane32).astype(BF)
            mv_ref[pl.ds(at + 32, 32), :] = m.astype(BF)
            mv_ref[pl.ds(at + 64, 32), :] = sooner(m, lane32).astype(BF)

    def eight(q):
        window = pv_ref[pl.ds(pl.multiple_of(q * 384, 128), 480), :]
        middle(q * 8, 8, mm(w2_ref[:, :480], window))

    pl.loop(1, 3)(eight)

    ready("wdec", "q3s", "q3m", "bdec", "wout", "bout")
    taps = [wdec_ref[dr, dt] for dr in range(3) for dt in range(3)]
    wskip = jnp.concatenate([t[:, 32:] for t in taps], axis=1)
    wup = jnp.concatenate([t[:, :32] for t in taps], axis=1)
    w3s_ref[...] = jnp.zeros(w3s_ref.shape, BF)
    for n in range(4):
        skip = mm(wskip, q3s_ref[n]).astype(BF)
        wide = jnp.concatenate([mm(wup, q3m_ref[n]), jnp.zeros((16, 256), F32)], axis=1)
        for r in range(4):
            w3s_ref[pl.ds(r * 64 + n * 16, 16), pl.ds(128 * r, 256)] = skip
            w3m_ref[pl.ds(r * 64 + n * 16, 16), :] = (
                pltpu.roll(wide, 96 * r, 1) if r else wide
            ).astype(BF)
    b3_ref[...] = column(bdec_ref, 16, HALF)
    rep = (iota((16, 256), 1) % 16 == iota((16, 256), 0)).astype(F32).astype(BF)
    wrow = mm(wout_ref[...], rep)
    orow = iota((16, 256), 0)
    block = (orow % 8 // 2) * 4 + orow // 8 * 2 + orow % 2
    wo = jnp.where(iota((16, 256), 1) // 16 == block, wrow, 0.0).astype(BF)
    own_ref[...] = mm(clean, split)
    alive_ref[...] = mm(diag, jnp.ones((ROWS, HALF), BF))

    forward(1, 0)

    def decode(q):
        skips = ev_ref[pl.ds(pl.multiple_of(q * 512, 512) + 192, 640), :]
        mids = mv_ref[pl.ds(pl.multiple_of(q * 384, 128), 576), :]
        acc = mm(w3s_ref[...], skips) + mm(w3m_ref[:, :576], mids)
        acc = acc.reshape(16, 16, HALF) + b3_ref[...][None]
        decoded = jnp.maximum(acc, 0.0).astype(BF).reshape(256, HALF)
        branch = mm(wo, decoded)
        here = pl.ds(pl.multiple_of(q * 8, 8), 8)
        alive = alive_ref[here, :]
        for ps in range(2):
            lanes = slice(ps * HALF, (ps + 1) * HALF)
            dp_ref[here, lanes] = alive * (
                own_ref[here, lanes] + branch[ps * 8 : ps * 8 + 8] + bout_ref[0]
            )

    def results(h):
        here = pl.ds(pl.multiple_of(h * 32, 32), 32)
        return pltpu.make_async_copy(sd_ref.at[h], den_ref.at[here], den_sem.at[h])

    def finish(h):
        here = pl.ds(pl.multiple_of(h * 32, 32), 32)
        natural = lax.dot_general(
            dp_ref[here, :].astype(BF), split, (((1,), (1,)), ((), ())), preferred_element_type=F32
        ).astype(BF)
        sd_ref[h] = natural
        results(h).start()

    to_partner = pltpu.make_async_remote_copy(
        src_ref=sd_ref.at[1 - p], dst_ref=xw_ref.at[p],
        send_sem=x_send.at[0], recv_sem=x_recv.at[0],
        device_id=(z, c, 1 - p), device_id_type=MESH)

    def to_previous(h):
        return pltpu.make_async_remote_copy(
            src_ref=sd_ref.at[h], dst_ref=xw_ref.at[2],
            send_sem=x_send.at[1 + h], recv_sem=x_recv.at[1],
            device_id=(zl, c, h), device_id_type=MESH)

    for q in (2, 3):
        decode(q)
    forward(1, 1)
    decode(4)

    for h in halos:
        h.wait_recv()
    far = iota((24, 16), 0)
    far = jnp.where(far < 8, far, far + 56)
    away = iota((24, 16), 1)
    above = jnp.where((far + 11 == away) & (c > 0), 1.0, 0.0).astype(BF)
    below = jnp.where((far == away + 69) & (away < 5) & (c < NC - 1), 1.0, 0.0).astype(BF)
    near = iota((24, 64), 0)
    near = jnp.where(near < 8, near, near + 56)
    kept = jnp.where(near == iota((24, 64), 1) + 5, 1.0, 0.0).astype(BF)
    edges = variants(mm(kept, clean) + mm(above, halo_ref[0]) + mm(below, halo_ref[1]))
    for n in range(6):
        for h in range(2):
            cut = edges[n][:, h * 128 : (h + 1) * 128]
            cv_ref[h, pl.ds(n, 8, stride=8), :] = cut[:8]
            cv_ref[h, pl.ds(512 + n, 16, stride=8), :] = cut[8:]
    encode(0)
    encode(8)

    @pl.when(c == 0)
    def _():
        ev_ref[0:256, :] = jnp.zeros((256, HALF), BF)

    @pl.when(c == NC - 1)
    def _():
        ev_ref[68 * 64 : 72 * 64, :] = jnp.zeros((256, HALF), BF)

    for i in (0, 1, 2, 3, 32, 33, 34, 35):
        pool(i)

    pl.loop(0, 4, step=3)(eight)
    middle(32, 2, mm(w2_ref[0:64, :192], pv_ref[pl.ds(1536, 192), :]))

    @pl.when(c == 0)
    def _():
        mv_ref[0:96, :] = jnp.zeros((96, HALF), BF)

    @pl.when(c == NC - 1)
    def _():
        mv_ref[33 * 96 : 34 * 96, :] = jnp.zeros((96, HALF), BF)

    pl.loop(5 * (1 - p), 5 * (1 - p) + 1)(decode)
    forward(2, 0)
    pl.loop(5 * (1 - p) + 1, 8 - 6 * p)(decode)
    finish(1 - p)
    to_partner.start()

    @pl.when(p == 0)
    def _():
        to_previous(1).start()

    forward(2, 1)
    pl.loop(5 * p, 2 + 6 * p)(decode)
    finish(p)

    @pl.when(p == 0)
    def _():
        to_previous(0).start()

    xw_ref[p] = sd_ref[p]

    ready("f")

    def transform(first, count):
        wide = mm(tg_ref[first : first + count].reshape(count * 128, TL), f_ref[...])
        ts_ref[first : first + count] = wide.reshape(count, 128, 2 * TL)

    transform(0, 5)

    rrow = iota((128, 32), 0)
    repeat = jnp.where(rrow // 4 == iota((128, 32), 1), 1.0, 0.0).astype(BF)
    lane1k = iota((128, 2 * TL), 1)
    sign = jnp.where((lane1k % 2 == 1), -1.0, 1.0)
    to_partner.wait_recv()
    for n in range(2):
        xr_ref[pl.ds(n * 128, 128), :] = mm(repeat, xw_ref[n]).astype(BF)
    spectra = mm(xr_ref[...], f_ref[...])
    z_ref[0] = spectra[0:128] + sign * spectra[128:256]
    z_ref[1] = spectra[128:256]

    forward(3, 0)

    lane512 = iota((8, TL), 1)

    def product(n, k):
        a = jnp.zeros((8, TL), F32)
        b = jnp.zeros((8, TL), F32)
        d = jnp.zeros((8, TL), F32)
        for s in range(16):
            here = pl.ds(s * 8, 8)
            tr = ts_ref[k, here, 0:TL]
            ti = ts_ref[k, here, TL : 2 * TL]
            sr = z_ref[n, here, 0:TL]
            si = z_ref[n, here, TL : 2 * TL]
            a = a + sr * tr
            b = b + si * ti
            d = d + (si * tr - sr * ti)
        a = a + pltpu.roll(a, 4, 0)
        b = b + pltpu.roll(b, 4, 0)
        d = d + pltpu.roll(d, 4, 0)
        at = pl.ds(pl.multiple_of(n * 64 + k * 8, 8), 8)
        g_ref[at, 0:TL] = jnp.where(lane512 == 0, a, a + b)
        g_ref[at, TL : 2 * TL] = jnp.where(lane512 == 0, b, d)

    pl.loop(0, 5)(functools.partial(product, 0))
    right(2, 1).wait_recv()
    left(2, 0).wait_recv()
    transform(5, 2)
    pl.loop(5, 7)(functools.partial(product, 0))

    to_previous(0).wait_recv()
    following = xw_ref[2] * jnp.where(z == NZ - 1, 0.0, 1.0).astype(BF)
    z_ref[1] = z_ref[1] + sign * mm(mm(repeat, following).astype(BF), f_ref[...])
    pl.loop(0, 7)(functools.partial(product, 1))
    right(3, 0).wait_recv()
    left(3, 1).wait_recv()
    transform(7, 1)
    pl.loop(0, 2)(lambda n: product(n, 7))

    ready("i")
    lags = mm(g_ref[...].astype(BF), i_ref[...])
    for t in range(4):
        lag_ref[t] = lags[:, t * 128 : (t + 1) * 128]

    lane8 = iota((8, 128), 1) // 32
    for n in range(2):
        for t in range(4):
            quarter = [lag_ref[t, pl.ds(n * 64 + k, 8, stride=8), :] for k in range(4)]
            for o in range(4):
                piece = jnp.zeros((8, 128), F32)
                for k in range(4):
                    shift = (k - o) % 4 * 32
                    moved = pltpu.roll(quarter[k], shift, 1) if shift else quarter[k]
                    piece = jnp.where(lane8 == k, moved, piece)
                rs_ref[n * NC + t * 4 + o] = piece

    @pl.loop(1, 2 * NC)
    def _(d):
        other = lax.rem(me + d, 2 * NC)
        pltpu.make_async_remote_copy(
            src_ref=rs_ref.at[other], dst_ref=rr_ref.at[d - 1],
            send_sem=rs_send.at[0], recv_sem=rs_recv.at[0],
            device_id=(z, lax.rem(other, NC), other // NC), device_id_type=MESH).start()

    shares = pltpu.make_async_remote_copy(
        src_ref=rr_ref, dst_ref=rr_ref, send_sem=rs_send.at[0], recv_sem=rs_recv.at[0],
        device_id=(z, c, 1 - p), device_id_type=MESH)
    shares.wait_recv()
    parts = [rs_ref[me]] + [rr_ref[d] for d in range(2 * NC - 1)]
    while len(parts) > 1:
        parts = [parts[n] + parts[n + 1] for n in range(0, len(parts), 2)]
    as_ref[...] = parts[0].reshape(8, 1, 128)

    places = [0, 1, -1, 2, -2, 3, -3, 4]
    for d in range(1, NZ):
        pltpu.make_async_remote_copy(
            src_ref=as_ref.at[d], dst_ref=ar_ref.at[z],
            send_sem=a_send.at[d], recv_sem=a_recv.at[z],
            device_id=(lax.rem(z + NZ - places[d], NZ), c, p), device_id_type=MESH).start()

    ar_ref[z] = as_ref[0]

    def landing(d):
        other = lax.rem(z + NZ + places[d], NZ)
        return pltpu.make_async_remote_copy(
            src_ref=as_ref.at[d], dst_ref=ar_ref.at[other],
            send_sem=a_send.at[d], recv_sem=a_recv.at[other],
            device_id=(other, c, p), device_id_type=MESH)

    for d in range(1, NZ):
        landing(d).wait_recv()

    found = ar_ref[...].reshape(8, 128)
    turned = [found] + [pltpu.roll(found, 128 - 32 * k, 1) for k in range(1, 4)]
    ready("assign")
    for r in range(4):
        local = lax.rem(assign_ref[r], 4)
        row = jnp.zeros((8, 128), F32)
        for k in range(4):
            row = row + jnp.where(local == k, 1.0, 0.0) * turned[k]
        corr_ref[r] = row[:, :32].reshape(8, 1, 32)

    results(0).wait()
    results(1).wait()
    for h in halos:
        h.wait_send()
    for s in range(3):
        for n in range(2):
            right(s, n).wait_send()
            left(s, n).wait_send()
    right(3, 0).wait_send()
    left(3, 1).wait_send()
    to_partner.wait_send()

    @pl.when(p == 0)
    def _():
        to_previous(0).wait_send()
        to_previous(1).wait_send()

    shares.wait_send()
    for d in range(1, NZ):
        landing(d).wait_send()


def body(raw, dead_mask, templates, assign, w_enc, b_enc, w_mid, b_mid, w_dec, b_dec, w_out, b_out):
    vm = pl.BlockSpec(memory_space=pltpu.VMEM)
    hbm = pl.BlockSpec(memory_space=pltpu.HBM)
    dma = pltpu.SemaphoreType.DMA
    q3s, q3m = decoder_tables()
    tables = [
        jnp.asarray(t, BF)
        for t in (encoder_table(), middle_table(), q3s, q3m, spectrum_table(), lag_table())
    ]
    operands = [
        raw,
        dead_mask.reshape(1, ROWS),
        templates,
        assign,
        w_enc.transpose(1, 2, 3, 0).reshape(3, 3, 16),
        b_enc,
        w_mid.transpose(2, 3, 1, 0),
        b_mid,
        w_dec.transpose(2, 3, 0, 1),
        b_dec,
        w_out.reshape(1, 16),
        b_out,
    ] + tables
    scalars = (3, 5, 7, 9, 11)
    landing_places = [
        (pltpu.SMEM if n in scalars else pltpu.VMEM)(x.shape, x.dtype)
        for n, x in enumerate(operands)
    ]
    return pl.pallas_call(
        kernel,
        out_shape=(
            jax.ShapeDtypeStruct((ROWS, TL), BF),
            jax.ShapeDtypeStruct((4, 8, 1, 32), F32),
        ),
        in_specs=[hbm] * len(operands),
        out_specs=(hbm, vm),
        scratch_shapes=landing_places + [
            pltpu.VMEM((ROWS, TL), BF),
            pltpu.VMEM((2, 16, TL), BF),
            pltpu.VMEM((2, 640, 128), F32),
            pltpu.VMEM((512, 128), BF),
            pltpu.VMEM((256, 512), BF),
            pltpu.VMEM((256, 640), BF),
            pltpu.VMEM((256, 640), BF),
            pltpu.VMEM((72 * 64, HALF), BF),
            pltpu.VMEM((36 * 48, HALF), BF),
            pltpu.VMEM((34 * 96, HALF), BF),
            pltpu.VMEM((ROWS, TL), F32),
            pltpu.VMEM((ROWS, TL), F32),
            pltpu.VMEM((ROWS, HALF), F32),
            pltpu.VMEM((32, HALF), F32),
            pltpu.VMEM((16, HALF), F32),
            pltpu.VMEM((NZ, 128, TL), BF),
            pltpu.VMEM((NZ, 128, 2 * TL), F32),
            pltpu.VMEM((2, 32, TL), BF),
            pltpu.VMEM((3, 32, TL), BF),
            pltpu.VMEM((256, TL), BF),
            pltpu.VMEM((2, 128, 2 * TL), F32),
            pltpu.VMEM((128, 2 * TL), F32),
            pltpu.VMEM((4, 128, 128), F32),
            pltpu.VMEM((2 * NC, 8, 128), F32),
            pltpu.VMEM((2 * NC - 1, 8, 128), F32),
            pltpu.VMEM((NZ, 1, 128), F32),
            pltpu.VMEM((NZ, 1, 128), F32),
            dma((len(operands),)),
            dma((2,)),
            dma((2,)),
            dma((2,)),
            dma((2, 8)),
            dma((2, 8)),
            dma((3,)),
            dma((2,)),
            dma((1,)),
            dma((1,)),
            dma((NZ,)),
            dma((NZ,)),
        ],
        compiler_params=pltpu.CompilerParams(
            collective_id=0, has_side_effects=True, vmem_limit_bytes=56 * 1024 * 1024
        ),
    )(*operands)


def solution(mesh):
    return jax.shard_map(
        body,
        mesh=mesh,
        in_specs=(
            P("chan", ("tmpl", "tm")),
            P("chan"),
            P("tmpl", "chan", None),
            P("tmpl"),
            P(),
            P(),
            P(),
            P(),
            P(),
            P(),
            P(),
            P(),
        ),
        out_specs=(P("chan", ("tmpl", "tm")), P("tmpl", None, "tm", "chan")),
        check_vma=False,
    )
```

```python
import functools
import math

import jax
import jax.numpy as jnp
import numpy as np
from jax import lax
from jax.experimental import pallas as pl
from jax.experimental.pallas import tpu as pltpu
from jax.sharding import PartitionSpec as P

BF = jnp.bfloat16
F32 = jnp.float32
MESH = pl.DeviceIdType.MESH
ROWS = 64
TL = 512
HALF = 256
NZ = 8
NC = 16
BIG = -1e30


def middle_table():
    q = np.zeros((3, 3, 16, 512), np.float32)
    for g in range(16):
        for rr in range(3):
            for v in range(3):
                q[rr, v, g, rr * 48 + v * 16 + g] = 1
    return q.reshape(144, 512)


def encoder_table():
    q = np.zeros((4, 3, 3, 128), np.float32)
    for v in range(4):
        for rr in range(3):
            for dt in range(3):
                q[v, rr, dt, rr * 8 + v + dt] = 1
    return q.reshape(4, 9, 128)


def decoder_table():
    q = np.zeros((4, 3, 3, 48, 640), np.float32)
    skip_at = [96, 160, 320, 384]
    up_at = [0, 224, 448]
    for ps in range(2):
        for pr in range(2):
            n = ps * 2 + pr
            for rr in range(4):
                for v in range(4):
                    if 0 <= rr - pr <= 2 and 0 <= v - ps <= 2:
                        for g in range(16):
                            q[n, rr - pr, v - ps, 32 + g, skip_at[rr] + v * 16 + g] = 1
            for dr in range(3):
                for dt in range(3):
                    rr = (pr + dr - 1) // 2 + 1
                    v = (ps + dt - 1) // 2 + 1
                    for m in range(32):
                        q[n, dr, dt, m, up_at[rr] + v * 32 + m] = 1
    return q.reshape(4, 432, 640)


def spectrum_table():
    s = np.arange(TL)[:, None]
    f = np.arange(TL)[None, :]
    phase = ((s * f) % (2 * TL)) * (math.pi / TL)
    re = np.cos(phase)
    im = -np.sin(phase)
    im[:, 0] = np.where(np.arange(TL) % 2 == 0, 1.0, -1.0)
    return np.concatenate([re, im], axis=1).astype(np.float32)


def lag_table():
    f = np.arange(TL)[:, None]
    j = np.arange(TL)[None, :]
    phase = ((f * j) % (2 * TL)) * (math.pi / TL)
    re = np.cos(phase) * 2
    im = -np.sin(phase) * 2
    re[0] = 1
    im[0] = np.where(np.arange(TL) % 2 == 0, 1.0, -1.0)
    return (np.concatenate([re, im], axis=0) / (2 * TL)).astype(np.float32)


def iota(shape, dim):
    return lax.broadcasted_iota(jnp.int32, shape, dim)


def mm(a, b):
    return jnp.dot(a, b, preferred_element_type=F32)


def column(ref, count, lanes):
    rows = iota((count, lanes), 0)
    out = jnp.zeros((count, lanes), F32)
    for g in range(count):
        out = jnp.where(rows == g, ref[g], out)
    return out


def kernel(
    raw_hbm, mask_hbm, tmpl_hbm, assign_hbm, wenc_hbm, benc_hbm, wmid_hbm, bmid_hbm,
    wdec_hbm, bdec_hbm, wout_hbm, bout_hbm, q1_hbm, q2_hbm, q3_hbm, f_hbm, i_hbm,
    den_ref, corr_ref,
    raw_ref, mask_ref, tmpl_ref, assign_ref, wenc_ref, benc_ref, wmid_ref, bmid_ref,
    wdec_ref, bdec_ref, wout_ref, bout_ref, q1_ref, q2_ref, q3_ref, f_ref, i_ref,
    clean_ref, halo_ref, cv_ref, w1_ref, w2_ref, wf_ref, w3_ref,
    u_ref, pv_ref, dp_ref, own_ref, alive_ref, b2_ref, tg_ref, ts_ref, sd_ref, xw_ref,
    xr_ref, z_ref, g_ref, lag_ref, rs_ref, rr_ref, as_ref, ar_ref,
    tab_sem, den_sem, halo_send, halo_recv, ring_send, ring_recv, x_send, x_recv,
    rs_send, rs_recv, a_send, a_recv, hello_sem,
):
    z = lax.axis_index("tmpl")
    c = lax.axis_index("chan")
    p = lax.axis_index("tm")
    me = p * NC + c
    zr = lax.rem(z + 1, NZ)
    zl = lax.rem(z + NZ - 1, NZ)

    loads = {}
    sources = [
        ("raw", raw_hbm, raw_ref), ("mask", mask_hbm, mask_ref), ("tmpl", tmpl_hbm, tmpl_ref),
        ("wenc", wenc_hbm, wenc_ref), ("q1", q1_hbm, q1_ref), ("benc", benc_hbm, benc_ref),
        ("wmid", wmid_hbm, wmid_ref), ("q2", q2_hbm, q2_ref), ("bmid", bmid_hbm, bmid_ref),
        ("wdec", wdec_hbm, wdec_ref), ("q3", q3_hbm, q3_ref),
        ("bdec", bdec_hbm, bdec_ref), ("wout", wout_hbm, wout_ref), ("bout", bout_hbm, bout_ref),
        ("f", f_hbm, f_ref), ("assign", assign_hbm, assign_ref), ("i", i_hbm, i_ref),
    ]

    def fetch(first, last):
        for n in range(first, last):
            name, source, target = sources[n]
            loads[name] = pltpu.make_async_copy(source, target, tab_sem.at[n])
            loads[name].start()

    def ready(*names):
        for name in names:
            loads[name].wait()

    fetch(0, 3)

    barrier = pltpu.get_barrier_semaphore()
    up = lax.rem(c + NC - 1, NC)
    down = lax.rem(c + 1, NC)
    flip = lambda n: c + n - 2 * n * lax.rem(c // n, 2)
    partners = [(z, flip(n), p) for n in (1, 2, 4, 8)] + [(z, c, 1 - p)]
    greeted = partners[1:] + [
        (z, up, p), (z, down, p), (zr, c, p), (zl, c, p), (zr, c, 1 - p), (zl, c, 1 - p)
    ]
    for device in greeted:
        pl.semaphore_signal(barrier, inc=1, device_id=device, device_id_type=MESH)
    fetch(3, len(sources))

    def greet(n):
        pl.semaphore_signal(hello_sem.at[n], inc=1, device_id=partners[n], device_id_type=MESH)

    def greeting(n):
        pl.semaphore_wait(hello_sem.at[n], 1)
        if n < 4:
            greet(n + 1)

    ready("raw", "mask")
    mask = mask_ref[...].astype(F32)
    diag = jnp.where(iota((ROWS, ROWS), 0) == iota((ROWS, ROWS), 1), mask, 0.0).astype(BF)
    clean = mm(diag, raw_ref[...]).astype(BF)
    clean_ref[...] = clean

    ready("tmpl")
    rows = iota((128, 256), 0)
    pick = (rows % 4) * 64 + p * 32 + rows // 4 == iota((128, 256), 1)
    tg_ref[0] = mm(jnp.where(pick, 1.0, 0.0).astype(BF), tmpl_ref[...].reshape(256, TL)).astype(BF)

    pl.semaphore_wait(barrier, len(greeted))
    greet(0)

    halos = [
        pltpu.make_async_remote_copy(
            src_ref=clean_ref.at[pl.ds(0, 16)], dst_ref=halo_ref.at[1],
            send_sem=halo_send.at[0], recv_sem=halo_recv.at[0],
            device_id=(z, up, p), device_id_type=MESH),
        pltpu.make_async_remote_copy(
            src_ref=clean_ref.at[pl.ds(48, 16)], dst_ref=halo_ref.at[0],
            send_sem=halo_send.at[1], recv_sem=halo_recv.at[1],
            device_id=(z, down, p), device_id_type=MESH),
    ]
    for h in halos:
        h.start()

    def right(s, n):
        part = pl.ds(n * 32, 32)
        return pltpu.make_async_remote_copy(
            src_ref=tg_ref.at[max(2 * s - 1, 0), part], dst_ref=tg_ref.at[2 * s + 1, part],
            send_sem=ring_send.at[0, 4 * s + n], recv_sem=ring_recv.at[0, 4 * s + n],
            device_id=(zr, c, p), device_id_type=MESH)

    def left(s, n):
        part = pl.ds(96 - n * 32, 32)
        return pltpu.make_async_remote_copy(
            src_ref=tg_ref.at[2 * s, part], dst_ref=tg_ref.at[min(2 * s + 2, 7), part],
            send_sem=ring_send.at[1, 4 * s + n], recv_sem=ring_recv.at[1, 4 * s + n],
            device_id=(zl, c, p), device_id_type=MESH)

    def forward(s, n):
        right(s - 1, n).wait_recv()
        right(s, n).start()
        left(s - 1, n).wait_recv()
        left(s, n).start()

    def arrived(s, first, last):
        for n in range(first, last):
            right(s, n).wait_recv()
            left(s, n).wait_recv()

    for n in range(4):
        right(0, n).start()
        left(0, n).start()

    scol = iota((TL, TL), 1)
    split = jnp.where(
        iota((TL, TL), 0) == (scol % HALF) * 2 + scol // HALF, 1.0, 0.0
    ).astype(BF)
    later = lambda x, lanes: jnp.where(lanes == 0, jnp.zeros_like(x), pltpu.roll(x, 1, 1))
    sooner = lambda x, lanes: jnp.where(lanes == HALF - 1, jnp.zeros_like(x), pltpu.roll(x, HALF - 1, 1))

    def variants(tall):
        parted = mm(tall.astype(BF), split)
        even = parted[:, :HALF]
        odd = parted[:, HALF:]
        lanes = iota(even.shape, 1)
        return [
            later(even, lanes), later(odd, lanes), even, odd, sooner(even, lanes), sooner(odd, lanes)
        ]

    inner = jnp.where(iota((80, 64), 0) == iota((80, 64), 1) + 5, 1.0, 0.0).astype(BF)
    slots = variants(mm(inner, clean))
    slots.append(jnp.ones((80, HALF), F32))
    edge = jnp.where(iota((80, HALF), 0) % 2 == 0, 0, HALF - 1)
    slots.append(jnp.where(iota((80, HALF), 1) == edge, 1.0, 0.0))
    for n in range(8):
        for h in range(2):
            cv_ref[h, pl.ds(n, 80, stride=8), :] = slots[n][:, h * 128 : (h + 1) * 128]

    ready("wenc", "q1", "benc")
    lane128 = iota((64, 128), 1)
    row64 = iota((64, 128), 0)
    bias = column(benc_ref, 16, 128)
    hi = bias.astype(BF).astype(F32)
    mid = (bias - hi).astype(BF).astype(F32)
    low = bias - hi - mid
    four = lambda x: jnp.concatenate([x] * 4, axis=0)
    fixed = jnp.where(lane128 == 6, four(hi), 0.0)
    fixed = jnp.where(lane128 == 14, four(mid), fixed)
    fixed = jnp.where(lane128 == 22, four(low), fixed)
    fixed = jnp.where((lane128 == 7) & (row64 < 16), BIG, fixed)
    fixed = jnp.where((lane128 == 15) & (row64 >= 48), BIG, fixed)
    wenc = jnp.concatenate([wenc_ref[r] for r in range(3)], axis=0)
    over = lambda w, q: lax.dot_general(w, q, (((0,), (0,)), ((), ())), preferred_element_type=F32)
    base1 = jnp.concatenate([over(wenc, q1_ref[v]) for v in range(4)], axis=0)
    for r in range(8):
        w1_ref[pl.ds(r * 64, 64), :] = (
            (pltpu.roll(base1, 8 * r, 1) if r else base1) + fixed
        ).astype(BF)

    def staggered(start, end, items):
        held = None
        for item in items:
            value = start(item)
            if held is not None:
                end(*held)
            held = (item, value)
        end(*held)

    def encode(q):
        window = jnp.concatenate([cv_ref[h, q * 64 : q * 64 + 128, :] for h in range(2)], axis=1)
        return mm(w1_ref[...], window.astype(BF))

    def encoded(q, e):
        e = jnp.maximum(e, 0.0).astype(BF)
        for k in range(8):
            at = (4 * q + k // 2) * 224 + k % 2 * 160
            u_ref[at : at + 64, :] = e[k * 64 : (k + 1) * 64]

    staggered(encode, encoded, range(1, 8))

    lane16 = iota((16, HALF), 1)

    def pool(i):
        first = pl.multiple_of(i * 224, 16)
        part = lambda o: u_ref[pl.ds(first + o, 16), :].astype(F32)
        pooled = (part(16) + part(32) + part(176) + part(192)) * 0.25
        at = pl.multiple_of(i * 48, 16)
        pv_ref[pl.ds(at, 16), :] = later(pooled, lane16).astype(BF)
        pv_ref[pl.ds(at + 16, 16), :] = pooled.astype(BF)
        pv_ref[pl.ds(at + 32, 16), :] = sooner(pooled, lane16).astype(BF)

    pl.loop(4, 32, unroll=7)(pool)
    greeting(0)

    ready("wmid", "q2", "bmid")
    base2 = over(wmid_ref[...].reshape(144, 32), q2_ref[...])
    for r in range(8):
        w2_ref[pl.ds(r * 32, 32), :] = (
            pltpu.roll(base2, 48 * r, 1) if r else base2
        ).astype(BF)
    b2_ref[...] = column(bmid_ref, 32, HALF)

    lane32 = iota((32, HALF), 1)

    def convolve(q):
        if q == 4:
            return mm(w2_ref[0:64, :192], pv_ref[1536:1728, :])
        return mm(w2_ref[:, :480], pv_ref[q * 384 : q * 384 + 480, :])

    def middle(q, acc):
        for r in range(2 if q == 4 else 8):
            m = jnp.maximum(acc[r * 32 : (r + 1) * 32] + b2_ref[...], 0.0).astype(BF)
            at = (q * 8 + r + 1) * 224 + 64
            u_ref[at : at + 32, :] = later(m, lane32)
            u_ref[at + 32 : at + 64, :] = m
            u_ref[at + 64 : at + 96, :] = sooner(m, lane32)

    staggered(convolve, middle, (1, 2))

    ready("wdec", "q3", "bdec", "wout", "bout")
    wdec = jnp.concatenate([wdec_ref[dr, dt] for dr in range(3) for dt in range(3)], axis=1)
    for n in range(4):
        wide = jnp.concatenate([mm(wdec, q3_ref[n]), jnp.zeros((16, 640), F32)], axis=1)
        for r in range(4):
            turned = pltpu.roll(wide, 224 * r, 1) if r else wide
            for t in range(10):
                wf_ref[t, pl.ds(n // 2 * 8 + 2 * r + n % 2, 16, stride=16), :] = (
                    turned[:, t * 128 : (t + 1) * 128]
                )
    w3_ref[...] = jnp.concatenate([wf_ref[t] for t in range(10)], axis=1).astype(BF)
    wrow = mm(wout_ref[...], jnp.eye(16, dtype=F32).astype(BF))
    wout = [wrow[:, g : g + 1] for g in range(16)]
    own_ref[...] = mm(clean, split)
    alive_ref[...] = mm(diag, jnp.ones((ROWS, HALF), BF))

    forward(1, 0)

    def gather(q):
        first = q * 896 + 288
        if not isinstance(q, int):
            first = pl.multiple_of(first, 32)
        return mm(w3_ref[:, :1216], u_ref[pl.ds(first, 1216), :])

    def decode(q, acc):
        branch = None
        for g in range(16):
            tile = jnp.maximum(acc[g * 16 : (g + 1) * 16] + bdec_ref[g], 0.0)
            term = tile.astype(BF).astype(F32) * wout[g]
            branch = term if branch is None else branch + term
        here = pl.ds(q * 8 if isinstance(q, int) else pl.multiple_of(q * 8, 8), 8)
        alive = alive_ref[here, :]
        for ps in range(2):
            lanes = slice(ps * HALF, (ps + 1) * HALF)
            dp_ref[here, lanes] = alive * (
                own_ref[here, lanes] + branch[ps * 8 : ps * 8 + 8] + bout_ref[0]
            )

    def results(h):
        here = pl.ds(pl.multiple_of(h * 32, 32), 32)
        return pltpu.make_async_copy(sd_ref.at[h], den_ref.at[here], den_sem.at[h])

    def finish(h):
        here = pl.ds(pl.multiple_of(h * 32, 32), 32)
        natural = lax.dot_general(
            dp_ref[here, :].astype(BF), split, (((1,), (1,)), ((), ())), preferred_element_type=F32
        ).astype(BF)
        sd_ref[h] = natural
        results(h).start()

    to_partner = pltpu.make_async_remote_copy(
        src_ref=sd_ref.at[1 - p], dst_ref=xw_ref.at[p],
        send_sem=x_send.at[0], recv_sem=x_recv.at[0],
        device_id=(z, c, 1 - p), device_id_type=MESH)

    def to_previous(h):
        return pltpu.make_async_remote_copy(
            src_ref=sd_ref.at[h], dst_ref=xw_ref.at[2],
            send_sem=x_send.at[1 + h], recv_sem=x_recv.at[1],
            device_id=(zl, c, h), device_id_type=MESH)

    staggered(gather, decode, (2, 3, 4))
    forward(1, 1)
    forward(1, 2)
    greeting(1)

    for h in halos:
        h.wait_recv()
    far = iota((24, 16), 0)
    far = jnp.where(far < 8, far, far + 56)
    away = iota((24, 16), 1)
    above = jnp.where((far + 11 == away) & (c > 0), 1.0, 0.0).astype(BF)
    below = jnp.where((far == away + 69) & (away < 5) & (c < NC - 1), 1.0, 0.0).astype(BF)
    near = iota((24, 64), 0)
    near = jnp.where(near < 8, near, near + 56)
    kept = jnp.where(near == iota((24, 64), 1) + 5, 1.0, 0.0).astype(BF)
    edges = variants(mm(kept, clean) + mm(above, halo_ref[0]) + mm(below, halo_ref[1]))
    for n in range(6):
        for h in range(2):
            cut = edges[n][:, h * 128 : (h + 1) * 128]
            cv_ref[h, pl.ds(n, 8, stride=8), :] = cut[:8]
            cv_ref[h, pl.ds(512 + n, 16, stride=8), :] = cut[8:]
    staggered(encode, encoded, (0, 8))

    @pl.when(c == 0)
    def _():
        u_ref[0:448, :] = jnp.zeros((448, HALF), BF)

    @pl.when(c == NC - 1)
    def _():
        u_ref[34 * 224 : 36 * 224, :] = jnp.zeros((448, HALF), BF)

    for i in (0, 1, 2, 3, 32, 33, 34, 35):
        pool(i)

    staggered(convolve, middle, (0, 3, 4))

    @pl.when(c == 0)
    def _():
        u_ref[288:384, :] = jnp.zeros((96, HALF), BF)

    @pl.when(c == NC - 1)
    def _():
        u_ref[34 * 224 + 64 : 34 * 224 + 160, :] = jnp.zeros((96, HALF), BF)

    forward(1, 3)
    greeting(2)
    theirs = 6 * (1 - p)
    staggered(gather, decode, (5, theirs, theirs + 1))
    finish(1 - p)
    to_partner.start()

    @pl.when(p == 0)
    def _():
        to_previous(1).start()

    forward(2, 0)
    greeting(3)
    staggered(gather, decode, (6 * p, 6 * p + 1))
    finish(p)

    @pl.when(p == 0)
    def _():
        to_previous(0).start()

    xw_ref[p] = sd_ref[p]
    forward(2, 1)

    ready("f")

    def transform(first, count):
        wide = mm(tg_ref[first : first + count].reshape(count * 128, TL), f_ref[...])
        ts_ref[first : first + count] = wide.reshape(count, 128, 2 * TL)

    transform(0, 3)
    forward(2, 2)
    greeting(4)

    rrow = iota((128, 32), 0)
    repeat = jnp.where(rrow // 4 == iota((128, 32), 1), 1.0, 0.0).astype(BF)
    lane1k = iota((128, 2 * TL), 1)
    sign = jnp.where((lane1k % 2 == 1), -1.0, 1.0)
    to_partner.wait_recv()
    for n in range(2):
        xr_ref[pl.ds(n * 128, 128), :] = mm(repeat, xw_ref[n]).astype(BF)
    spectra = mm(xr_ref[...], f_ref[...])
    z_ref[0] = spectra[0:128] + sign * spectra[128:256]
    z_ref[1] = spectra[128:256]

    forward(2, 3)
    transform(3, 2)

    lane512 = iota((8, TL), 1)

    def product(n, k):
        a = jnp.zeros((8, TL), F32)
        b = jnp.zeros((8, TL), F32)
        d = jnp.zeros((8, TL), F32)
        for s in range(16):
            here = pl.ds(s * 8, 8)
            tr = ts_ref[k, here, 0:TL]
            ti = ts_ref[k, here, TL : 2 * TL]
            sr = z_ref[n, here, 0:TL]
            si = z_ref[n, here, TL : 2 * TL]
            a = a + sr * tr
            b = b + si * ti
            d = d + (si * tr - sr * ti)
        a = a + pltpu.roll(a, 4, 0)
        b = b + pltpu.roll(b, 4, 0)
        d = d + pltpu.roll(d, 4, 0)
        at = pl.ds(pl.multiple_of(n * 64 + k * 8, 8), 8)
        g_ref[at, 0:TL] = jnp.where(lane512 == 0, a, a + b)
        g_ref[at, TL : 2 * TL] = jnp.where(lane512 == 0, b, d)

    pl.loop(0, 5, unroll=True)(functools.partial(product, 0))
    forward(3, 0)

    to_previous(0).wait_recv()
    following = xw_ref[2] * jnp.where(z == NZ - 1, 0.0, 1.0).astype(BF)
    z_ref[1] = z_ref[1] + sign * mm(mm(repeat, following).astype(BF), f_ref[...])
    pl.loop(0, 5, unroll=True)(functools.partial(product, 1))
    forward(3, 1)
    arrived(2, 2, 4)
    transform(5, 2)
    pl.loop(5, 7, unroll=True)(functools.partial(product, 0))
    pl.loop(5, 7, unroll=True)(functools.partial(product, 1))
    arrived(3, 0, 2)
    transform(7, 1)
    pl.loop(0, 2, unroll=True)(lambda n: product(n, 7))

    ready("i")
    lags = mm(g_ref[...].astype(BF), i_ref[...])
    for t in range(4):
        lag_ref[t] = lags[:, t * 128 : (t + 1) * 128]

    lane8 = iota((8, 128), 1) // 32
    for n in range(2):
        for t in range(4):
            quarter = [lag_ref[t, pl.ds(n * 64 + k, 8, stride=8), :] for k in range(4)]
            for o in range(4):
                piece = jnp.zeros((8, 128), F32)
                for k in range(4):
                    shift = (k - o) % 4 * 32
                    moved = pltpu.roll(quarter[k], shift, 1) if shift else quarter[k]
                    piece = jnp.where(lane8 == k, moved, piece)
                rs_ref[n * NC + t * 4 + o] = piece

    @pl.loop(1, 2 * NC)
    def _(d):
        other = lax.rem(me + d, 2 * NC)
        pltpu.make_async_remote_copy(
            src_ref=rs_ref.at[other], dst_ref=rr_ref.at[d - 1],
            send_sem=rs_send.at[0], recv_sem=rs_recv.at[0],
            device_id=(z, lax.rem(other, NC), other // NC), device_id_type=MESH).start()

    shares = pltpu.make_async_remote_copy(
        src_ref=rr_ref, dst_ref=rr_ref, send_sem=rs_send.at[0], recv_sem=rs_recv.at[0],
        device_id=(z, c, 1 - p), device_id_type=MESH)
    shares.wait_recv()
    parts = [rs_ref[me]] + [rr_ref[d] for d in range(2 * NC - 1)]
    while len(parts) > 1:
        parts = [parts[n] + parts[n + 1] for n in range(0, len(parts), 2)]
    as_ref[...] = parts[0].reshape(8, 1, 128)

    places = [0, 1, -1, 2, -2, 3, -3, 4]
    for d in range(1, NZ):
        pltpu.make_async_remote_copy(
            src_ref=as_ref.at[d], dst_ref=ar_ref.at[z],
            send_sem=a_send.at[d], recv_sem=a_recv.at[z],
            device_id=(lax.rem(z + NZ - places[d], NZ), c, p), device_id_type=MESH).start()

    ar_ref[z] = as_ref[0]

    def landing(d):
        other = lax.rem(z + NZ + places[d], NZ)
        return pltpu.make_async_remote_copy(
            src_ref=as_ref.at[d], dst_ref=ar_ref.at[other],
            send_sem=a_send.at[d], recv_sem=a_recv.at[other],
            device_id=(other, c, p), device_id_type=MESH)

    for d in range(1, NZ):
        landing(d).wait_recv()

    found = ar_ref[...].reshape(8, 128)
    turned = [found] + [pltpu.roll(found, 128 - 32 * k, 1) for k in range(1, 4)]
    ready("assign")
    for r in range(4):
        local = lax.rem(assign_ref[r], 4)
        row = jnp.zeros((8, 128), F32)
        for k in range(4):
            row = row + jnp.where(local == k, 1.0, 0.0) * turned[k]
        corr_ref[r] = row[:, :32].reshape(8, 1, 32)

    results(0).wait()
    results(1).wait()
    for h in halos:
        h.wait_send()
    for s in range(4):
        for n in range(4 if s < 3 else 2):
            right(s, n).wait_send()
            left(s, n).wait_send()
    to_partner.wait_send()

    @pl.when(p == 0)
    def _():
        to_previous(0).wait_send()
        to_previous(1).wait_send()

    shares.wait_send()
    for d in range(1, NZ):
        landing(d).wait_send()


def body(raw, dead_mask, templates, assign, w_enc, b_enc, w_mid, b_mid, w_dec, b_dec, w_out, b_out):
    vm = pl.BlockSpec(memory_space=pltpu.VMEM)
    hbm = pl.BlockSpec(memory_space=pltpu.HBM)
    dma = pltpu.SemaphoreType.DMA
    tables = [
        jnp.asarray(t, BF)
        for t in (encoder_table(), middle_table(), decoder_table(), spectrum_table(), lag_table())
    ]
    operands = [
        raw,
        dead_mask.reshape(1, ROWS),
        templates,
        assign,
        w_enc.transpose(1, 2, 3, 0).reshape(3, 3, 16),
        b_enc,
        w_mid.transpose(2, 3, 1, 0),
        b_mid,
        w_dec.transpose(2, 3, 0, 1),
        b_dec,
        w_out.reshape(1, 16),
        b_out,
    ] + tables
    scalars = (3, 5, 7, 9, 11)
    landing_places = [
        (pltpu.SMEM if n in scalars else pltpu.VMEM)(x.shape, x.dtype)
        for n, x in enumerate(operands)
    ]
    return pl.pallas_call(
        kernel,
        out_shape=(
            jax.ShapeDtypeStruct((ROWS, TL), BF),
            jax.ShapeDtypeStruct((4, 8, 1, 32), F32),
        ),
        in_specs=[hbm] * len(operands),
        out_specs=(hbm, vm),
        scratch_shapes=landing_places + [
            pltpu.VMEM((ROWS, TL), BF),
            pltpu.VMEM((2, 16, TL), BF),
            pltpu.VMEM((2, 640, 128), F32),
            pltpu.VMEM((512, 128), BF),
            pltpu.VMEM((256, 512), BF),
            pltpu.VMEM((10, 256, 128), F32),
            pltpu.VMEM((256, 1280), BF),
            pltpu.VMEM((36 * 224, HALF), BF),
            pltpu.VMEM((36 * 48, HALF), BF),
            pltpu.VMEM((ROWS, TL), F32),
            pltpu.VMEM((ROWS, TL), F32),
            pltpu.VMEM((ROWS, HALF), F32),
            pltpu.VMEM((32, HALF), F32),
            pltpu.VMEM((NZ, 128, TL), BF),
            pltpu.VMEM((NZ, 128, 2 * TL), F32),
            pltpu.VMEM((2, 32, TL), BF),
            pltpu.VMEM((3, 32, TL), BF),
            pltpu.VMEM((256, TL), BF),
            pltpu.VMEM((2, 128, 2 * TL), F32),
            pltpu.VMEM((128, 2 * TL), F32),
            pltpu.VMEM((4, 128, 128), F32),
            pltpu.VMEM((2 * NC, 8, 128), F32),
            pltpu.VMEM((2 * NC - 1, 8, 128), F32),
            pltpu.VMEM((NZ, 1, 128), F32),
            pltpu.VMEM((NZ, 1, 128), F32),
            dma((len(operands),)),
            dma((2,)),
            dma((2,)),
            dma((2,)),
            dma((2, 14)),
            dma((2, 14)),
            dma((3,)),
            dma((2,)),
            dma((1,)),
            dma((1,)),
            dma((NZ,)),
            dma((NZ,)),
            pltpu.SemaphoreType.REGULAR((5,)),
        ],
        compiler_params=pltpu.CompilerParams(
            collective_id=0, has_side_effects=True, vmem_limit_bytes=56 * 1024 * 1024
        ),
    )(*operands)


def solution(mesh):
    return jax.shard_map(
        body,
        mesh=mesh,
        in_specs=(
            P("chan", ("tmpl", "tm")),
            P("chan"),
            P("tmpl", "chan", None),
            P("tmpl"),
            P(),
            P(),
            P(),
            P(),
            P(),
            P(),
            P(),
            P(),
        ),
        out_specs=(P("chan", ("tmpl", "tm")), P("tmpl", None, "tm", "chan")),
        check_vma=False,
    )
```

```python
import functools
import math

import jax
import jax.numpy as jnp
import numpy as np
from jax import lax
from jax.experimental import pallas as pl
from jax.experimental.pallas import tpu as pltpu
from jax.sharding import PartitionSpec as P

BF = jnp.bfloat16
F32 = jnp.float32
MESH = pl.DeviceIdType.MESH
ROWS = 64
TL = 512
HALF = 256
NZ = 8
NC = 16
BIG = -1e30


def middle_table():
    q = np.zeros((3, 3, 16, 512), np.float32)
    for g in range(16):
        for rr in range(3):
            for v in range(3):
                q[rr, v, g, rr * 48 + v * 16 + g] = 1
    return q.reshape(144, 512)


def encoder_table():
    q = np.zeros((4, 3, 3, 128), np.float32)
    for v in range(4):
        for rr in range(3):
            for dt in range(3):
                q[v, rr, dt, rr * 8 + v + dt] = 1
    return q.reshape(4, 9, 128)


def decoder_table():
    q = np.zeros((4, 3, 3, 48, 640), np.float32)
    skip_at = [96, 160, 320, 384]
    up_at = [0, 224, 448]
    for ps in range(2):
        for pr in range(2):
            n = ps * 2 + pr
            for rr in range(4):
                for v in range(4):
                    if 0 <= rr - pr <= 2 and 0 <= v - ps <= 2:
                        for g in range(16):
                            q[n, rr - pr, v - ps, 32 + g, skip_at[rr] + v * 16 + g] = 1
            for dr in range(3):
                for dt in range(3):
                    rr = (pr + dr - 1) // 2 + 1
                    v = (ps + dt - 1) // 2 + 1
                    for m in range(32):
                        q[n, dr, dt, m, up_at[rr] + v * 32 + m] = 1
    return q.reshape(4, 432, 640)


def spectrum_table():
    s = np.arange(TL)[:, None]
    f = np.arange(TL)[None, :]
    phase = ((s * f) % (2 * TL)) * (math.pi / TL)
    re = np.cos(phase)
    im = -np.sin(phase)
    im[:, 0] = np.where(np.arange(TL) % 2 == 0, 1.0, -1.0)
    return np.concatenate([re, im], axis=1).astype(np.float32)


def lag_table():
    f = np.arange(TL)[:, None]
    j = np.arange(TL)[None, :]
    phase = ((f * j) % (2 * TL)) * (math.pi / TL)
    re = np.cos(phase) * 2
    im = -np.sin(phase) * 2
    re[0] = 1
    im[0] = np.where(np.arange(TL) % 2 == 0, 1.0, -1.0)
    return (np.concatenate([re, im], axis=0) / (2 * TL)).astype(np.float32)


def iota(shape, dim):
    return lax.broadcasted_iota(jnp.int32, shape, dim)


def mm(a, b):
    return jnp.dot(a, b, preferred_element_type=F32)


def column(ref, count, lanes):
    rows = iota((count, lanes), 0)
    out = jnp.zeros((count, lanes), F32)
    for g in range(count):
        out = jnp.where(rows == g, ref[g], out)
    return out


def kernel(
    raw_hbm, mask_hbm, tmpl_hbm, assign_hbm, wenc_hbm, benc_hbm, wmid_hbm, bmid_hbm,
    wdec_hbm, bdec_hbm, wout_hbm, bout_hbm, q1_hbm, q2_hbm, q3_hbm, f_hbm, i_hbm,
    den_ref, corr_ref,
    raw_ref, mask_ref, tmpl_ref, assign_ref, wenc_ref, benc_ref, wmid_ref, bmid_ref,
    wdec_ref, bdec_ref, wout_ref, bout_ref, q1_ref, q2_ref, q3_ref, f_ref, i_ref,
    clean_ref, halo_ref, cv_ref, w1_ref, w2_ref, wf_ref, w3_ref,
    u_ref, pv_ref, dp_ref, own_ref, alive_ref, b2_ref, tg_ref, ts_ref, sd_ref, xw_ref,
    xr_ref, z_ref, g_ref, lag_ref, rs_ref, rr_ref, as_ref, ar_ref,
    tab_sem, den_sem, halo_send, halo_recv, ring_send, ring_recv, x_send, x_recv,
    rs_send, rs_recv, a_send, a_recv, hello_sem,
):
    z = lax.axis_index("tmpl")
    c = lax.axis_index("chan")
    p = lax.axis_index("tm")
    me = p * NC + c
    zr = lax.rem(z + 1, NZ)
    zl = lax.rem(z + NZ - 1, NZ)

    loads = {}
    sources = [
        ("raw", raw_hbm, raw_ref), ("mask", mask_hbm, mask_ref), ("tmpl", tmpl_hbm, tmpl_ref),
        ("wenc", wenc_hbm, wenc_ref), ("q1", q1_hbm, q1_ref), ("benc", benc_hbm, benc_ref),
        ("wmid", wmid_hbm, wmid_ref), ("q2", q2_hbm, q2_ref), ("bmid", bmid_hbm, bmid_ref),
        ("wdec", wdec_hbm, wdec_ref), ("q3", q3_hbm, q3_ref),
        ("bdec", bdec_hbm, bdec_ref), ("wout", wout_hbm, wout_ref), ("bout", bout_hbm, bout_ref),
        ("f", f_hbm, f_ref), ("assign", assign_hbm, assign_ref), ("i", i_hbm, i_ref),
    ]

    def fetch(first, last):
        for n in range(first, last):
            name, source, target = sources[n]
            loads[name] = pltpu.make_async_copy(source, target, tab_sem.at[n])
            loads[name].start()

    def ready(*names):
        for name in names:
            loads[name].wait()

    fetch(0, 3)

    barrier = pltpu.get_barrier_semaphore()
    up = lax.rem(c + NC - 1, NC)
    down = lax.rem(c + 1, NC)
    flip = lambda n: c + n - 2 * n * lax.rem(c // n, 2)
    partners = [(z, flip(n), p) for n in (1, 2, 4, 8)] + [(z, c, 1 - p)]
    greeted = partners[1:] + [
        (z, up, p), (z, down, p), (zr, c, p), (zl, c, p), (zr, c, 1 - p), (zl, c, 1 - p)
    ]
    for device in greeted:
        pl.semaphore_signal(barrier, inc=1, device_id=device, device_id_type=MESH)
    fetch(3, len(sources))

    def greet(n):
        pl.semaphore_signal(hello_sem.at[n], inc=1, device_id=partners[n], device_id_type=MESH)

    def greeting(n):
        pl.semaphore_wait(hello_sem.at[n], 1)
        if n < 4:
            greet(n + 1)

    ready("raw", "mask")
    mask = mask_ref[...].astype(F32)
    diag = jnp.where(iota((ROWS, ROWS), 0) == iota((ROWS, ROWS), 1), mask, 0.0).astype(BF)
    clean = mm(diag, raw_ref[...]).astype(BF)
    clean_ref[...] = clean

    ready("tmpl")
    rows = iota((128, 256), 0)
    pick = (rows % 4) * 64 + p * 32 + rows // 4 == iota((128, 256), 1)
    tg_ref[0] = mm(jnp.where(pick, 1.0, 0.0).astype(BF), tmpl_ref[...].reshape(256, TL)).astype(BF)

    pl.semaphore_wait(barrier, len(greeted))
    greet(0)

    halos = [
        pltpu.make_async_remote_copy(
            src_ref=clean_ref.at[pl.ds(0, 16)], dst_ref=halo_ref.at[1],
            send_sem=halo_send.at[0], recv_sem=halo_recv.at[0],
            device_id=(z, up, p), device_id_type=MESH),
        pltpu.make_async_remote_copy(
            src_ref=clean_ref.at[pl.ds(48, 16)], dst_ref=halo_ref.at[0],
            send_sem=halo_send.at[1], recv_sem=halo_recv.at[1],
            device_id=(z, down, p), device_id_type=MESH),
    ]
    for h in halos:
        h.start()

    def right(s, n):
        part = pl.ds(n * 32, 32)
        source, target, hops = (3, 7, 2) if s == 3 else (max(2 * s - 1, 0), 2 * s + 1, 1)
        return pltpu.make_async_remote_copy(
            src_ref=tg_ref.at[source, part], dst_ref=tg_ref.at[target, part],
            send_sem=ring_send.at[0, 4 * s + n], recv_sem=ring_recv.at[0, 4 * s + n],
            device_id=(lax.rem(z + hops, NZ), c, p), device_id_type=MESH)

    def left(s, n):
        part = pl.ds(96 - n * 32, 32)
        source, target, hops = (4, 7, 2) if s == 3 else (2 * s, 2 * s + 2, 1)
        return pltpu.make_async_remote_copy(
            src_ref=tg_ref.at[source, part], dst_ref=tg_ref.at[target, part],
            send_sem=ring_send.at[1, 4 * s + n], recv_sem=ring_recv.at[1, 4 * s + n],
            device_id=(lax.rem(z + NZ - hops, NZ), c, p), device_id_type=MESH)

    def forward(s, n):
        right(s - 1, n).wait_recv()
        left(s - 1, n).wait_recv()
        if s == 2 and n < 2:
            right(3, n).start()
            left(3, n).start()
        right(s, n).start()
        left(s, n).start()

    def arrived(s, first, last):
        for n in range(first, last):
            right(s, n).wait_recv()
            left(s, n).wait_recv()

    for n in range(4):
        right(0, n).start()
        left(0, n).start()

    scol = iota((TL, TL), 1)
    split = jnp.where(
        iota((TL, TL), 0) == (scol % HALF) * 2 + scol // HALF, 1.0, 0.0
    ).astype(BF)
    later = lambda x, lanes: jnp.where(lanes == 0, jnp.zeros_like(x), pltpu.roll(x, 1, 1))
    sooner = lambda x, lanes: jnp.where(lanes == HALF - 1, jnp.zeros_like(x), pltpu.roll(x, HALF - 1, 1))

    def variants(tall):
        parted = mm(tall.astype(BF), split)
        even = parted[:, :HALF]
        odd = parted[:, HALF:]
        lanes = iota(even.shape, 1)
        return [
            later(even, lanes), later(odd, lanes), even, odd, sooner(even, lanes), sooner(odd, lanes)
        ]

    inner = jnp.where(iota((80, 64), 0) == iota((80, 64), 1) + 5, 1.0, 0.0).astype(BF)
    slots = variants(mm(inner, clean))
    slots.append(jnp.ones((80, HALF), F32))
    edge = jnp.where(iota((80, HALF), 0) % 2 == 0, 0, HALF - 1)
    slots.append(jnp.where(iota((80, HALF), 1) == edge, 1.0, 0.0))
    for n in range(8):
        for h in range(2):
            cv_ref[h, pl.ds(n, 80, stride=8), :] = slots[n][:, h * 128 : (h + 1) * 128]

    ready("wenc", "q1", "benc")
    lane128 = iota((64, 128), 1)
    row64 = iota((64, 128), 0)
    bias = column(benc_ref, 16, 128)
    hi = bias.astype(BF).astype(F32)
    mid = (bias - hi).astype(BF).astype(F32)
    low = bias - hi - mid
    four = lambda x: jnp.concatenate([x] * 4, axis=0)
    fixed = jnp.where(lane128 == 6, four(hi), 0.0)
    fixed = jnp.where(lane128 == 14, four(mid), fixed)
    fixed = jnp.where(lane128 == 22, four(low), fixed)
    fixed = jnp.where((lane128 == 7) & (row64 < 16), BIG, fixed)
    fixed = jnp.where((lane128 == 15) & (row64 >= 48), BIG, fixed)
    wenc = jnp.concatenate([wenc_ref[r] for r in range(3)], axis=0)
    over = lambda w, q: lax.dot_general(w, q, (((0,), (0,)), ((), ())), preferred_element_type=F32)
    base1 = jnp.concatenate([over(wenc, q1_ref[v]) for v in range(4)], axis=0)
    for r in range(8):
        w1_ref[pl.ds(r * 64, 64), :] = (
            (pltpu.roll(base1, 8 * r, 1) if r else base1) + fixed
        ).astype(BF)

    def staggered(start, end, items):
        held = None
        for item in items:
            value = start(item)
            if held is not None:
                end(*held)
            held = (item, value)
        end(*held)

    def encode(q):
        window = jnp.concatenate([cv_ref[h, q * 64 : q * 64 + 128, :] for h in range(2)], axis=1)
        return mm(w1_ref[...], window.astype(BF))

    def encoded(q, e):
        e = jnp.maximum(e, 0.0).astype(BF)
        for k in range(8):
            at = (4 * q + k // 2) * 224 + k % 2 * 160
            u_ref[at : at + 64, :] = e[k * 64 : (k + 1) * 64]

    staggered(encode, encoded, range(1, 8))

    lane16 = iota((16, HALF), 1)

    def pool(i):
        first = pl.multiple_of(i * 224, 16)
        part = lambda o: u_ref[pl.ds(first + o, 16), :].astype(F32)
        pooled = (part(16) + part(32) + part(176) + part(192)) * 0.25
        at = pl.multiple_of(i * 48, 16)
        pv_ref[pl.ds(at, 16), :] = later(pooled, lane16).astype(BF)
        pv_ref[pl.ds(at + 16, 16), :] = pooled.astype(BF)
        pv_ref[pl.ds(at + 32, 16), :] = sooner(pooled, lane16).astype(BF)

    pl.loop(4, 32, unroll=7)(pool)
    greeting(0)

    ready("wmid", "q2", "bmid")
    base2 = over(wmid_ref[...].reshape(144, 32), q2_ref[...])
    for r in range(8):
        w2_ref[pl.ds(r * 32, 32), :] = (
            pltpu.roll(base2, 48 * r, 1) if r else base2
        ).astype(BF)
    b2_ref[...] = column(bmid_ref, 32, HALF)

    lane32 = iota((32, HALF), 1)

    def convolve(q):
        if q == 4:
            return mm(w2_ref[0:64, :192], pv_ref[1536:1728, :])
        return mm(w2_ref[:, :480], pv_ref[q * 384 : q * 384 + 480, :])

    def middle(q, acc):
        for r in range(2 if q == 4 else 8):
            m = jnp.maximum(acc[r * 32 : (r + 1) * 32] + b2_ref[...], 0.0).astype(BF)
            at = (q * 8 + r + 1) * 224 + 64
            u_ref[at : at + 32, :] = later(m, lane32)
            u_ref[at + 32 : at + 64, :] = m
            u_ref[at + 64 : at + 96, :] = sooner(m, lane32)

    staggered(convolve, middle, (1, 2))
    forward(1, 0)
    forward(1, 1)

    ready("wdec", "q3", "bdec", "wout", "bout")
    wdec = jnp.concatenate([wdec_ref[dr, dt] for dr in range(3) for dt in range(3)], axis=1)
    for n in range(4):
        wide = jnp.concatenate([mm(wdec, q3_ref[n]), jnp.zeros((16, 640), F32)], axis=1)
        for r in range(4):
            turned = pltpu.roll(wide, 224 * r, 1) if r else wide
            for t in range(10):
                wf_ref[t, pl.ds(n // 2 * 8 + 2 * r + n % 2, 16, stride=16), :] = (
                    turned[:, t * 128 : (t + 1) * 128]
                )
    w3_ref[...] = jnp.concatenate([wf_ref[t] for t in range(10)], axis=1).astype(BF)
    wrow = mm(wout_ref[...], jnp.eye(16, dtype=F32).astype(BF))
    wout = [wrow[:, g : g + 1] for g in range(16)]
    own_ref[...] = mm(clean, split)
    alive_ref[...] = mm(diag, jnp.ones((ROWS, HALF), BF))

    forward(1, 2)
    forward(1, 3)

    def gather(q):
        first = q * 896 + 288
        if not isinstance(q, int):
            first = pl.multiple_of(first, 32)
        return mm(w3_ref[:, :1216], u_ref[pl.ds(first, 1216), :])

    def decode(q, acc):
        branch = None
        for g in range(16):
            tile = jnp.maximum(acc[g * 16 : (g + 1) * 16] + bdec_ref[g], 0.0)
            term = tile.astype(BF).astype(F32) * wout[g]
            branch = term if branch is None else branch + term
        here = pl.ds(q * 8 if isinstance(q, int) else pl.multiple_of(q * 8, 8), 8)
        alive = alive_ref[here, :]
        for ps in range(2):
            lanes = slice(ps * HALF, (ps + 1) * HALF)
            dp_ref[here, lanes] = alive * (
                own_ref[here, lanes] + branch[ps * 8 : ps * 8 + 8] + bout_ref[0]
            )

    def results(h):
        here = pl.ds(pl.multiple_of(h * 32, 32), 32)
        return pltpu.make_async_copy(sd_ref.at[h], den_ref.at[here], den_sem.at[h])

    def finish(h):
        here = pl.ds(pl.multiple_of(h * 32, 32), 32)
        natural = lax.dot_general(
            dp_ref[here, :].astype(BF), split, (((1,), (1,)), ((), ())), preferred_element_type=F32
        ).astype(BF)
        sd_ref[h] = natural
        results(h).start()

    to_partner = pltpu.make_async_remote_copy(
        src_ref=sd_ref.at[1 - p], dst_ref=xw_ref.at[p],
        send_sem=x_send.at[0], recv_sem=x_recv.at[0],
        device_id=(z, c, 1 - p), device_id_type=MESH)

    def to_previous(h):
        return pltpu.make_async_remote_copy(
            src_ref=sd_ref.at[h], dst_ref=xw_ref.at[2],
            send_sem=x_send.at[1 + h], recv_sem=x_recv.at[1],
            device_id=(zl, c, h), device_id_type=MESH)

    staggered(gather, decode, (2, 3, 4))
    greeting(1)

    for h in halos:
        h.wait_recv()
    far = iota((24, 16), 0)
    far = jnp.where(far < 8, far, far + 56)
    away = iota((24, 16), 1)
    above = jnp.where((far + 11 == away) & (c > 0), 1.0, 0.0).astype(BF)
    below = jnp.where((far == away + 69) & (away < 5) & (c < NC - 1), 1.0, 0.0).astype(BF)
    near = iota((24, 64), 0)
    near = jnp.where(near < 8, near, near + 56)
    kept = jnp.where(near == iota((24, 64), 1) + 5, 1.0, 0.0).astype(BF)
    edges = variants(mm(kept, clean) + mm(above, halo_ref[0]) + mm(below, halo_ref[1]))
    for n in range(6):
        for h in range(2):
            cut = edges[n][:, h * 128 : (h + 1) * 128]
            cv_ref[h, pl.ds(n, 8, stride=8), :] = cut[:8]
            cv_ref[h, pl.ds(512 + n, 16, stride=8), :] = cut[8:]
    staggered(encode, encoded, (0, 8))

    @pl.when(c == 0)
    def _():
        u_ref[0:448, :] = jnp.zeros((448, HALF), BF)

    @pl.when(c == NC - 1)
    def _():
        u_ref[34 * 224 : 36 * 224, :] = jnp.zeros((448, HALF), BF)

    for i in (0, 1, 2, 3, 32, 33, 34, 35):
        pool(i)

    forward(2, 0)
    staggered(convolve, middle, (0, 3, 4))

    @pl.when(c == 0)
    def _():
        u_ref[288:384, :] = jnp.zeros((96, HALF), BF)

    @pl.when(c == NC - 1)
    def _():
        u_ref[34 * 224 + 64 : 34 * 224 + 160, :] = jnp.zeros((96, HALF), BF)

    forward(2, 1)
    greeting(2)
    theirs = 6 * (1 - p)
    staggered(gather, decode, (5, theirs, theirs + 1))
    finish(1 - p)
    to_partner.start()

    @pl.when(p == 0)
    def _():
        to_previous(1).start()

    forward(2, 2)
    forward(2, 3)
    greeting(3)
    staggered(gather, decode, (6 * p, 6 * p + 1))
    finish(p)

    @pl.when(p == 0)
    def _():
        to_previous(0).start()

    xw_ref[p] = sd_ref[p]

    ready("f")

    def transform(first, count):
        wide = mm(tg_ref[first : first + count].reshape(count * 128, TL), f_ref[...])
        ts_ref[first : first + count] = wide.reshape(count, 128, 2 * TL)

    transform(0, 3)
    greeting(4)

    rrow = iota((128, 32), 0)
    repeat = jnp.where(rrow // 4 == iota((128, 32), 1), 1.0, 0.0).astype(BF)
    lane1k = iota((128, 2 * TL), 1)
    sign = jnp.where((lane1k % 2 == 1), -1.0, 1.0)
    to_partner.wait_recv()
    for n in range(2):
        xr_ref[pl.ds(n * 128, 128), :] = mm(repeat, xw_ref[n]).astype(BF)
    spectra = mm(xr_ref[...], f_ref[...])
    z_ref[0] = spectra[0:128] + sign * spectra[128:256]
    z_ref[1] = spectra[128:256]

    transform(3, 2)

    lane512 = iota((8, TL), 1)

    def product(n, k):
        a = jnp.zeros((8, TL), F32)
        b = jnp.zeros((8, TL), F32)
        d = jnp.zeros((8, TL), F32)
        for s in range(16):
            here = pl.ds(s * 8, 8)
            tr = ts_ref[k, here, 0:TL]
            ti = ts_ref[k, here, TL : 2 * TL]
            sr = z_ref[n, here, 0:TL]
            si = z_ref[n, here, TL : 2 * TL]
            a = a + sr * tr
            b = b + si * ti
            d = d + (si * tr - sr * ti)
        a = a + pltpu.roll(a, 4, 0)
        b = b + pltpu.roll(b, 4, 0)
        d = d + pltpu.roll(d, 4, 0)
        at = pl.ds(pl.multiple_of(n * 64 + k * 8, 8), 8)
        g_ref[at, 0:TL] = jnp.where(lane512 == 0, a, a + b)
        g_ref[at, TL : 2 * TL] = jnp.where(lane512 == 0, b, d)

    pl.loop(0, 5, unroll=True)(functools.partial(product, 0))
    to_previous(0).wait_recv()
    following = xw_ref[2] * jnp.where(z == NZ - 1, 0.0, 1.0).astype(BF)
    z_ref[1] = z_ref[1] + sign * mm(mm(repeat, following).astype(BF), f_ref[...])
    pl.loop(0, 5, unroll=True)(functools.partial(product, 1))
    arrived(2, 0, 4)
    transform(5, 2)
    pl.loop(5, 7, unroll=True)(functools.partial(product, 0))
    pl.loop(5, 7, unroll=True)(functools.partial(product, 1))
    arrived(3, 0, 2)
    transform(7, 1)
    pl.loop(0, 2, unroll=True)(lambda n: product(n, 7))

    ready("i")
    lags = mm(g_ref[...].astype(BF), i_ref[...])
    for t in range(4):
        lag_ref[t] = lags[:, t * 128 : (t + 1) * 128]

    lane8 = iota((8, 128), 1) // 32
    for n in range(2):
        for t in range(4):
            quarter = [lag_ref[t, pl.ds(n * 64 + k, 8, stride=8), :] for k in range(4)]
            for o in range(4):
                piece = jnp.zeros((8, 128), F32)
                for k in range(4):
                    shift = (k - o) % 4 * 32
                    moved = pltpu.roll(quarter[k], shift, 1) if shift else quarter[k]
                    piece = jnp.where(lane8 == k, moved, piece)
                rs_ref[n * NC + t * 4 + o] = piece

    hops = [0, 2, 1, 1]
    steps = [0, 1, 2, 1]
    for d in sorted(range(1, 2 * NC), key=lambda d: -hops[d // 8] - steps[d // 2 % 4]):
        other = lax.rem(me + d, 2 * NC)
        pltpu.make_async_remote_copy(
            src_ref=rs_ref.at[other], dst_ref=rr_ref.at[d - 1],
            send_sem=rs_send.at[0], recv_sem=rs_recv.at[0],
            device_id=(z, lax.rem(other, NC), other // NC), device_id_type=MESH).start()

    shares = pltpu.make_async_remote_copy(
        src_ref=rr_ref, dst_ref=rr_ref, send_sem=rs_send.at[0], recv_sem=rs_recv.at[0],
        device_id=(z, c, 1 - p), device_id_type=MESH)
    shares.wait_recv()
    parts = [rs_ref[me]] + [rr_ref[d] for d in range(2 * NC - 1)]
    while len(parts) > 1:
        parts = [parts[n] + parts[n + 1] for n in range(0, len(parts), 2)]
    as_ref[...] = parts[0].reshape(8, 1, 128)

    places = [0, 1, -1, 2, -2, 3, -3, 4]
    for d in range(NZ - 1, 0, -1):
        pltpu.make_async_remote_copy(
            src_ref=as_ref.at[d], dst_ref=ar_ref.at[z],
            send_sem=a_send.at[d], recv_sem=a_recv.at[z],
            device_id=(lax.rem(z + NZ - places[d], NZ), c, p), device_id_type=MESH).start()

    ar_ref[z] = as_ref[0]

    def landing(d):
        other = lax.rem(z + NZ + places[d], NZ)
        return pltpu.make_async_remote_copy(
            src_ref=as_ref.at[d], dst_ref=ar_ref.at[other],
            send_sem=a_send.at[d], recv_sem=a_recv.at[other],
            device_id=(other, c, p), device_id_type=MESH)

    for d in range(1, NZ):
        landing(d).wait_recv()

    found = ar_ref[...].reshape(8, 128)
    turned = [found] + [pltpu.roll(found, 128 - 32 * k, 1) for k in range(1, 4)]
    ready("assign")
    for r in range(4):
        local = lax.rem(assign_ref[r], 4)
        row = jnp.zeros((8, 128), F32)
        for k in range(4):
            row = row + jnp.where(local == k, 1.0, 0.0) * turned[k]
        corr_ref[r] = row[:, :32].reshape(8, 1, 32)

    results(0).wait()
    results(1).wait()
    for h in halos:
        h.wait_send()
    for s in range(4):
        for n in range(4 if s < 3 else 2):
            right(s, n).wait_send()
            left(s, n).wait_send()
    to_partner.wait_send()

    @pl.when(p == 0)
    def _():
        to_previous(0).wait_send()
        to_previous(1).wait_send()

    shares.wait_send()
    for d in range(1, NZ):
        landing(d).wait_send()


def body(raw, dead_mask, templates, assign, w_enc, b_enc, w_mid, b_mid, w_dec, b_dec, w_out, b_out):
    vm = pl.BlockSpec(memory_space=pltpu.VMEM)
    hbm = pl.BlockSpec(memory_space=pltpu.HBM)
    dma = pltpu.SemaphoreType.DMA
    tables = [
        jnp.asarray(t, BF)
        for t in (encoder_table(), middle_table(), decoder_table(), spectrum_table(), lag_table())
    ]
    operands = [
        raw,
        dead_mask.reshape(1, ROWS),
        templates,
        assign,
        w_enc.transpose(1, 2, 3, 0).reshape(3, 3, 16),
        b_enc,
        w_mid.transpose(2, 3, 1, 0),
        b_mid,
        w_dec.transpose(2, 3, 0, 1),
        b_dec,
        w_out.reshape(1, 16),
        b_out,
    ] + tables
    scalars = (3, 5, 7, 9, 11)
    landing_places = [
        (pltpu.SMEM if n in scalars else pltpu.VMEM)(x.shape, x.dtype)
        for n, x in enumerate(operands)
    ]
    return pl.pallas_call(
        kernel,
        out_shape=(
            jax.ShapeDtypeStruct((ROWS, TL), BF),
            jax.ShapeDtypeStruct((4, 8, 1, 32), F32),
        ),
        in_specs=[hbm] * len(operands),
        out_specs=(hbm, vm),
        scratch_shapes=landing_places + [
            pltpu.VMEM((ROWS, TL), BF),
            pltpu.VMEM((2, 16, TL), BF),
            pltpu.VMEM((2, 640, 128), F32),
            pltpu.VMEM((512, 128), BF),
            pltpu.VMEM((256, 512), BF),
            pltpu.VMEM((10, 256, 128), F32),
            pltpu.VMEM((256, 1280), BF),
            pltpu.VMEM((36 * 224, HALF), BF),
            pltpu.VMEM((36 * 48, HALF), BF),
            pltpu.VMEM((ROWS, TL), F32),
            pltpu.VMEM((ROWS, TL), F32),
            pltpu.VMEM((ROWS, HALF), F32),
            pltpu.VMEM((32, HALF), F32),
            pltpu.VMEM((NZ, 128, TL), BF),
            pltpu.VMEM((NZ, 128, 2 * TL), F32),
            pltpu.VMEM((2, 32, TL), BF),
            pltpu.VMEM((3, 32, TL), BF),
            pltpu.VMEM((256, TL), BF),
            pltpu.VMEM((2, 128, 2 * TL), F32),
            pltpu.VMEM((128, 2 * TL), F32),
            pltpu.VMEM((4, 128, 128), F32),
            pltpu.VMEM((2 * NC, 8, 128), F32),
            pltpu.VMEM((2 * NC - 1, 8, 128), F32),
            pltpu.VMEM((NZ, 1, 128), F32),
            pltpu.VMEM((NZ, 1, 128), F32),
            dma((len(operands),)),
            dma((2,)),
            dma((2,)),
            dma((2,)),
            dma((2, 14)),
            dma((2, 14)),
            dma((3,)),
            dma((2,)),
            dma((1,)),
            dma((1,)),
            dma((NZ,)),
            dma((NZ,)),
            pltpu.SemaphoreType.REGULAR((5,)),
        ],
        compiler_params=pltpu.CompilerParams(
            collective_id=0, has_side_effects=True, vmem_limit_bytes=56 * 1024 * 1024
        ),
    )(*operands)


def solution(mesh):
    return jax.shard_map(
        body,
        mesh=mesh,
        in_specs=(
            P("chan", ("tmpl", "tm")),
            P("chan"),
            P("tmpl", "chan", None),
            P("tmpl"),
            P(),
            P(),
            P(),
            P(),
            P(),
            P(),
            P(),
            P(),
        ),
        out_specs=(P("chan", ("tmpl", "tm")), P("tmpl", None, "tm", "chan")),
        check_vma=False,
    )
```

```python
import functools
import math

import jax
import jax.numpy as jnp
import numpy as np
from jax import lax
from jax.experimental import pallas as pl
from jax.experimental.pallas import tpu as pltpu
from jax.sharding import PartitionSpec as P

BF = jnp.bfloat16
F32 = jnp.float32
MESH = pl.DeviceIdType.MESH
ROWS = 64
TL = 512
HALF = 256
NZ = 8
NC = 16
BIG = -1e30


def middle_table():
    q = np.zeros((3, 3, 16, 512), np.float32)
    for g in range(16):
        for rr in range(3):
            for v in range(3):
                q[rr, v, g, rr * 48 + v * 16 + g] = 1
    return q.reshape(144, 512)


def encoder_table():
    q = np.zeros((4, 3, 3, 128), np.float32)
    for v in range(4):
        for rr in range(3):
            for dt in range(3):
                q[v, rr, dt, rr * 8 + v + dt] = 1
    return q.reshape(4, 9, 128)


def decoder_table():
    q = np.zeros((4, 3, 3, 48, 640), np.float32)
    skip_at = [96, 160, 320, 384]
    up_at = [0, 224, 448]
    for ps in range(2):
        for pr in range(2):
            n = ps * 2 + pr
            for rr in range(4):
                for v in range(4):
                    if 0 <= rr - pr <= 2 and 0 <= v - ps <= 2:
                        for g in range(16):
                            q[n, rr - pr, v - ps, 32 + g, skip_at[rr] + v * 16 + g] = 1
            for dr in range(3):
                for dt in range(3):
                    rr = (pr + dr - 1) // 2 + 1
                    v = (ps + dt - 1) // 2 + 1
                    for m in range(32):
                        q[n, dr, dt, m, up_at[rr] + v * 32 + m] = 1
    return q.reshape(4, 432, 640)


def spectrum_table():
    s = np.arange(TL)[:, None]
    f = np.arange(TL)[None, :]
    phase = ((s * f) % (2 * TL)) * (math.pi / TL)
    re = np.cos(phase)
    im = -np.sin(phase)
    im[:, 0] = np.where(np.arange(TL) % 2 == 0, 1.0, -1.0)
    return np.concatenate([re, im], axis=1).astype(np.float32)


def lag_table():
    f = np.arange(TL)[:, None]
    j = np.arange(TL)[None, :]
    phase = ((f * j) % (2 * TL)) * (math.pi / TL)
    re = np.cos(phase) * 2
    im = -np.sin(phase) * 2
    re[0] = 1
    im[0] = np.where(np.arange(TL) % 2 == 0, 1.0, -1.0)
    return (np.concatenate([re, im], axis=0) / (2 * TL)).astype(np.float32)


def iota(shape, dim):
    return lax.broadcasted_iota(jnp.int32, shape, dim)


def mm(a, b):
    return jnp.dot(a, b, preferred_element_type=F32)


def column(ref, count, lanes):
    rows = iota((count, lanes), 0)
    out = jnp.zeros((count, lanes), F32)
    for g in range(count):
        out = jnp.where(rows == g, ref[g], out)
    return out


def kernel(
    raw_hbm, mask_hbm, tmpl_hbm, assign_hbm, wenc_hbm, benc_hbm, wmid_hbm, bmid_hbm,
    wdec_hbm, bdec_hbm, wout_hbm, bout_hbm, q1_hbm, q2_hbm, q3_hbm, f_hbm, i_hbm,
    den_ref, corr_ref,
    raw_ref, mask_ref, tmpl_ref, assign_ref, wenc_ref, benc_ref, wmid_ref, bmid_ref,
    wdec_ref, bdec_ref, wout_ref, bout_ref, q1_ref, q2_ref, q3_ref, f_ref, i_ref,
    clean_ref, halo_ref, cv_ref, w1_ref, w2_ref, wf_ref, w3_ref,
    u_ref, pv_ref, dp_ref, own_ref, alive_ref, b2_ref, tg_ref, ts_ref, sd_ref, xw_ref,
    xr_ref, z_ref, g_ref, lag_ref, rs_ref, rr_ref, as_ref, ar_ref,
    tab_sem, den_sem, halo_send, halo_recv, ring_send, ring_recv, x_send, x_recv,
    rs_send, rs_recv, a_send, a_recv, hello_sem,
):
    z = lax.axis_index("tmpl")
    c = lax.axis_index("chan")
    p = lax.axis_index("tm")
    me = p * NC + c
    zr = lax.rem(z + 1, NZ)
    zl = lax.rem(z + NZ - 1, NZ)

    loads = {}
    sources = [
        ("raw", raw_hbm, raw_ref), ("mask", mask_hbm, mask_ref), ("tmpl", tmpl_hbm, tmpl_ref),
        ("wenc", wenc_hbm, wenc_ref), ("q1", q1_hbm, q1_ref), ("benc", benc_hbm, benc_ref),
        ("wmid", wmid_hbm, wmid_ref), ("q2", q2_hbm, q2_ref), ("bmid", bmid_hbm, bmid_ref),
        ("wdec", wdec_hbm, wdec_ref), ("q3", q3_hbm, q3_ref),
        ("bdec", bdec_hbm, bdec_ref), ("wout", wout_hbm, wout_ref), ("bout", bout_hbm, bout_ref),
        ("f", f_hbm, f_ref), ("assign", assign_hbm, assign_ref), ("i", i_hbm, i_ref),
    ]

    def fetch(first, last):
        for n in range(first, last):
            name, source, target = sources[n]
            loads[name] = pltpu.make_async_copy(source, target, tab_sem.at[n])
            loads[name].start()

    def ready(*names):
        for name in names:
            loads[name].wait()

    fetch(0, 3)

    barrier = pltpu.get_barrier_semaphore()
    up = lax.rem(c + NC - 1, NC)
    down = lax.rem(c + 1, NC)
    flip = lambda n: c + n - 2 * n * lax.rem(c // n, 2)
    partners = [(z, flip(n), p) for n in (1, 2, 4, 8)] + [(z, c, 1 - p)]
    greeted = partners[1:] + [
        (z, up, p), (z, down, p), (zr, c, p), (zl, c, p), (zr, c, 1 - p), (zl, c, 1 - p)
    ]
    for device in greeted:
        pl.semaphore_signal(barrier, inc=1, device_id=device, device_id_type=MESH)
    fetch(3, len(sources))

    def greet(n):
        pl.semaphore_signal(hello_sem.at[n], inc=1, device_id=partners[n], device_id_type=MESH)

    def greeting(n):
        pl.semaphore_wait(hello_sem.at[n], 1)
        if n < 4:
            greet(n + 1)

    ready("raw", "mask")
    mask = mask_ref[...].astype(F32)
    diag = jnp.where(iota((ROWS, ROWS), 0) == iota((ROWS, ROWS), 1), mask, 0.0).astype(BF)
    clean = mm(diag, raw_ref[...]).astype(BF)
    clean_ref[...] = clean

    ready("tmpl")
    rows = iota((128, 256), 0)
    pick = (rows % 4) * 64 + p * 32 + rows // 4 == iota((128, 256), 1)
    tg_ref[0] = mm(jnp.where(pick, 1.0, 0.0).astype(BF), tmpl_ref[...].reshape(256, TL)).astype(BF)

    pl.semaphore_wait(barrier, len(greeted))
    greet(0)

    halos = [
        pltpu.make_async_remote_copy(
            src_ref=clean_ref.at[pl.ds(0, 16)], dst_ref=halo_ref.at[1],
            send_sem=halo_send.at[0], recv_sem=halo_recv.at[0],
            device_id=(z, up, p), device_id_type=MESH),
        pltpu.make_async_remote_copy(
            src_ref=clean_ref.at[pl.ds(48, 16)], dst_ref=halo_ref.at[0],
            send_sem=halo_send.at[1], recv_sem=halo_recv.at[1],
            device_id=(z, down, p), device_id_type=MESH),
    ]
    def right(s, n):
        part = pl.ds(n * 32, 32)
        source, target, hops = (3, 7, 2) if s == 3 else (max(2 * s - 1, 0), 2 * s + 1, 1)
        return pltpu.make_async_remote_copy(
            src_ref=tg_ref.at[source, part], dst_ref=tg_ref.at[target, part],
            send_sem=ring_send.at[0, 4 * s + n], recv_sem=ring_recv.at[0, 4 * s + n],
            device_id=(lax.rem(z + hops, NZ), c, p), device_id_type=MESH)

    def left(s, n):
        part = pl.ds(96 - n * 32, 32)
        source, target, hops = (4, 7, 2) if s == 3 else (2 * s, 2 * s + 2, 1)
        return pltpu.make_async_remote_copy(
            src_ref=tg_ref.at[source, part], dst_ref=tg_ref.at[target, part],
            send_sem=ring_send.at[1, 4 * s + n], recv_sem=ring_recv.at[1, 4 * s + n],
            device_id=(lax.rem(z + NZ - hops, NZ), c, p), device_id_type=MESH)

    def forward(s, n):
        right(s - 1, n).wait_recv()
        left(s - 1, n).wait_recv()
        if s == 2 and n < 2:
            right(3, n).start()
            left(3, n).start()
        right(s, n).start()
        left(s, n).start()

    def arrived(s, first, last):
        for n in range(first, last):
            right(s, n).wait_recv()
            left(s, n).wait_recv()

    for n in range(2):
        right(0, n).start()
        left(0, n).start()
    for h in halos:
        h.start()
    for n in range(2, 4):
        right(0, n).start()
        left(0, n).start()

    scol = iota((TL, TL), 1)
    split = jnp.where(
        iota((TL, TL), 0) == (scol % HALF) * 2 + scol // HALF, 1.0, 0.0
    ).astype(BF)
    later = lambda x, lanes: jnp.where(lanes == 0, jnp.zeros_like(x), pltpu.roll(x, 1, 1))
    sooner = lambda x, lanes: jnp.where(lanes == HALF - 1, jnp.zeros_like(x), pltpu.roll(x, HALF - 1, 1))

    def variants(tall):
        parted = mm(tall.astype(BF), split)
        even = parted[:, :HALF]
        odd = parted[:, HALF:]
        lanes = iota(even.shape, 1)
        return [
            later(even, lanes), later(odd, lanes), even, odd, sooner(even, lanes), sooner(odd, lanes)
        ]

    inner = jnp.where(iota((80, 64), 0) == iota((80, 64), 1) + 5, 1.0, 0.0).astype(BF)
    slots = variants(mm(inner, clean))
    slots.append(jnp.ones((80, HALF), F32))
    edge = jnp.where(iota((80, HALF), 0) % 2 == 0, 0, HALF - 1)
    slots.append(jnp.where(iota((80, HALF), 1) == edge, 1.0, 0.0))
    for n in range(8):
        for h in range(2):
            cv_ref[h, pl.ds(n, 80, stride=8), :] = slots[n][:, h * 128 : (h + 1) * 128]

    ready("wenc", "q1", "benc")
    lane128 = iota((64, 128), 1)
    row64 = iota((64, 128), 0)
    bias = column(benc_ref, 16, 128)
    hi = bias.astype(BF).astype(F32)
    mid = (bias - hi).astype(BF).astype(F32)
    low = bias - hi - mid
    four = lambda x: jnp.concatenate([x] * 4, axis=0)
    fixed = jnp.where(lane128 == 6, four(hi), 0.0)
    fixed = jnp.where(lane128 == 14, four(mid), fixed)
    fixed = jnp.where(lane128 == 22, four(low), fixed)
    fixed = jnp.where((lane128 == 7) & (row64 < 16), BIG, fixed)
    fixed = jnp.where((lane128 == 15) & (row64 >= 48), BIG, fixed)
    wenc = jnp.concatenate([wenc_ref[r] for r in range(3)], axis=0)
    over = lambda w, q: lax.dot_general(w, q, (((0,), (0,)), ((), ())), preferred_element_type=F32)
    base1 = jnp.concatenate([over(wenc, q1_ref[v]) for v in range(4)], axis=0)
    for r in range(8):
        w1_ref[pl.ds(r * 64, 64), :] = (
            (pltpu.roll(base1, 8 * r, 1) if r else base1) + fixed
        ).astype(BF)

    def staggered(start, end, items):
        held = None
        for item in items:
            value = start(item)
            if held is not None:
                end(*held)
            held = (item, value)
        end(*held)

    def encode(q):
        window = jnp.concatenate([cv_ref[h, q * 64 : q * 64 + 128, :] for h in range(2)], axis=1)
        return mm(w1_ref[...], window.astype(BF))

    def encoded(q, e):
        e = jnp.maximum(e, 0.0).astype(BF)
        for k in range(8):
            at = (4 * q + k // 2) * 224 + k % 2 * 160
            u_ref[at : at + 64, :] = e[k * 64 : (k + 1) * 64]

    staggered(encode, encoded, range(1, 8))

    lane16 = iota((16, HALF), 1)

    def pool(i):
        first = pl.multiple_of(i * 224, 16)
        part = lambda o: u_ref[pl.ds(first + o, 16), :].astype(F32)
        pooled = (part(16) + part(32) + part(176) + part(192)) * 0.25
        at = pl.multiple_of(i * 48, 16)
        pv_ref[pl.ds(at, 16), :] = later(pooled, lane16).astype(BF)
        pv_ref[pl.ds(at + 16, 16), :] = pooled.astype(BF)
        pv_ref[pl.ds(at + 32, 16), :] = sooner(pooled, lane16).astype(BF)

    pl.loop(4, 32, unroll=7)(pool)
    greeting(0)

    ready("wmid", "q2", "bmid")
    base2 = over(wmid_ref[...].reshape(144, 32), q2_ref[...])
    for r in range(8):
        w2_ref[pl.ds(r * 32, 32), :] = (
            pltpu.roll(base2, 48 * r, 1) if r else base2
        ).astype(BF)
    b2_ref[...] = column(bmid_ref, 32, HALF)

    lane32 = iota((32, HALF), 1)

    def convolve(q):
        if q == 4:
            return mm(w2_ref[0:64, :192], pv_ref[1536:1728, :])
        return mm(w2_ref[:, :480], pv_ref[q * 384 : q * 384 + 480, :])

    def middle(q, acc):
        for r in range(2 if q == 4 else 8):
            m = jnp.maximum(acc[r * 32 : (r + 1) * 32] + b2_ref[...], 0.0).astype(BF)
            at = (q * 8 + r + 1) * 224 + 64
            u_ref[at : at + 32, :] = later(m, lane32)
            u_ref[at + 32 : at + 64, :] = m
            u_ref[at + 64 : at + 96, :] = sooner(m, lane32)

    staggered(convolve, middle, (1, 2))
    forward(1, 0)
    forward(1, 1)

    ready("wdec", "q3", "bdec", "wout", "bout")
    wdec = jnp.concatenate([wdec_ref[dr, dt] for dr in range(3) for dt in range(3)], axis=1)
    for n in range(4):
        wide = jnp.concatenate([mm(wdec, q3_ref[n]), jnp.zeros((16, 640), F32)], axis=1)
        for r in range(4):
            turned = pltpu.roll(wide, 224 * r, 1) if r else wide
            for t in range(10):
                wf_ref[t, pl.ds(n // 2 * 8 + 2 * r + n % 2, 16, stride=16), :] = (
                    turned[:, t * 128 : (t + 1) * 128]
                )
    w3_ref[...] = jnp.concatenate([wf_ref[t] for t in range(10)], axis=1).astype(BF)
    wrow = mm(wout_ref[...], jnp.eye(16, dtype=F32).astype(BF))
    wout = [wrow[:, g : g + 1] for g in range(16)]
    own_ref[...] = mm(clean, split)
    alive_ref[...] = mm(diag, jnp.ones((ROWS, HALF), BF))

    forward(1, 2)
    forward(1, 3)

    def gather(q):
        first = q * 896 + 288
        if not isinstance(q, int):
            first = pl.multiple_of(first, 32)
        return mm(w3_ref[:, :1216], u_ref[pl.ds(first, 1216), :])

    def decode(q, acc):
        branch = None
        for g in range(16):
            tile = jnp.maximum(acc[g * 16 : (g + 1) * 16] + bdec_ref[g], 0.0)
            term = tile.astype(BF).astype(F32) * wout[g]
            branch = term if branch is None else branch + term
        here = pl.ds(q * 8 if isinstance(q, int) else pl.multiple_of(q * 8, 8), 8)
        alive = alive_ref[here, :]
        for ps in range(2):
            lanes = slice(ps * HALF, (ps + 1) * HALF)
            dp_ref[here, lanes] = alive * (
                own_ref[here, lanes] + branch[ps * 8 : ps * 8 + 8] + bout_ref[0]
            )

    def results(h):
        here = pl.ds(pl.multiple_of(h * 32, 32), 32)
        return pltpu.make_async_copy(sd_ref.at[h], den_ref.at[here], den_sem.at[h])

    def finish(h):
        here = pl.ds(pl.multiple_of(h * 32, 32), 32)
        natural = lax.dot_general(
            dp_ref[here, :].astype(BF), split, (((1,), (1,)), ((), ())), preferred_element_type=F32
        ).astype(BF)
        sd_ref[h] = natural
        results(h).start()

    to_partner = pltpu.make_async_remote_copy(
        src_ref=sd_ref.at[1 - p], dst_ref=xw_ref.at[p],
        send_sem=x_send.at[0], recv_sem=x_recv.at[0],
        device_id=(z, c, 1 - p), device_id_type=MESH)

    def to_previous(h):
        return pltpu.make_async_remote_copy(
            src_ref=sd_ref.at[h], dst_ref=xw_ref.at[2],
            send_sem=x_send.at[1 + h], recv_sem=x_recv.at[1],
            device_id=(zl, c, h), device_id_type=MESH)

    staggered(gather, decode, (2, 3, 4))
    greeting(1)

    for h in halos:
        h.wait_recv()
    far = iota((24, 16), 0)
    far = jnp.where(far < 8, far, far + 56)
    away = iota((24, 16), 1)
    above = jnp.where((far + 11 == away) & (c > 0), 1.0, 0.0).astype(BF)
    below = jnp.where((far == away + 69) & (away < 5) & (c < NC - 1), 1.0, 0.0).astype(BF)
    near = iota((24, 64), 0)
    near = jnp.where(near < 8, near, near + 56)
    kept = jnp.where(near == iota((24, 64), 1) + 5, 1.0, 0.0).astype(BF)
    edges = variants(mm(kept, clean) + mm(above, halo_ref[0]) + mm(below, halo_ref[1]))
    for n in range(6):
        for h in range(2):
            cut = edges[n][:, h * 128 : (h + 1) * 128]
            cv_ref[h, pl.ds(n, 8, stride=8), :] = cut[:8]
            cv_ref[h, pl.ds(512 + n, 16, stride=8), :] = cut[8:]
    staggered(encode, encoded, (0, 8))

    @pl.when(c == 0)
    def _():
        u_ref[0:448, :] = jnp.zeros((448, HALF), BF)

    @pl.when(c == NC - 1)
    def _():
        u_ref[34 * 224 : 36 * 224, :] = jnp.zeros((448, HALF), BF)

    for i in (0, 1, 2, 3, 32, 33, 34, 35):
        pool(i)

    forward(2, 0)
    staggered(convolve, middle, (0, 3, 4))

    @pl.when(c == 0)
    def _():
        u_ref[288:384, :] = jnp.zeros((96, HALF), BF)

    @pl.when(c == NC - 1)
    def _():
        u_ref[34 * 224 + 64 : 34 * 224 + 160, :] = jnp.zeros((96, HALF), BF)

    forward(2, 1)
    greeting(2)
    theirs = 6 * (1 - p)
    staggered(gather, decode, (5, theirs, theirs + 1))
    finish(1 - p)
    to_partner.start()

    @pl.when(p == 0)
    def _():
        to_previous(1).start()

    forward(2, 2)
    forward(2, 3)
    greeting(3)
    staggered(gather, decode, (6 * p, 6 * p + 1))
    finish(p)

    @pl.when(p == 0)
    def _():
        to_previous(0).start()

    xw_ref[p] = sd_ref[p]

    ready("f")

    def transform(first, count):
        wide = mm(tg_ref[first : first + count].reshape(count * 128, TL), f_ref[...])
        ts_ref[first : first + count] = wide.reshape(count, 128, 2 * TL)

    transform(0, 3)
    greeting(4)

    rrow = iota((128, 32), 0)
    repeat = jnp.where(rrow // 4 == iota((128, 32), 1), 1.0, 0.0).astype(BF)
    lane1k = iota((128, 2 * TL), 1)
    sign = jnp.where((lane1k % 2 == 1), -1.0, 1.0)
    to_partner.wait_recv()
    for n in range(2):
        xr_ref[pl.ds(n * 128, 128), :] = mm(repeat, xw_ref[n]).astype(BF)
    spectra = mm(xr_ref[...], f_ref[...])
    z_ref[0] = spectra[0:128] + sign * spectra[128:256]
    z_ref[1] = spectra[128:256]

    transform(3, 2)

    lane512 = iota((8, TL), 1)

    def product(n, k):
        a = jnp.zeros((8, TL), F32)
        b = jnp.zeros((8, TL), F32)
        d = jnp.zeros((8, TL), F32)
        for s in range(16):
            here = pl.ds(s * 8, 8)
            tr = ts_ref[k, here, 0:TL]
            ti = ts_ref[k, here, TL : 2 * TL]
            sr = z_ref[n, here, 0:TL]
            si = z_ref[n, here, TL : 2 * TL]
            a = a + sr * tr
            b = b + si * ti
            d = d + (si * tr - sr * ti)
        a = a + pltpu.roll(a, 4, 0)
        b = b + pltpu.roll(b, 4, 0)
        d = d + pltpu.roll(d, 4, 0)
        at = pl.ds(pl.multiple_of(n * 64 + k * 8, 8), 8)
        g_ref[at, 0:TL] = jnp.where(lane512 == 0, a, a + b)
        g_ref[at, TL : 2 * TL] = jnp.where(lane512 == 0, b, d)

    pl.loop(0, 5, unroll=True)(functools.partial(product, 0))
    to_previous(0).wait_recv()
    following = xw_ref[2] * jnp.where(z == NZ - 1, 0.0, 1.0).astype(BF)
    z_ref[1] = z_ref[1] + sign * mm(mm(repeat, following).astype(BF), f_ref[...])
    pl.loop(0, 5, unroll=True)(functools.partial(product, 1))
    arrived(2, 0, 4)
    arrived(3, 0, 2)
    transform(5, 3)
    pl.loop(5, 8, unroll=True)(functools.partial(product, 0))
    pl.loop(5, 8, unroll=True)(functools.partial(product, 1))

    ready("i")
    lags = mm(g_ref[...].astype(BF), i_ref[...])
    for t in range(4):
        lag_ref[t] = lags[:, t * 128 : (t + 1) * 128]

    lane8 = iota((8, 128), 1) // 32
    for n in range(2):
        for t in range(4):
            quarter = [lag_ref[t, pl.ds(n * 64 + k, 8, stride=8), :] for k in range(4)]
            for o in range(4):
                piece = jnp.zeros((8, 128), F32)
                for k in range(4):
                    shift = (k - o) % 4 * 32
                    moved = pltpu.roll(quarter[k], shift, 1) if shift else quarter[k]
                    piece = jnp.where(lane8 == k, moved, piece)
                rs_ref[n * NC + t * 4 + o] = piece

    hops = [0, 2, 1, 1]
    steps = [0, 1, 2, 1]
    for d in sorted(range(1, 2 * NC), key=lambda d: -hops[d // 8] - steps[d // 2 % 4]):
        other = lax.rem(me + d, 2 * NC)
        pltpu.make_async_remote_copy(
            src_ref=rs_ref.at[other], dst_ref=rr_ref.at[d - 1],
            send_sem=rs_send.at[0], recv_sem=rs_recv.at[0],
            device_id=(z, lax.rem(other, NC), other // NC), device_id_type=MESH).start()

    shares = pltpu.make_async_remote_copy(
        src_ref=rr_ref, dst_ref=rr_ref, send_sem=rs_send.at[0], recv_sem=rs_recv.at[0],
        device_id=(z, c, 1 - p), device_id_type=MESH)
    shares.wait_recv()
    parts = [rs_ref[me]] + [rr_ref[d] for d in range(2 * NC - 1)]
    while len(parts) > 1:
        parts = [parts[n] + parts[n + 1] for n in range(0, len(parts), 2)]
    as_ref[...] = parts[0].reshape(8, 1, 128)

    places = [0, 1, -1, 2, -2, 3, -3, 4]
    for d in range(NZ - 1, 0, -1):
        pltpu.make_async_remote_copy(
            src_ref=as_ref.at[d], dst_ref=ar_ref.at[z],
            send_sem=a_send.at[d], recv_sem=a_recv.at[z],
            device_id=(lax.rem(z + NZ - places[d], NZ), c, p), device_id_type=MESH).start()

    ar_ref[z] = as_ref[0]

    def landing(d):
        other = lax.rem(z + NZ + places[d], NZ)
        return pltpu.make_async_remote_copy(
            src_ref=as_ref.at[d], dst_ref=ar_ref.at[other],
            send_sem=a_send.at[d], recv_sem=a_recv.at[other],
            device_id=(other, c, p), device_id_type=MESH)

    for d in range(1, NZ):
        landing(d).wait_recv()

    found = ar_ref[...].reshape(8, 128)
    turned = [found] + [pltpu.roll(found, 128 - 32 * k, 1) for k in range(1, 4)]
    ready("assign")
    for r in range(4):
        local = lax.rem(assign_ref[r], 4)
        row = jnp.zeros((8, 128), F32)
        for k in range(4):
            row = row + jnp.where(local == k, 1.0, 0.0) * turned[k]
        corr_ref[r] = row[:, :32].reshape(8, 1, 32)

    results(0).wait()
    results(1).wait()
    for h in halos:
        h.wait_send()
    for s in range(4):
        for n in range(4 if s < 3 else 2):
            right(s, n).wait_send()
            left(s, n).wait_send()
    to_partner.wait_send()

    @pl.when(p == 0)
    def _():
        to_previous(0).wait_send()
        to_previous(1).wait_send()

    shares.wait_send()
    for d in range(1, NZ):
        landing(d).wait_send()


def body(raw, dead_mask, templates, assign, w_enc, b_enc, w_mid, b_mid, w_dec, b_dec, w_out, b_out):
    vm = pl.BlockSpec(memory_space=pltpu.VMEM)
    hbm = pl.BlockSpec(memory_space=pltpu.HBM)
    dma = pltpu.SemaphoreType.DMA
    tables = [
        jnp.asarray(t, BF)
        for t in (encoder_table(), middle_table(), decoder_table(), spectrum_table(), lag_table())
    ]
    operands = [
        raw,
        dead_mask.reshape(1, ROWS),
        templates,
        assign,
        w_enc.transpose(1, 2, 3, 0).reshape(3, 3, 16),
        b_enc,
        w_mid.transpose(2, 3, 1, 0),
        b_mid,
        w_dec.transpose(2, 3, 0, 1),
        b_dec,
        w_out.reshape(1, 16),
        b_out,
    ] + tables
    scalars = (3, 5, 7, 9, 11)
    landing_places = [
        (pltpu.SMEM if n in scalars else pltpu.VMEM)(x.shape, x.dtype)
        for n, x in enumerate(operands)
    ]
    return pl.pallas_call(
        kernel,
        out_shape=(
            jax.ShapeDtypeStruct((ROWS, TL), BF),
            jax.ShapeDtypeStruct((4, 8, 1, 32), F32),
        ),
        in_specs=[hbm] * len(operands),
        out_specs=(hbm, vm),
        scratch_shapes=landing_places + [
            pltpu.VMEM((ROWS, TL), BF),
            pltpu.VMEM((2, 16, TL), BF),
            pltpu.VMEM((2, 640, 128), F32),
            pltpu.VMEM((512, 128), BF),
            pltpu.VMEM((256, 512), BF),
            pltpu.VMEM((10, 256, 128), F32),
            pltpu.VMEM((256, 1280), BF),
            pltpu.VMEM((36 * 224, HALF), BF),
            pltpu.VMEM((36 * 48, HALF), BF),
            pltpu.VMEM((ROWS, TL), F32),
            pltpu.VMEM((ROWS, TL), F32),
            pltpu.VMEM((ROWS, HALF), F32),
            pltpu.VMEM((32, HALF), F32),
            pltpu.VMEM((NZ, 128, TL), BF),
            pltpu.VMEM((NZ, 128, 2 * TL), F32),
            pltpu.VMEM((2, 32, TL), BF),
            pltpu.VMEM((3, 32, TL), BF),
            pltpu.VMEM((256, TL), BF),
            pltpu.VMEM((2, 128, 2 * TL), F32),
            pltpu.VMEM((128, 2 * TL), F32),
            pltpu.VMEM((4, 128, 128), F32),
            pltpu.VMEM((2 * NC, 8, 128), F32),
            pltpu.VMEM((2 * NC - 1, 8, 128), F32),
            pltpu.VMEM((NZ, 1, 128), F32),
            pltpu.VMEM((NZ, 1, 128), F32),
            dma((len(operands),)),
            dma((2,)),
            dma((2,)),
            dma((2,)),
            dma((2, 14)),
            dma((2, 14)),
            dma((3,)),
            dma((2,)),
            dma((1,)),
            dma((1,)),
            dma((NZ,)),
            dma((NZ,)),
            pltpu.SemaphoreType.REGULAR((5,)),
        ],
        compiler_params=pltpu.CompilerParams(
            collective_id=0, has_side_effects=True, vmem_limit_bytes=56 * 1024 * 1024
        ),
    )(*operands)


def solution(mesh):
    return jax.shard_map(
        body,
        mesh=mesh,
        in_specs=(
            P("chan", ("tmpl", "tm")),
            P("chan"),
            P("tmpl", "chan", None),
            P("tmpl"),
            P(),
            P(),
            P(),
            P(),
            P(),
            P(),
            P(),
            P(),
        ),
        out_specs=(P("chan", ("tmpl", "tm")), P("tmpl", None, "tm", "chan")),
        check_vma=False,
    )
```

```python
import functools
import math

import jax
import jax.numpy as jnp
import numpy as np
from jax import lax
from jax.experimental import pallas as pl
from jax.experimental.pallas import tpu as pltpu
from jax.sharding import PartitionSpec as P

BF = jnp.bfloat16
F32 = jnp.float32
MESH = pl.DeviceIdType.MESH
ROWS = 64
TL = 512
HALF = 256
NZ = 8
NC = 16
BIG = -1e30


def middle_table():
    q = np.zeros((3, 3, 16, 512), np.float32)
    for g in range(16):
        for rr in range(3):
            for v in range(3):
                q[rr, v, g, rr * 48 + v * 16 + g] = 1
    return q.reshape(144, 512)


def encoder_table():
    q = np.zeros((4, 3, 3, 128), np.float32)
    for v in range(4):
        for rr in range(3):
            for dt in range(3):
                q[v, rr, dt, rr * 8 + v + dt] = 1
    return q.reshape(4, 9, 128)


def decoder_table():
    q = np.zeros((4, 3, 3, 48, 640), np.float32)
    skip_at = [96, 160, 320, 384]
    up_at = [0, 224, 448]
    for ps in range(2):
        for pr in range(2):
            n = ps * 2 + pr
            for rr in range(4):
                for v in range(4):
                    if 0 <= rr - pr <= 2 and 0 <= v - ps <= 2:
                        for g in range(16):
                            q[n, rr - pr, v - ps, 32 + g, skip_at[rr] + v * 16 + g] = 1
            for dr in range(3):
                for dt in range(3):
                    rr = (pr + dr - 1) // 2 + 1
                    v = (ps + dt - 1) // 2 + 1
                    for m in range(32):
                        q[n, dr, dt, m, up_at[rr] + v * 32 + m] = 1
    return q.reshape(4, 432, 640)


def spectrum_table():
    s = np.arange(TL)[:, None]
    f = np.arange(TL)[None, :]
    phase = ((s * f) % (2 * TL)) * (math.pi / TL)
    re = np.cos(phase)
    im = -np.sin(phase)
    im[:, 0] = np.where(np.arange(TL) % 2 == 0, 1.0, -1.0)
    return np.concatenate([re, im], axis=1).astype(np.float32)


def lag_table():
    f = np.arange(TL)[:, None]
    j = np.arange(TL)[None, :]
    phase = ((f * j) % (2 * TL)) * (math.pi / TL)
    re = np.cos(phase) * 2
    im = -np.sin(phase) * 2
    re[0] = 1
    im[0] = np.where(np.arange(TL) % 2 == 0, 1.0, -1.0)
    return (np.concatenate([re, im], axis=0) / (2 * TL)).astype(np.float32)


def iota(shape, dim):
    return lax.broadcasted_iota(jnp.int32, shape, dim)


def mm(a, b):
    return jnp.dot(a, b, preferred_element_type=F32)


def column(ref, count, lanes):
    rows = iota((count, lanes), 0)
    out = jnp.zeros((count, lanes), F32)
    for g in range(count):
        out = jnp.where(rows == g, ref[g], out)
    return out


def kernel(
    raw_hbm, mask_hbm, tmpl_hbm, assign_hbm, wenc_hbm, benc_hbm, wmid_hbm, bmid_hbm,
    wdec_hbm, bdec_hbm, wout_hbm, bout_hbm, q1_hbm, q2_hbm, q3_hbm, f_hbm, i_hbm,
    den_ref, corr_ref,
    raw_ref, mask_ref, tmpl_ref, assign_ref, wenc_ref, benc_ref, wmid_ref, bmid_ref,
    wdec_ref, bdec_ref, wout_ref, bout_ref, q1_ref, q2_ref, q3_ref, f_ref, i_ref,
    clean_ref, halo_ref, cv_ref, w1_ref, w2_ref, wf_ref, w3_ref,
    u_ref, pv_ref, dp_ref, own_ref, alive_ref, b2_ref, tg_ref, ts_ref, sd_ref, xw_ref,
    xr_ref, z_ref, g_ref, lag_ref, rs_ref, rr_ref, as_ref, ar_ref,
    tab_sem, den_sem, halo_send, halo_recv, ring_send, ring_recv, x_send, x_recv,
    rs_send, rs_recv, a_send, a_recv, hello_sem,
):
    z = lax.axis_index("tmpl")
    c = lax.axis_index("chan")
    p = lax.axis_index("tm")
    me = p * NC + c
    zr = lax.rem(z + 1, NZ)
    zl = lax.rem(z + NZ - 1, NZ)

    loads = {}
    sources = [
        ("raw", raw_hbm, raw_ref), ("mask", mask_hbm, mask_ref), ("tmpl", tmpl_hbm, tmpl_ref),
        ("wenc", wenc_hbm, wenc_ref), ("q1", q1_hbm, q1_ref), ("benc", benc_hbm, benc_ref),
        ("wmid", wmid_hbm, wmid_ref), ("q2", q2_hbm, q2_ref), ("bmid", bmid_hbm, bmid_ref),
        ("wdec", wdec_hbm, wdec_ref), ("q3", q3_hbm, q3_ref),
        ("bdec", bdec_hbm, bdec_ref), ("wout", wout_hbm, wout_ref), ("bout", bout_hbm, bout_ref),
        ("f", f_hbm, f_ref), ("assign", assign_hbm, assign_ref), ("i", i_hbm, i_ref),
    ]

    def fetch(first, last):
        for n in range(first, last):
            name, source, target = sources[n]
            loads[name] = pltpu.make_async_copy(source, target, tab_sem.at[n])
            loads[name].start()

    def ready(*names):
        for name in names:
            loads[name].wait()

    fetch(0, 3)

    barrier = pltpu.get_barrier_semaphore()
    up = lax.rem(c + NC - 1, NC)
    down = lax.rem(c + 1, NC)
    flip = lambda n: n - 2 * n * lax.rem(c // n, 2)
    partners = [
        (z, c + flip(1), p), (z, c + flip(2), p), (z, c + flip(2) + flip(4), p),
        (z, c, 1 - p), (z, c + flip(8), 1 - p),
    ]
    greeted = partners[1:] + [
        (z, up, p), (z, down, p), (zr, c, p), (zl, c, p), (zr, c, 1 - p), (zl, c, 1 - p)
    ]
    for device in greeted:
        pl.semaphore_signal(barrier, inc=1, device_id=device, device_id_type=MESH)
    fetch(3, len(sources))

    def greet(n):
        pl.semaphore_signal(hello_sem.at[n], inc=1, device_id=partners[n], device_id_type=MESH)

    def greeting(n):
        pl.semaphore_wait(hello_sem.at[n], 1)
        if n < 4:
            greet(n + 1)

    ready("raw", "mask")
    mask = mask_ref[...].astype(F32)
    diag = jnp.where(iota((ROWS, ROWS), 0) == iota((ROWS, ROWS), 1), mask, 0.0).astype(BF)
    clean = mm(diag, raw_ref[...]).astype(BF)
    clean_ref[...] = clean

    ready("tmpl")
    rows = iota((128, 256), 0)
    pick = (rows % 4) * 64 + p * 32 + rows // 4 == iota((128, 256), 1)
    tg_ref[0] = mm(jnp.where(pick, 1.0, 0.0).astype(BF), tmpl_ref[...].reshape(256, TL)).astype(BF)

    pl.semaphore_wait(barrier, len(greeted))
    greet(0)

    halos = [
        pltpu.make_async_remote_copy(
            src_ref=clean_ref.at[pl.ds(0, 16)], dst_ref=halo_ref.at[1],
            send_sem=halo_send.at[0], recv_sem=halo_recv.at[0],
            device_id=(z, up, p), device_id_type=MESH),
        pltpu.make_async_remote_copy(
            src_ref=clean_ref.at[pl.ds(48, 16)], dst_ref=halo_ref.at[0],
            send_sem=halo_send.at[1], recv_sem=halo_recv.at[1],
            device_id=(z, down, p), device_id_type=MESH),
    ]
    def right(s, n):
        part = pl.ds(n * 32, 32)
        source, target, hops = (3, 7, 2) if s == 3 else (max(2 * s - 1, 0), 2 * s + 1, 1)
        return pltpu.make_async_remote_copy(
            src_ref=tg_ref.at[source, part], dst_ref=tg_ref.at[target, part],
            send_sem=ring_send.at[0, 4 * s + n], recv_sem=ring_recv.at[0, 4 * s + n],
            device_id=(lax.rem(z + hops, NZ), c, p), device_id_type=MESH)

    def left(s, n):
        part = pl.ds(96 - n * 32, 32)
        source, target, hops = (4, 7, 2) if s == 3 else (2 * s, 2 * s + 2, 1)
        return pltpu.make_async_remote_copy(
            src_ref=tg_ref.at[source, part], dst_ref=tg_ref.at[target, part],
            send_sem=ring_send.at[1, 4 * s + n], recv_sem=ring_recv.at[1, 4 * s + n],
            device_id=(lax.rem(z + NZ - hops, NZ), c, p), device_id_type=MESH)

    def forward(s, n):
        right(s - 1, n).wait_recv()
        left(s - 1, n).wait_recv()
        if s == 2 and n < 2:
            right(3, n).start()
            left(3, n).start()
        right(s, n).start()
        left(s, n).start()

    def arrived(s, first, last):
        for n in range(first, last):
            right(s, n).wait_recv()
            left(s, n).wait_recv()

    for n in range(2):
        right(0, n).start()
        left(0, n).start()
    for h in halos:
        h.start()
    for n in range(2, 4):
        right(0, n).start()
        left(0, n).start()

    scol = iota((TL, TL), 1)
    split = jnp.where(
        iota((TL, TL), 0) == (scol % HALF) * 2 + scol // HALF, 1.0, 0.0
    ).astype(BF)
    later = lambda x, lanes: jnp.where(lanes == 0, jnp.zeros_like(x), pltpu.roll(x, 1, 1))
    sooner = lambda x, lanes: jnp.where(lanes == HALF - 1, jnp.zeros_like(x), pltpu.roll(x, HALF - 1, 1))

    def variants(tall):
        parted = mm(tall.astype(BF), split)
        even = parted[:, :HALF]
        odd = parted[:, HALF:]
        lanes = iota(even.shape, 1)
        return [
            later(even, lanes), later(odd, lanes), even, odd, sooner(even, lanes), sooner(odd, lanes)
        ]

    inner = jnp.where(iota((80, 64), 0) == iota((80, 64), 1) + 5, 1.0, 0.0).astype(BF)
    slots = variants(mm(inner, clean))
    slots.append(jnp.ones((80, HALF), F32))
    edge = jnp.where(iota((80, HALF), 0) % 2 == 0, 0, HALF - 1)
    slots.append(jnp.where(iota((80, HALF), 1) == edge, 1.0, 0.0))
    for n in range(8):
        for h in range(2):
            cv_ref[h, pl.ds(n, 80, stride=8), :] = slots[n][:, h * 128 : (h + 1) * 128]

    ready("wenc", "q1", "benc")
    lane128 = iota((64, 128), 1)
    row64 = iota((64, 128), 0)
    bias = column(benc_ref, 16, 128)
    hi = bias.astype(BF).astype(F32)
    mid = (bias - hi).astype(BF).astype(F32)
    low = bias - hi - mid
    four = lambda x: jnp.concatenate([x] * 4, axis=0)
    fixed = jnp.where(lane128 == 6, four(hi), 0.0)
    fixed = jnp.where(lane128 == 14, four(mid), fixed)
    fixed = jnp.where(lane128 == 22, four(low), fixed)
    fixed = jnp.where((lane128 == 7) & (row64 < 16), BIG, fixed)
    fixed = jnp.where((lane128 == 15) & (row64 >= 48), BIG, fixed)
    wenc = jnp.concatenate([wenc_ref[r] for r in range(3)], axis=0)
    over = lambda w, q: lax.dot_general(w, q, (((0,), (0,)), ((), ())), preferred_element_type=F32)
    base1 = jnp.concatenate([over(wenc, q1_ref[v]) for v in range(4)], axis=0)
    for r in range(8):
        w1_ref[pl.ds(r * 64, 64), :] = (
            (pltpu.roll(base1, 8 * r, 1) if r else base1) + fixed
        ).astype(BF)

    def staggered(start, end, items):
        held = None
        for item in items:
            value = start(item)
            if held is not None:
                end(*held)
            held = (item, value)
        end(*held)

    def encode(q):
        window = jnp.concatenate([cv_ref[h, q * 64 : q * 64 + 128, :] for h in range(2)], axis=1)
        return mm(w1_ref[...], window.astype(BF))

    def encoded(q, e):
        e = jnp.maximum(e, 0.0).astype(BF)
        for k in range(8):
            at = (4 * q + k // 2) * 224 + k % 2 * 160
            u_ref[at : at + 64, :] = e[k * 64 : (k + 1) * 64]

    staggered(encode, encoded, range(1, 8))

    lane16 = iota((16, HALF), 1)

    def pool(i):
        first = pl.multiple_of(i * 224, 16)
        part = lambda o: u_ref[pl.ds(first + o, 16), :].astype(F32)
        pooled = (part(16) + part(32) + part(176) + part(192)) * 0.25
        at = pl.multiple_of(i * 48, 16)
        pv_ref[pl.ds(at, 16), :] = later(pooled, lane16).astype(BF)
        pv_ref[pl.ds(at + 16, 16), :] = pooled.astype(BF)
        pv_ref[pl.ds(at + 32, 16), :] = sooner(pooled, lane16).astype(BF)

    pl.loop(4, 32, unroll=7)(pool)
    greeting(0)

    ready("wmid", "q2", "bmid")
    base2 = over(wmid_ref[...].reshape(144, 32), q2_ref[...])
    for r in range(8):
        w2_ref[pl.ds(r * 32, 32), :] = (
            pltpu.roll(base2, 48 * r, 1) if r else base2
        ).astype(BF)
    b2_ref[...] = column(bmid_ref, 32, HALF)

    lane32 = iota((32, HALF), 1)

    def convolve(q):
        if q == 4:
            return mm(w2_ref[0:64, :192], pv_ref[1536:1728, :])
        return mm(w2_ref[:, :480], pv_ref[q * 384 : q * 384 + 480, :])

    def middle(q, acc):
        for r in range(2 if q == 4 else 8):
            m = jnp.maximum(acc[r * 32 : (r + 1) * 32] + b2_ref[...], 0.0).astype(BF)
            at = (q * 8 + r + 1) * 224 + 64
            u_ref[at : at + 32, :] = later(m, lane32)
            u_ref[at + 32 : at + 64, :] = m
            u_ref[at + 64 : at + 96, :] = sooner(m, lane32)

    staggered(convolve, middle, (1, 2))
    forward(1, 0)
    forward(1, 1)

    ready("wdec", "q3", "bdec", "wout", "bout")
    wdec = jnp.concatenate([wdec_ref[dr, dt] for dr in range(3) for dt in range(3)], axis=1)
    for n in range(4):
        wide = jnp.concatenate([mm(wdec, q3_ref[n]), jnp.zeros((16, 640), F32)], axis=1)
        for r in range(4):
            turned = pltpu.roll(wide, 224 * r, 1) if r else wide
            for t in range(10):
                wf_ref[t, pl.ds(n // 2 * 8 + 2 * r + n % 2, 16, stride=16), :] = (
                    turned[:, t * 128 : (t + 1) * 128]
                )
    w3_ref[...] = jnp.concatenate([wf_ref[t] for t in range(10)], axis=1).astype(BF)
    wrow = mm(wout_ref[...], jnp.eye(16, dtype=F32).astype(BF))
    wout = [wrow[:, g : g + 1] for g in range(16)]
    own_ref[...] = mm(clean, split)
    alive_ref[...] = mm(diag, jnp.ones((ROWS, HALF), BF))

    forward(1, 2)
    forward(1, 3)

    def gather(q):
        first = q * 896 + 288
        if not isinstance(q, int):
            first = pl.multiple_of(first, 32)
        return mm(w3_ref[:, :1216], u_ref[pl.ds(first, 1216), :])

    def decode(q, acc):
        branch = None
        for g in range(16):
            tile = jnp.maximum(acc[g * 16 : (g + 1) * 16] + bdec_ref[g], 0.0)
            term = tile.astype(BF).astype(F32) * wout[g]
            branch = term if branch is None else branch + term
        here = pl.ds(q * 8 if isinstance(q, int) else pl.multiple_of(q * 8, 8), 8)
        alive = alive_ref[here, :]
        for ps in range(2):
            lanes = slice(ps * HALF, (ps + 1) * HALF)
            dp_ref[here, lanes] = alive * (
                own_ref[here, lanes] + branch[ps * 8 : ps * 8 + 8] + bout_ref[0]
            )

    def results(h):
        here = pl.ds(pl.multiple_of(h * 32, 32), 32)
        return pltpu.make_async_copy(sd_ref.at[h], den_ref.at[here], den_sem.at[h])

    def finish(h):
        here = pl.ds(pl.multiple_of(h * 32, 32), 32)
        natural = lax.dot_general(
            dp_ref[here, :].astype(BF), split, (((1,), (1,)), ((), ())), preferred_element_type=F32
        ).astype(BF)
        sd_ref[h] = natural
        results(h).start()

    to_partner = pltpu.make_async_remote_copy(
        src_ref=sd_ref.at[1 - p], dst_ref=xw_ref.at[p],
        send_sem=x_send.at[0], recv_sem=x_recv.at[0],
        device_id=(z, c, 1 - p), device_id_type=MESH)

    def to_previous(h):
        return pltpu.make_async_remote_copy(
            src_ref=sd_ref.at[h], dst_ref=xw_ref.at[2],
            send_sem=x_send.at[1 + h], recv_sem=x_recv.at[1],
            device_id=(zl, c, h), device_id_type=MESH)

    staggered(gather, decode, (2, 3, 4))
    greeting(1)

    for h in halos:
        h.wait_recv()
    far = iota((24, 16), 0)
    far = jnp.where(far < 8, far, far + 56)
    away = iota((24, 16), 1)
    above = jnp.where((far + 11 == away) & (c > 0), 1.0, 0.0).astype(BF)
    below = jnp.where((far == away + 69) & (away < 5) & (c < NC - 1), 1.0, 0.0).astype(BF)
    near = iota((24, 64), 0)
    near = jnp.where(near < 8, near, near + 56)
    kept = jnp.where(near == iota((24, 64), 1) + 5, 1.0, 0.0).astype(BF)
    edges = variants(mm(kept, clean) + mm(above, halo_ref[0]) + mm(below, halo_ref[1]))
    for n in range(6):
        for h in range(2):
            cut = edges[n][:, h * 128 : (h + 1) * 128]
            cv_ref[h, pl.ds(n, 8, stride=8), :] = cut[:8]
            cv_ref[h, pl.ds(512 + n, 16, stride=8), :] = cut[8:]
    staggered(encode, encoded, (0, 8))

    @pl.when(c == 0)
    def _():
        u_ref[0:448, :] = jnp.zeros((448, HALF), BF)

    @pl.when(c == NC - 1)
    def _():
        u_ref[34 * 224 : 36 * 224, :] = jnp.zeros((448, HALF), BF)

    for i in (0, 1, 2, 3, 32, 33, 34, 35):
        pool(i)

    forward(2, 0)
    staggered(convolve, middle, (0, 3, 4))

    @pl.when(c == 0)
    def _():
        u_ref[288:384, :] = jnp.zeros((96, HALF), BF)

    @pl.when(c == NC - 1)
    def _():
        u_ref[34 * 224 + 64 : 34 * 224 + 160, :] = jnp.zeros((96, HALF), BF)

    forward(2, 1)
    greeting(2)
    theirs = 6 * (1 - p)
    staggered(gather, decode, (5, theirs, theirs + 1))
    finish(1 - p)
    to_partner.start()

    @pl.when(p == 0)
    def _():
        to_previous(1).start()

    forward(2, 2)
    forward(2, 3)
    greeting(3)
    staggered(gather, decode, (6 * p, 6 * p + 1))
    finish(p)

    @pl.when(p == 0)
    def _():
        to_previous(0).start()

    xw_ref[p] = sd_ref[p]

    ready("f")

    def transform(first, count):
        wide = mm(tg_ref[first : first + count].reshape(count * 128, TL), f_ref[...])
        ts_ref[first : first + count] = wide.reshape(count, 128, 2 * TL)

    transform(0, 3)
    greeting(4)

    rrow = iota((128, 32), 0)
    repeat = jnp.where(rrow // 4 == iota((128, 32), 1), 1.0, 0.0).astype(BF)
    lane1k = iota((128, 2 * TL), 1)
    sign = jnp.where((lane1k % 2 == 1), -1.0, 1.0)
    to_partner.wait_recv()
    for n in range(2):
        xr_ref[pl.ds(n * 128, 128), :] = mm(repeat, xw_ref[n]).astype(BF)
    spectra = mm(xr_ref[...], f_ref[...])
    z_ref[0] = spectra[0:128] + sign * spectra[128:256]
    z_ref[1] = spectra[128:256]

    transform(3, 2)

    lane512 = iota((8, TL), 1)

    def product(n, k):
        a = jnp.zeros((8, TL), F32)
        b = jnp.zeros((8, TL), F32)
        d = jnp.zeros((8, TL), F32)
        for s in range(16):
            here = pl.ds(s * 8, 8)
            tr = ts_ref[k, here, 0:TL]
            ti = ts_ref[k, here, TL : 2 * TL]
            sr = z_ref[n, here, 0:TL]
            si = z_ref[n, here, TL : 2 * TL]
            a = a + sr * tr
            b = b + si * ti
            d = d + (si * tr - sr * ti)
        a = a + pltpu.roll(a, 4, 0)
        b = b + pltpu.roll(b, 4, 0)
        d = d + pltpu.roll(d, 4, 0)
        at = pl.ds(pl.multiple_of(n * 64 + k * 8, 8), 8)
        g_ref[at, 0:TL] = jnp.where(lane512 == 0, a, a + b)
        g_ref[at, TL : 2 * TL] = jnp.where(lane512 == 0, b, d)

    pl.loop(0, 5, unroll=True)(functools.partial(product, 0))
    to_previous(0).wait_recv()
    following = xw_ref[2] * jnp.where(z == NZ - 1, 0.0, 1.0).astype(BF)
    z_ref[1] = z_ref[1] + sign * mm(mm(repeat, following).astype(BF), f_ref[...])
    pl.loop(0, 5, unroll=True)(functools.partial(product, 1))
    arrived(2, 0, 4)
    arrived(3, 0, 2)
    transform(5, 3)
    pl.loop(5, 8, unroll=True)(functools.partial(product, 0))
    pl.loop(5, 8, unroll=True)(functools.partial(product, 1))

    ready("i")
    lags = mm(g_ref[...].astype(BF), i_ref[...])
    for t in range(4):
        lag_ref[t] = lags[:, t * 128 : (t + 1) * 128]

    lane8 = iota((8, 128), 1) // 32
    for n in range(2):
        for t in range(4):
            quarter = [lag_ref[t, pl.ds(n * 64 + k, 8, stride=8), :] for k in range(4)]
            for o in range(4):
                piece = jnp.zeros((8, 128), F32)
                for k in range(4):
                    shift = (k - o) % 4 * 32
                    moved = pltpu.roll(quarter[k], shift, 1) if shift else quarter[k]
                    piece = jnp.where(lane8 == k, moved, piece)
                rs_ref[n * NC + t * 4 + o] = piece

    hops = [0, 2, 1, 1]
    steps = [0, 1, 2, 1]
    for d in sorted(range(1, 2 * NC), key=lambda d: -hops[d // 8] - steps[d // 2 % 4]):
        other = lax.rem(me + d, 2 * NC)
        pltpu.make_async_remote_copy(
            src_ref=rs_ref.at[other], dst_ref=rr_ref.at[d - 1],
            send_sem=rs_send.at[0], recv_sem=rs_recv.at[0],
            device_id=(z, lax.rem(other, NC), other // NC), device_id_type=MESH).start()

    shares = pltpu.make_async_remote_copy(
        src_ref=rr_ref, dst_ref=rr_ref, send_sem=rs_send.at[0], recv_sem=rs_recv.at[0],
        device_id=(z, c, 1 - p), device_id_type=MESH)
    shares.wait_recv()
    parts = [rs_ref[me]] + [rr_ref[d] for d in range(2 * NC - 1)]
    while len(parts) > 1:
        parts = [parts[n] + parts[n + 1] for n in range(0, len(parts), 2)]
    as_ref[...] = parts[0].reshape(8, 1, 128)

    places = [0, 1, -1, 2, -2, 3, -3, 4]
    for d in range(NZ - 1, 0, -1):
        pltpu.make_async_remote_copy(
            src_ref=as_ref.at[d], dst_ref=ar_ref.at[z],
            send_sem=a_send.at[d], recv_sem=a_recv.at[z],
            device_id=(lax.rem(z + NZ - places[d], NZ), c, p), device_id_type=MESH).start()

    ar_ref[z] = as_ref[0]

    def landing(d):
        other = lax.rem(z + NZ + places[d], NZ)
        return pltpu.make_async_remote_copy(
            src_ref=as_ref.at[d], dst_ref=ar_ref.at[other],
            send_sem=a_send.at[d], recv_sem=a_recv.at[other],
            device_id=(other, c, p), device_id_type=MESH)

    for d in range(1, NZ):
        landing(d).wait_recv()

    found = ar_ref[...].reshape(8, 128)
    turned = [found] + [pltpu.roll(found, 128 - 32 * k, 1) for k in range(1, 4)]
    ready("assign")
    for r in range(4):
        local = lax.rem(assign_ref[r], 4)
        row = jnp.zeros((8, 128), F32)
        for k in range(4):
            row = row + jnp.where(local == k, 1.0, 0.0) * turned[k]
        corr_ref[r] = row[:, :32].reshape(8, 1, 32)

    results(0).wait()
    results(1).wait()
    for h in halos:
        h.wait_send()
    for s in range(4):
        for n in range(4 if s < 3 else 2):
            right(s, n).wait_send()
            left(s, n).wait_send()
    to_partner.wait_send()

    @pl.when(p == 0)
    def _():
        to_previous(0).wait_send()
        to_previous(1).wait_send()

    shares.wait_send()
    for d in range(1, NZ):
        landing(d).wait_send()


def body(raw, dead_mask, templates, assign, w_enc, b_enc, w_mid, b_mid, w_dec, b_dec, w_out, b_out):
    vm = pl.BlockSpec(memory_space=pltpu.VMEM)
    hbm = pl.BlockSpec(memory_space=pltpu.HBM)
    dma = pltpu.SemaphoreType.DMA
    tables = [
        jnp.asarray(t, BF)
        for t in (encoder_table(), middle_table(), decoder_table(), spectrum_table(), lag_table())
    ]
    operands = [
        raw,
        dead_mask.reshape(1, ROWS),
        templates,
        assign,
        w_enc.transpose(1, 2, 3, 0).reshape(3, 3, 16),
        b_enc,
        w_mid.transpose(2, 3, 1, 0),
        b_mid,
        w_dec.transpose(2, 3, 0, 1),
        b_dec,
        w_out.reshape(1, 16),
        b_out,
    ] + tables
    scalars = (3, 5, 7, 9, 11)
    landing_places = [
        (pltpu.SMEM if n in scalars else pltpu.VMEM)(x.shape, x.dtype)
        for n, x in enumerate(operands)
    ]
    return pl.pallas_call(
        kernel,
        out_shape=(
            jax.ShapeDtypeStruct((ROWS, TL), BF),
            jax.ShapeDtypeStruct((4, 8, 1, 32), F32),
        ),
        in_specs=[hbm] * len(operands),
        out_specs=(hbm, vm),
        scratch_shapes=landing_places + [
            pltpu.VMEM((ROWS, TL), BF),
            pltpu.VMEM((2, 16, TL), BF),
            pltpu.VMEM((2, 640, 128), F32),
            pltpu.VMEM((512, 128), BF),
            pltpu.VMEM((256, 512), BF),
            pltpu.VMEM((10, 256, 128), F32),
            pltpu.VMEM((256, 1280), BF),
            pltpu.VMEM((36 * 224, HALF), BF),
            pltpu.VMEM((36 * 48, HALF), BF),
            pltpu.VMEM((ROWS, TL), F32),
            pltpu.VMEM((ROWS, TL), F32),
            pltpu.VMEM((ROWS, HALF), F32),
            pltpu.VMEM((32, HALF), F32),
            pltpu.VMEM((NZ, 128, TL), BF),
            pltpu.VMEM((NZ, 128, 2 * TL), F32),
            pltpu.VMEM((2, 32, TL), BF),
            pltpu.VMEM((3, 32, TL), BF),
            pltpu.VMEM((256, TL), BF),
            pltpu.VMEM((2, 128, 2 * TL), F32),
            pltpu.VMEM((128, 2 * TL), F32),
            pltpu.VMEM((4, 128, 128), F32),
            pltpu.VMEM((2 * NC, 8, 128), F32),
            pltpu.VMEM((2 * NC - 1, 8, 128), F32),
            pltpu.VMEM((NZ, 1, 128), F32),
            pltpu.VMEM((NZ, 1, 128), F32),
            dma((len(operands),)),
            dma((2,)),
            dma((2,)),
            dma((2,)),
            dma((2, 14)),
            dma((2, 14)),
            dma((3,)),
            dma((2,)),
            dma((1,)),
            dma((1,)),
            dma((NZ,)),
            dma((NZ,)),
            pltpu.SemaphoreType.REGULAR((5,)),
        ],
        compiler_params=pltpu.CompilerParams(
            collective_id=0, has_side_effects=True, vmem_limit_bytes=56 * 1024 * 1024
        ),
    )(*operands)


def solution(mesh):
    return jax.shard_map(
        body,
        mesh=mesh,
        in_specs=(
            P("chan", ("tmpl", "tm")),
            P("chan"),
            P("tmpl", "chan", None),
            P("tmpl"),
            P(),
            P(),
            P(),
            P(),
            P(),
            P(),
            P(),
            P(),
        ),
        out_specs=(P("chan", ("tmpl", "tm")), P("tmpl", None, "tm", "chan")),
        check_vma=False,
    )
```
